32 devices in a mesh: wide: 8 (over z, x), narrow: 4 (over y, core).
Axes of the slice: x: 2, y: 2, z: 4, core: 2. Of those that a mesh axis runs over, the one named last changes fastest.
Arguments:
- enc_ids: int32 [2, 8, 1024], P(None, 'wide'), may hold values from 0 to 32127
- enc_len: int32 [2, 8], P(None, 'wide'), may hold values from 512 to 1024
- tgt_ids: int32 [2, 8, 256], replicated, may hold values from 0 to 32127
- tgt_len: int32 [2, 8], replicated, may hold values from 53 to 256, as said below
- span_mask: int32 [2, 8, 256], replicated, may hold values 0 or 1
- buckets: int32 [2047], replicated, may hold values from 0 to 31
- attn_in: float32 [3, 768, 2304], P(None, 'wide', 'narrow'), may hold values from -0.0625 to 0.0625
- attn_out: float32 [3, 768, 768], P(None, 'narrow', 'wide'), may hold values from -4 to 4
- ff_in: float32 [2, 768, 3072], P(None, 'wide', 'narrow'), may hold values from -0.21875 to 0.21875
- ff_out: float32 [2, 3072, 768], P(None, 'narrow', 'wide'), may hold values from -0.21875 to 0.21875
- table: float32 [32128, 768], P('wide')
- gains: float32 [7, 768], P(None, 'narrow')
- rel: float32 [2, 32, 12], P(None, None, 'narrow'), may hold values from -6 to 6
- mom_attn_in: float32 [3, 768, 2304], P(None, 'wide', 'narrow'), may hold values from -5.340576e-05 to 5.340576e-05
- mom_attn_out: float32 [3, 768, 768], P(None, 'narrow', 'wide'), may hold values from -5.340576e-05 to 5.340576e-05
- mom_ff_in: float32 [2, 768, 3072], P(None, 'wide', 'narrow'), may hold values from -5.340576e-05 to 5.340576e-05
- mom_ff_out: float32 [2, 3072, 768], P(None, 'narrow', 'wide'), may hold values from -5.340576e-05 to 5.340576e-05
- mom_table: float32 [32128, 768], P('wide'), may hold values from -5.340576e-05 to 5.340576e-05
- mom_gains: float32 [7, 768], P(None, 'narrow'), may hold values from -0.00024414062 to 0.00024414062
- mom_rel: float32 [2, 32, 12], P(None, None, 'narrow'), may hold values from -0.00024414062 to 0.00024414062
- avg_attn_in: float32 [3, 768, 2304], P(None, 'wide', 'narrow'), may hold values from -0.0625 to 0.0625
- avg_attn_out: float32 [3, 768, 768], P(None, 'narrow', 'wide'), may hold values from -4 to 4
- avg_ff_in: float32 [2, 768, 3072], P(None, 'wide', 'narrow'), may hold values from -0.21875 to 0.21875
- avg_ff_out: float32 [2, 3072, 768], P(None, 'narrow', 'wide'), may hold values from -0.21875 to 0.21875
- avg_table: float32 [32128, 768], P('wide'), may hold values from -6 to 6
- avg_gains: float32 [7, 768], P(None, 'narrow'), may hold values from 0.5 to 1.5
- avg_rel: float32 [2, 32, 12], P(None, None, 'narrow'), may hold values from -6 to 6
Outputs:
- loss_sum: float32 [], replicated
- loss_count: float32 [], replicated
- grad_norm: float32 [], replicated
- new_attn_in: float32 [3, 768, 2304], P(None, 'wide', 'narrow')
- new_attn_out: float32 [3, 768, 768], P(None, 'narrow', 'wide')
- new_ff_in: float32 [2, 768, 3072], P(None, 'wide', 'narrow')
- new_ff_out: float32 [2, 3072, 768], P(None, 'narrow', 'wide')
- new_table: float32 [32128, 768], P('wide')
- new_gains: float32 [7, 768], P(None, 'narrow')
- new_rel: float32 [2, 32, 12], P(None, None, 'narrow')
- clipped_attn_in: float32 [3, 768, 2304], P(None, 'wide', 'narrow')
- clipped_attn_out: float32 [3, 768, 768], P(None, 'narrow', 'wide')
- clipped_ff_in: float32 [2, 768, 3072], P(None, 'wide', 'narrow')
- clipped_ff_out: float32 [2, 3072, 768], P(None, 'narrow', 'wide')
- clipped_table: float32 [32128, 768], P('wide')
- clipped_gains: float32 [7, 768], P(None, 'narrow')
- clipped_rel: float32 [2, 32, 12], P(None, None, 'narrow')
- average_attn_in: float32 [3, 768, 2304], P(None, 'wide', 'narrow')
- average_attn_out: float32 [3, 768, 768], P(None, 'narrow', 'wide')
- average_ff_in: float32 [2, 768, 3072], P(None, 'wide', 'narrow')
- average_ff_out: float32 [2, 3072, 768], P(None, 'narrow', 'wide')
- average_table: float32 [32128, 768], P('wide')
- average_gains: float32 [7, 768], P(None, 'narrow')
- average_rel: float32 [2, 32, 12], P(None, None, 'narrow')
The draws below stay inside these ranges and needn't reach their ends.
Inputs may be any that keep to these rules, and one draw needn't show every extreme that they name: `tgt_len`: target lengths rise with the example's place in the micro-batch; the last example of each micro-batch has the full padded length.
All inputs are finite; a program needn't handle non-finite values.
Results may differ from the reference program's by a relative error of at most 0.011.
Values may be sent and summed in bfloat16 or wider, within the bound.
A program may use at most 512 MiB of HBM per device.

```python
import math
import jax
import jax.numpy as jnp
import numpy as np
from jax import lax

D = 768
H = 12
DH = 64
FF = 3072
V = 32128
NB = 32
LENC = 1024
LDEC = 256
MICRO = 2
EX_DEV = 1
EXAMPLES = 8
PARAMS = 41195520


def draw_tgt_len(key, part):
    key = jax.random.fold_in(key, 7)
    example = jnp.arange(EXAMPLES, dtype=jnp.int32)
    groups = EXAMPLES // EX_DEV
    place = example // EX_DEV
    base = LDEC // 3 + (LDEC - LDEC // 3) * place // max(groups - 1, 1)
    jitter = jax.random.randint(key, (MICRO, EXAMPLES), 0, LDEC // 8 + 1)
    jitter = jnp.where(example[None, :] == EXAMPLES - 1, 0, jitter)
    return jnp.maximum(base[None, :] - jitter, 1).astype(jnp.int32)


def draw_buckets(key, part):
    key = jax.random.fold_in(key, 17)
    half_count = NB // 2
    exact_count = half_count // 2
    limits = [math.ceil(exact_count * (128.0 / exact_count) ** (step / exact_count)) for step in range(exact_count)]
    offsets = jnp.arange(2 * LENC - 1, dtype=jnp.int32) - (LENC - 1)
    magnitude = jnp.abs(offsets)
    passed = jnp.zeros(offsets.shape, jnp.int32)
    for limit in limits:
        passed = passed + (magnitude >= limit).astype(jnp.int32)
    klass = jnp.where(magnitude < exact_count, magnitude, exact_count - 1 + passed)
    klass = klass + half_count * (offsets > 0).astype(jnp.int32)
    labels = jax.random.permutation(key, NB).astype(jnp.int32)
    return labels[klass].astype(jnp.int32)


def draw_table(key, part):
    key = jax.random.fold_in(key, 11)
    position = jnp.arange(V, dtype=jnp.float32)[:, None] / V
    values = jax.random.normal(key, (V, D), jnp.float32)
    return values * 0.8 * (1.0 + position)


def draw_gains(key, part):
    key = jax.random.fold_in(key, 13)
    position = jnp.arange(D, dtype=jnp.float32)[None, :] / D
    factor = jax.random.uniform(key, (7, D), jnp.float32, 0.85, 1.15)
    return (0.6 + 1.2 * position) * factor


def touch_ends(drawn, rng, smallest, largest):
    extent = drawn.shape
    index_at = [jax.random.randint(jax.random.fold_in(rng, axis), (), 0, extent[axis]) for axis in range(len(extent))]
    drawn = drawn.at[tuple(index_at)].set(smallest)
    longest = extent.index(max(extent))
    index_at[longest] = (index_at[longest] + 1) % extent[longest]
    return drawn.at[tuple(index_at)].set(largest)


def level_of(rng, shape, split, smallest, high):
    level = 1.0
    for axis_at, parts in split:
        heights = jax.random.uniform(jax.random.fold_in(jax.random.fold_in(rng, 6), axis_at), (parts,), jnp.float32, smallest / len(split), high / len(split))
        level = level * jnp.repeat(jnp.exp(heights), shape[axis_at] // parts).reshape((-1,) + (1,) * (len(shape) - 1 - axis_at))
    return level


def cumulative_ranks(number_of, lean):
    portions = [(1 << 20) // math.isqrt(grade ** lean) + 1 for grade in range(1, number_of + 1)]
    deviation = 1 + sum(portions) // (1 << 30)
    return np.cumsum(np.array([max(1, weight // deviation) for weight in portions]))


def ranked(own_key, dims, number_of, slope):
    listing = cumulative_ranks(number_of, slope)
    ticket = jax.random.randint(jax.random.fold_in(own_key, 1), dims, 0, int(listing[number_of - 1]))
    rank = jnp.searchsorted(jnp.asarray(listing, jnp.int32), ticket, side="right")
    return jax.random.permutation(jax.random.fold_in(own_key, 2), number_of)[rank].astype(jnp.int32)


def gaussian(key, extent, spread, most, split=(), held_as=jnp.bfloat16):
    level = level_of(key, extent, split, -0.22, 0.18) if split else 1.0
    result = jax.random.normal(key, extent, jnp.float32) * spread * level
    return jnp.minimum(jnp.maximum(result, -most), most).astype(held_as)


def setup_inputs(seed: int = 0) -> dict:
    key_list = jax.random.split(jax.random.key(seed), 28)
    return {
        "enc_ids": touch_ends(ranked(key_list[0], (MICRO, EXAMPLES, LENC), V, 2), jax.random.fold_in(key_list[0], 3), 0, V - 1).astype(jnp.int32),
        "enc_len": touch_ends(jax.random.randint(key_list[1], (MICRO, EXAMPLES), LENC // 2, LENC + 1), jax.random.fold_in(key_list[1], 1), LENC // 2, LENC).astype(jnp.int32),
        "tgt_ids": touch_ends(ranked(key_list[2], (MICRO, EXAMPLES, LDEC), V, 2), jax.random.fold_in(key_list[2], 3), 0, V - 1).astype(jnp.int32),
        "tgt_len": draw_tgt_len(jax.random.fold_in(key_list[27], 71), 0),
        "span_mask": touch_ends((jax.random.randint(key_list[4], (MICRO, EXAMPLES, LDEC), 0, 8) < 7).astype(jnp.int32), jax.random.fold_in(key_list[4], 1), 0, 1),
        "buckets": draw_buckets(jax.random.fold_in(key_list[27], 71), 0),
        "attn_in": gaussian(key_list[6], (3, D, 3 * H * DH), (12 * D) ** -0.5, 0.0625, ((1, 8), (2, 4)), jnp.float32),
        "attn_out": gaussian(key_list[7], (3, H * DH, D), 2 ** -0.5, 4.0, ((1, 4), (2, 8)), jnp.float32),
        "ff_in": gaussian(key_list[8], (2, D, FF), D ** -0.5, 0.21875, ((1, 8), (2, 4)), jnp.float32),
        "ff_out": gaussian(key_list[9], (2, FF, D), (FF // 4) ** -0.5, 0.21875, ((1, 4), (2, 8)), jnp.float32),
        "table": draw_table(jax.random.fold_in(key_list[27], 71), 0),
        "gains": draw_gains(jax.random.fold_in(key_list[27], 71), 0),
        "rel": gaussian(key_list[12], (2, NB, H), 1.0, 6.0, ((2, 4),), jnp.float32),
        "mom_attn_in": gaussian(key_list[13], (3, D, 3 * H * DH), (0.024 * PARAMS ** -0.5), 5.340576171875e-05, ((1, 8), (2, 4)), jnp.float32),
        "mom_attn_out": gaussian(key_list[14], (3, H * DH, D), (0.024 * PARAMS ** -0.5), 5.340576171875e-05, ((1, 4), (2, 8)), jnp.float32),
        "mom_ff_in": gaussian(key_list[15], (2, D, FF), (0.024 * PARAMS ** -0.5), 5.340576171875e-05, ((1, 8), (2, 4)), jnp.float32),
        "mom_ff_out": gaussian(key_list[16], (2, FF, D), (0.024 * PARAMS ** -0.5), 5.340576171875e-05, ((1, 4), (2, 8)), jnp.float32),
        "mom_table": gaussian(key_list[17], (V, D), (0.024 * PARAMS ** -0.5), 5.340576171875e-05, ((0, 8),), jnp.float32),
        "mom_gains": gaussian(key_list[18], (7, D), (0.1 * PARAMS ** -0.5), 0.00024414062, ((1, 4),), jnp.float32),
        "mom_rel": gaussian(key_list[19], (2, NB, H), (0.1 * PARAMS ** -0.5), 0.00024414062, ((2, 4),), jnp.float32),
        "avg_attn_in": gaussian(key_list[20], (3, D, 3 * H * DH), (12 * D) ** -0.5, 0.0625, ((1, 8), (2, 4)), jnp.float32),
        "avg_attn_out": gaussian(key_list[21], (3, H * DH, D), 2 ** -0.5, 4.0, ((1, 4), (2, 8)), jnp.float32),
        "avg_ff_in": gaussian(key_list[22], (2, D, FF), D ** -0.5, 0.21875, ((1, 8), (2, 4)), jnp.float32),
        "avg_ff_out": gaussian(key_list[23], (2, FF, D), (FF // 4) ** -0.5, 0.21875, ((1, 4), (2, 8)), jnp.float32),
        "avg_table": gaussian(key_list[24], (V, D), 1.0, 6.0, ((0, 8),), jnp.float32),
        "avg_gains": jnp.clip(1.0 + 0.1 * jax.random.normal(key_list[25], (7, D), jnp.float32), 0.5, 1.5),
        "avg_rel": gaussian(key_list[26], (2, NB, H), 1.0, 6.0, ((2, 4),), jnp.float32),
    }


@jax.custom_vjp
def low(v):
    return lax.optimization_barrier(v.astype(jnp.bfloat16)).astype(jnp.float32)

@jax.custom_vjp
def low_back(v):
    return v

def low_keep(v):
    return (low(v), None)

def low_pass(kept, grad):
    return (grad,)

def back_keep(v):
    return (v, None)

def back_low(kept, grad):
    return (low(grad),)
low.defvjp(low_keep, low_pass)
low_back.defvjp(back_keep, back_low)
epsilon = 1e-06
masked_score = -1000000000.0
momentum_decay = 0.9
average_decay = 0.9
clip_norm = 0.02
highest = lax.Precision.HIGHEST

def rounded(value):
    return low_back(low(value))

def rms(state, gain_row):
    return state * lax.rsqrt(lax.optimization_barrier(jnp.mean(state * state, axis=-1, keepdims=True)) + epsilon) * gain_row

def rel_bias(table_part, buckets, len_q, len_k):
    offsets = jnp.arange(len_k)[None, :] - jnp.arange(len_q)[:, None] + LENC - 1
    return jnp.transpose(table_part[buckets[offsets]], (2, 0, 1))

def attention(normed, source, weight_in, weight_out, bias):
    grouped = weight_in.reshape(D, H, 3, DH)
    queries = rounded(jnp.einsum('qd,dhx->qhx', normed, grouped[:, :, 0], precision=highest))
    key_rows = rounded(jnp.einsum('kd,dhx->khx', source, grouped[:, :, 1], precision=highest))
    value_rows = rounded(jnp.einsum('kd,dhx->khx', source, grouped[:, :, 2], precision=highest))
    scores = low_back(jnp.einsum('qhx,khx->hqk', queries, key_rows, precision=highest) + bias)
    probs = rounded(jax.nn.softmax(scores, axis=-1))
    mixed = jnp.einsum('hqk,khx->qhx', probs, value_rows, precision=highest)
    mixed = rounded(mixed.reshape(mixed.shape[0], H * DH))
    return low_back(jnp.dot(mixed, weight_out, precision=highest))

def feed(normed, weight_in, weight_out):
    pre = low_back(jnp.dot(normed, weight_in, precision=highest))
    return low_back(jnp.dot(rounded(jax.nn.gelu(pre)), weight_out, precision=highest))

def example_loss(lowered, buckets, enc_row, enc_length, tgt_row, weight_row):
    attn_in, attn_out, ff_in, ff_out, table_low, gains, rel = lowered
    enc_mask = jnp.where(jnp.arange(LENC) < enc_length, 0.0, masked_score).astype(jnp.float32)
    state = table_low[enc_row]
    normed = rounded(rms(state, gains[0]))
    state = state + attention(normed, normed, attn_in[0], attn_out[0], rel_bias(rel[0], buckets, LENC, LENC) + enc_mask)
    state = state + feed(rounded(rms(state, gains[1])), ff_in[0], ff_out[0])
    encoded = rounded(rms(state, gains[2]))
    dec_ids = jnp.concatenate([jnp.zeros((1,), jnp.int32), tgt_row[:-1].astype(jnp.int32)])
    causal = jnp.where(jnp.arange(LDEC)[None, :] <= jnp.arange(LDEC)[:, None], 0.0, masked_score).astype(jnp.float32)
    dec = table_low[dec_ids]
    normed = rounded(rms(dec, gains[3]))
    dec = dec + attention(normed, normed, attn_in[1], attn_out[1], rel_bias(rel[1], buckets, LDEC, LDEC) + causal)
    normed = rounded(rms(dec, gains[4]))
    dec = dec + attention(normed, encoded, attn_in[2], attn_out[2], enc_mask)
    dec = dec + feed(rounded(rms(dec, gains[5])), ff_in[1], ff_out[1])
    final = rounded(rms(dec, gains[6]) * D ** (-0.5))
    logits = low_back(jnp.dot(final, table_low.T, precision=highest))
    log_total = jax.nn.logsumexp(logits, axis=-1)
    hits = jnp.take_along_axis(logits, tgt_row[:, None], axis=-1)[:, 0]
    return jnp.sum(weight_row * (log_total - hits))

def reference(enc_ids, enc_len, tgt_ids, tgt_len, span_mask, buckets, attn_in, attn_out, ff_in, ff_out, table, gains, rel, mom_attn_in, mom_attn_out, mom_ff_in, mom_ff_out, mom_table, mom_gains, mom_rel, avg_attn_in, avg_attn_out, avg_ff_in, avg_ff_out, avg_table, avg_gains, avg_rel):
    row_weight = (jnp.arange(LDEC)[None, None, :] < tgt_len[:, :, None]).astype(jnp.float32) * span_mask.astype(jnp.float32)
    count = jnp.sum(row_weight)
    params = (attn_in, attn_out, ff_in, ff_out, table, gains, rel)

    def total_loss(values):
        lowered = (low(values[0]), low(values[1]), low(values[2]), low(values[3]), low(values[4]), values[5], values[6])

        def one_example(carry, items):
            return (carry + jax.checkpoint(example_loss)(lowered, buckets, *items), None)
        total = jnp.zeros((), jnp.float32)
        for micro in range(MICRO):
            total, unused = lax.scan(one_example, total, (enc_ids[micro], enc_len[micro], tgt_ids[micro], row_weight[micro]))
        return total
    loss_sum, pullback = jax.vjp(total_loss, params)
    grads = pullback(jnp.ones((), jnp.float32) / count)[0]
    norm = jnp.sqrt(sum((jnp.sum(grad * grad) for grad in grads)))
    scale = jnp.minimum(1.0, clip_norm / norm)
    base_rate = math.sqrt(PARAMS) / (3.0 * clip_norm)
    matrix_rate = base_rate / math.sqrt(D)
    rates = (matrix_rate, 16.0 * matrix_rate, matrix_rate, matrix_rate, base_rate, 0.3 * base_rate, 0.3 * base_rate)
    moms = (mom_attn_in, mom_attn_out, mom_ff_in, mom_ff_out, mom_table, mom_gains, mom_rel)
    avgs = (avg_attn_in, avg_attn_out, avg_ff_in, avg_ff_out, avg_table, avg_gains, avg_rel)
    fresh, scaled_grads, averages = ([], [], [])
    for index in range(7):
        clipped = grads[index] * scale
        moment = momentum_decay * moms[index] + clipped
        weight = params[index] - rates[index] * (clipped + momentum_decay * moment)
        fresh.append(weight)
        scaled_grads.append(clipped)
        averages.append(average_decay * avgs[index] + (1.0 - average_decay) * weight)
    return (loss_sum, count, norm, fresh[0], fresh[1], fresh[2], fresh[3], fresh[4], fresh[5], fresh[6], scaled_grads[0], scaled_grads[1], scaled_grads[2], scaled_grads[3], scaled_grads[4], scaled_grads[5], scaled_grads[6], averages[0], averages[1], averages[2], averages[3], averages[4], averages[5], averages[6])
```

```python
import functools
import math

import jax
import jax.numpy as jnp
from jax import lax
from jax.experimental import pallas as pl
from jax.experimental.pallas import tpu as pltpu
from jax.sharding import PartitionSpec as P

DH = 64
PARAMS = 41195520

epsilon = 1e-06
masked_score = -1000000000.0
momentum_decay = 0.9
average_decay = 0.9
clip_norm = 0.02
highest = lax.Precision.HIGHEST
bf16 = jnp.bfloat16
f32 = jnp.float32
CHUNK = 256


def dot(left, right, left_dim, right_dim):
    return lax.dot_general(
        left, right, (((left_dim,), (right_dim,)), ((), ())), preferred_element_type=f32
    )


def hop(values, axis, bit):
    size = lax.axis_size(axis)
    return lax.ppermute(values, axis, [(i, i ^ bit) for i in range(size)])


def swap(values):
    return hop(values, "narrow", 1)


def bits_down(axis):
    bit = lax.axis_size(axis) // 2
    while bit:
        yield bit
        bit //= 2


def bits_up(axis):
    return reversed(list(bits_down(axis)))


def gather_sorted(values, axis):
    index = lax.axis_index(axis)
    values = values[None]
    for bit in bits_down(axis):
        other = hop(values, axis, bit)
        upper = (index & bit) != 0
        values = jnp.stack(
            [jnp.where(upper, other, values), jnp.where(upper, values, other)], axis=1
        ).reshape(-1, *values.shape[1:])
    return values


def scatter_sorted(values, axis):
    index = lax.axis_index(axis)
    for bit in bits_up(axis):
        pairs = values.reshape(-1, 2, *values.shape[1:])
        mine = jnp.where((index & bit) != 0, 1, 0)
        kept = lax.dynamic_index_in_dim(pairs, mine, 1, keepdims=False)
        sent = lax.dynamic_index_in_dim(pairs, 1 - mine, 1, keepdims=False)
        other = hop(sent.astype(bf16), axis, bit)
        values = kept.astype(f32) + other.astype(f32)
        if values.shape[0] > 1:
            values = values.astype(bf16)
    return values[0]


def scatter_relative(values, axis, dtype):
    for bit in bits_up(axis):
        pairs = values.reshape(-1, 2, *values.shape[1:])
        other = hop(pairs[:, 1].astype(bf16), axis, bit)
        values = pairs[:, 0].astype(dtype) + other.astype(dtype)
    return values[0]


def gather_relative(values, axis):
    values = values[None]
    for bit in bits_down(axis):
        values = jnp.stack([values, hop(values, axis, bit)], axis=1)
        values = values.reshape(-1, *values.shape[2:])
    return values


def gather_direct(values, axis):
    size = lax.axis_size(axis)
    if size > 8:
        return gather_relative(values, axis)
    return jnp.stack([values] + [hop(values, axis, r) for r in range(1, size)])


def bias_strip(rel_row, base, width):
    length = rel_row.shape[1]
    row = pltpu.roll(jnp.broadcast_to(rel_row, (8, length)), length - base, 1)[:1]
    rows = jnp.broadcast_to(row, (128, length))
    return pltpu.roll(rows, 0, 1, stride=1, stride_axis=0)[:, :width]


def part_scores(keys, queries_h, strip, col, part, core, key_len, causal):
    scores = dot(keys, queries_h, 1, 1)
    rows, cols = scores.shape
    blocks = rows // 128
    if strip is not None:
        shifts = [(blocks - 1 - j) * 128 + col for j in range(blocks)]
        bias = jnp.concatenate([strip[:, s : s + cols] for s in shifts], axis=0)
        scores = scores + bias
    where_core = core if part == 0 else 1 - core
    key_at = where_core * rows + lax.broadcasted_iota(jnp.int32, (rows, 1), 0)
    if causal:
        query_at = lax.broadcasted_iota(jnp.int32, (1, cols), 1) + col + causal * core
        return jnp.where(key_at <= query_at, scores, masked_score)
    return jnp.where(key_at < key_len, scores, masked_score)


def bases_of(size, rows, core, centre):
    own = centre - (rows // 128 - 1) * 128
    other = own - rows + core * (2 * rows)
    return own, other


def forward_kernel(has_bias, causal, centre, scal, q_ref, kvo_ref, kvt_ref, *rest):
    if has_bias:
        rel_ref, mixed_ref, lse_ref, so_ref, st_ref = rest
    else:
        mixed_ref, lse_ref = rest
    core, key_len, head = scal[0], scal[1], pl.program_id(1)
    q_rows, k_rows = q_ref.shape[1], kvo_ref.shape[1]
    lanes = q_ref.shape[2]
    lane_mask = lax.broadcasted_iota(jnp.int32, (1, lanes), 1) // DH == head
    if has_bias:
        own, other = bases_of(lanes, k_rows, core, centre)
        so_ref[...] = bias_strip(rel_ref[0], own, so_ref.shape[1])
        st_ref[...] = bias_strip(rel_ref[0], other, st_ref.shape[1])
    step = min(CHUNK, q_rows)
    for col in range(0, q_rows, step):
        queries = jnp.where(lane_mask, q_ref[0, col : col + step, :], 0.0).astype(bf16)
        own_s = part_scores(
            kvo_ref[0, :, :lanes], queries, so_ref if has_bias else None,
            col, 0, core, key_len, causal,
        )
        oth_s = part_scores(
            kvt_ref[0, :, :lanes], queries, st_ref if has_bias else None,
            col, 1, core, key_len, causal,
        )
        top = jnp.maximum(
            jnp.max(own_s, axis=0, keepdims=True), jnp.max(oth_s, axis=0, keepdims=True)
        )
        own_e, oth_e = jnp.exp(own_s - top), jnp.exp(oth_s - top)
        total = jnp.sum(own_e, axis=0, keepdims=True) + jnp.sum(oth_e, axis=0, keepdims=True)
        inverse = 1.0 / total
        mixed = dot(kvo_ref[0, :, lanes:], (own_e * inverse).astype(bf16), 0, 0)
        mixed = mixed + dot(kvt_ref[0, :, lanes:], (oth_e * inverse).astype(bf16), 0, 0)
        mixed = mixed.T.astype(bf16)
        mixed_ref[0, col : col + step, :] = jnp.where(
            lane_mask, mixed, mixed_ref[0, col : col + step, :]
        )
        lse_ref[0, 0, :, col : col + step] = top + jnp.log(total)


def turned(i, j):
    return (i + 1 - 2 * (i % 2), 0, 0)


def attend(scal, q, kvo, kvt, rel_rows, centre, causal):
    groups, q_rows, lanes = q.shape
    k_rows = kvo.shape[1]
    heads = lanes // DH
    has_bias = rel_rows is not None
    width = q_rows + (k_rows // 128 - 1) * 128
    in_specs = [
        pl.BlockSpec(memory_space=pltpu.SMEM),
        pl.BlockSpec((1, q_rows, lanes), lambda i, j: (i, 0, 0)),
        pl.BlockSpec((1, k_rows, 2 * lanes), lambda i, j: (i, 0, 0)),
        pl.BlockSpec((1, k_rows, 2 * lanes), turned),
    ]
    args = [scal, q, kvo, kvt]
    scratch = []
    if has_bias:
        in_specs.append(pl.BlockSpec((1, 1, rel_rows.shape[2]), lambda i, j: (i * heads + j, 0, 0)))
        args.append(rel_rows)
        scratch = [pltpu.VMEM((128, width), f32)] * 2
    return pl.pallas_call(
        functools.partial(forward_kernel, has_bias, causal, centre),
        grid=(groups, heads),
        in_specs=in_specs,
        out_specs=[
            pl.BlockSpec((1, q_rows, lanes), lambda i, j: (i, 0, 0)),
            pl.BlockSpec((1, 1, 1, q_rows), lambda i, j: (i, j, 0, 0)),
        ],
        out_shape=[
            jax.ShapeDtypeStruct((groups, q_rows, lanes), bf16),
            jax.ShapeDtypeStruct((groups, heads, 1, q_rows), f32),
        ],
        scratch_shapes=scratch,
        compiler_params=pltpu.CompilerParams(vmem_limit_bytes=40 * 2**20),
    )(*args)


def fold(strip):
    rows, width = strip.shape
    while rows > 8:
        rows //= 2
        strip = strip[:rows] + pltpu.roll(strip[rows:], width - rows, 1)
    return strip


def backward_kernel(has_bias, causal, centre, scal, q_ref, kvo_ref, kvt_ref, up_ref, lse_ref, *rest):
    if has_bias:
        rel_ref, dq_ref, dkvo_ref, dkvt_ref, drel_ref, so_ref, st_ref, go_ref, gt_ref = rest[:9]
        dq_acc, ko_acc, vo_acc, kt_acc, vt_acc = rest[9:]
    else:
        dq_ref, dkvo_ref, dkvt_ref, dq_acc, ko_acc, vo_acc, kt_acc, vt_acc = rest
    core, key_len, head = scal[0], scal[1], pl.program_id(1)
    q_rows, k_rows = q_ref.shape[1], kvo_ref.shape[1]
    lanes = q_ref.shape[2]
    lane_mask = lax.broadcasted_iota(jnp.int32, (1, lanes), 1) // DH == head
    if has_bias:
        own, other = bases_of(lanes, k_rows, core, centre)
        so_ref[...] = bias_strip(rel_ref[0], own, so_ref.shape[1])
        st_ref[...] = bias_strip(rel_ref[0], other, st_ref.shape[1])
        go_ref[...] = jnp.zeros_like(go_ref)
        gt_ref[...] = jnp.zeros_like(gt_ref)

    @pl.when(head == 0)
    def clear():
        for acc in (ko_acc, vo_acc, kt_acc, vt_acc):
            acc[...] = jnp.zeros_like(acc)

    step = min(CHUNK, q_rows)
    for col in range(0, q_rows, step):
        queries = jnp.where(lane_mask, q_ref[0, col : col + step, :], 0.0).astype(bf16)
        ups = jnp.where(lane_mask, up_ref[0, col : col + step, :], 0.0).astype(bf16)
        lse = lse_ref[0, 0, :, col : col + step]
        sides = []
        delta = jnp.zeros((1, step), f32)
        for part, kv_ref, s_ref, k_acc, v_acc in (
            (0, kvo_ref, so_ref if has_bias else None, ko_acc, vo_acc),
            (1, kvt_ref, st_ref if has_bias else None, kt_acc, vt_acc),
        ):
            scores = part_scores(
                kv_ref[0, :, :lanes], queries, s_ref, col, part, core, key_len, causal
            )
            probs = jnp.exp(scores - lse)
            v_acc[...] += dot(probs.astype(bf16), ups, 1, 0)
            dprobs = dot(kv_ref[0, :, lanes:], ups, 1, 1).astype(bf16).astype(f32)
            delta = delta + jnp.sum(probs * dprobs, axis=0, keepdims=True)
            sides.append((probs, dprobs))
        dq = jnp.zeros((lanes, step), f32)
        for (probs, dprobs), kv_ref, g_ref, k_acc in (
            (sides[0], kvo_ref, go_ref if has_bias else None, ko_acc),
            (sides[1], kvt_ref, gt_ref if has_bias else None, kt_acc),
        ):
            ds = (probs * (dprobs - delta)).astype(bf16)
            k_acc[...] += dot(ds, queries, 1, 0)
            dq = dq + dot(kv_ref[0, :, :lanes], ds, 0, 0)
            if has_bias:
                wide_ds = ds.astype(f32)
                blocks = k_rows // 128
                for j in range(blocks):
                    at = (blocks - 1 - j) * 128 + col
                    g_ref[:, at : at + step] += wide_ds[j * 128 : (j + 1) * 128]
        dq_acc[col : col + step, :] = jnp.where(
            lane_mask, dq.T, dq_acc[col : col + step, :]
        )
    if has_bias:
        drel_ref[0, 0, 0] = fold(go_ref[...])
        drel_ref[0, 0, 1] = fold(gt_ref[...])

    @pl.when(head == pl.num_programs(1) - 1)
    def write():
        dq_ref[0] = dq_acc[...].astype(bf16)
        dkvo_ref[0] = jnp.concatenate([ko_acc[...], vo_acc[...]], axis=1)
        dkvt_ref[0] = jnp.concatenate([kt_acc[...], vt_acc[...]], axis=1).astype(bf16)


def attend_back(scal, q, kvo, kvt, up, lse, rel_rows, centre, causal):
    groups, q_rows, lanes = q.shape
    k_rows = kvo.shape[1]
    heads = lanes // DH
    has_bias = rel_rows is not None
    width = q_rows + (k_rows // 128 - 1) * 128
    gwidth = width + 128
    per_group = lambda i, j: (i, 0, 0)
    in_specs = [
        pl.BlockSpec(memory_space=pltpu.SMEM),
        pl.BlockSpec((1, q_rows, lanes), per_group),
        pl.BlockSpec((1, k_rows, 2 * lanes), per_group),
        pl.BlockSpec((1, k_rows, 2 * lanes), turned),
        pl.BlockSpec((1, q_rows, lanes), per_group),
        pl.BlockSpec((1, 1, 1, q_rows), lambda i, j: (i, j, 0, 0)),
    ]
    args = [scal, q, kvo, kvt, up, lse]
    out_specs = [
        pl.BlockSpec((1, q_rows, lanes), per_group),
        pl.BlockSpec((1, k_rows, 2 * lanes), per_group),
        pl.BlockSpec((1, k_rows, 2 * lanes), turned),
    ]
    out_shape = [
        jax.ShapeDtypeStruct((groups, q_rows, lanes), bf16),
        jax.ShapeDtypeStruct((groups, k_rows, 2 * lanes), f32),
        jax.ShapeDtypeStruct((groups, k_rows, 2 * lanes), bf16),
    ]
    scratch = []
    if has_bias:
        in_specs.append(pl.BlockSpec((1, 1, rel_rows.shape[2]), lambda i, j: (i * heads + j, 0, 0)))
        args.append(rel_rows)
        out_specs.append(pl.BlockSpec((1, 1, 2, 8, gwidth), lambda i, j: (i, j, 0, 0, 0)))
        out_shape.append(jax.ShapeDtypeStruct((groups, heads, 2, 8, gwidth), f32))
        scratch = [pltpu.VMEM((128, width), f32)] * 2 + [pltpu.VMEM((128, gwidth), f32)] * 2
    scratch = scratch + [pltpu.VMEM((q_rows, lanes), f32)] + [pltpu.VMEM((k_rows, lanes), f32)] * 4
    return pl.pallas_call(
        functools.partial(backward_kernel, has_bias, causal, centre),
        grid=(groups, heads),
        in_specs=in_specs,
        out_specs=out_specs,
        out_shape=out_shape,
        scratch_shapes=scratch,
        compiler_params=pltpu.CompilerParams(vmem_limit_bytes=40 * 2**20),
    )(*args)


def rel_grad_rows(drel, core, k_rows, centre, length):
    groups, heads, parts, eight, gwidth = drel.shape
    drel = drel.reshape(groups * heads, parts, eight, gwidth)
    line = sum(jnp.roll(drel[:, :, r, :], -r, axis=-1) for r in range(eight))
    line = jnp.roll(line, 127, axis=-1)
    own, other = bases_of(0, k_rows, core, centre)
    total = jnp.zeros((line.shape[0], length + gwidth + 128), f32)
    for part, base in ((0, own), (1, other)):
        old = lax.dynamic_slice_in_dim(total, base + 1, gwidth, 1)
        total = lax.dynamic_update_slice_in_dim(total, old + line[:, part], base + 1, 1)
    return total[:, 128 : 128 + length]


def rms_forward(inputs, gain_row):
    inverse = lax.rsqrt(jnp.mean(inputs * inputs, axis=-1, keepdims=True) + epsilon)
    return ((inputs * inverse * gain_row).astype(bf16), inverse)


def rms_backward(inputs, gain_row, inverse, upstream):
    upstream = upstream.astype(bf16).astype(f32)
    gain_grad = jnp.sum(upstream * inputs * inverse, axis=0)
    inner = jnp.sum(upstream * gain_row * inputs, axis=-1, keepdims=True)
    result = inverse * gain_row * upstream - inputs * (inverse**3 * inner / inputs.shape[-1])
    return (result, gain_grad)


def project(rows, weights):
    return jnp.einsum("rk,nkc->nrc", rows, weights, preferred_element_type=f32)


def project_back(grads, weights):
    return jnp.einsum("nrc,nkc->rk", grads, weights, preferred_element_type=f32)


def outer(rows, grads):
    return jnp.einsum("rk,nrc->nkc", rows, grads, preferred_element_type=f32)


MESH = pl.DeviceIdType.MESH


def greet(peers):
    barrier = pltpu.get_barrier_semaphore()
    for peer in peers:
        pl.semaphore_signal(barrier, inc=1, device_id=peer, device_id_type=MESH)
    pl.semaphore_wait(barrier, len(peers))


def remote(src, dst, send_sem, recv_sem, peer):
    return pltpu.make_async_remote_copy(
        src_ref=src, dst_ref=dst, send_sem=send_sem, recv_sem=recv_sem,
        device_id=peer, device_id_type=MESH,
    )


def start_kernel(
    units, vocab, ids_ref, table_ref, shard_ref, full_ref, mine_ref,
    ids_all, ids_col, looked, from_x, from_z1, from_z2, total,
    own_sem, w_send, w_recv, id_send, id_recv, e_send, e_recv,
):
    wide, narrow = lax.axis_index("wide"), lax.axis_index("narrow")
    flip = lambda bit: wide + bit - 2 * bit * (wide // bit % 2)
    z2, z1, x = wide // 4, wide // 2 % 2, wide % 2
    at_x, at_z1, at_z2 = (flip(1), narrow), (flip(2), narrow), (flip(4), narrow)
    at_core = (wide, narrow + 1 - 2 * (narrow % 2))
    at_y = (wide, narrow + 2 - 4 * (narrow // 2))
    others = []
    for r in range(1, 8):
        there = wide
        for bit in (1, 2, 4):
            if r & bit:
                there = there + bit - 2 * bit * (wide // bit % 2)
        others.append((there, narrow))
    greet(others + [at_core, at_y])

    def own(j):
        return pltpu.make_async_copy(shard_ref.at[j], full_ref.at[j, 0, z2, z1, x], own_sem.at[j])

    def copy(j, stage):
        if stage == 0:
            src, dst, peer = shard_ref.at[j], full_ref.at[j, 0, z2, z1, x], at_z2
        elif stage == 1:
            src = dst = full_ref.at[j, 0, :, z1, x]
            peer = at_z1
        elif stage == 2:
            src = dst = full_ref.at[j, 0, :, :, x]
            peer = at_x
        elif stage == 3:
            src, dst, peer = full_ref.at[j, 0], full_ref.at[j, 2], at_y
        elif stage == 4:
            src, dst, peer = full_ref.at[j, 0], full_ref.at[j, 1], at_core
        else:
            src, dst, peer = full_ref.at[j, 2], full_ref.at[j, 3], at_core
        return remote(src, dst, w_send.at[j, stage], w_recv.at[j, stage], peer)

    def advance(j, stage):
        if stage == 1:
            own(j).wait()
        if stage > 0:
            copy(j, {5: 3}.get(stage, stage - 1)).wait_recv()
        copy(j, stage).start()
        if stage == 3:
            copy(j, 4).start()

    def ids_copy(r):
        return remote(
            ids_all.at[0], ids_all.at[r], id_send.at[r], id_recv.at[r], others[r - 1]
        )

    ids_all[0] = ids_ref[...]
    for r in range(1, 8):
        ids_copy(r).start()
    for j in range(units):
        own(j).start()
    for j in range(min(3, units)):
        advance(j, 0)

    rows = ids_ref.shape[1]
    cut = total.shape[0]

    def look_up(r):
        if r > 0:
            ids_copy(r).wait_recv()
        ids = ids_all[r] - wide * vocab
        for t in range(rows // 128):
            ids_col[t * 128 : (t + 1) * 128] = jnp.broadcast_to(
                ids[:, t * 128 : (t + 1) * 128], (128, 128)
            ).T
        total[...] = jnp.zeros_like(total)

        def add(k, unused):
            lane = lax.broadcasted_iota(jnp.int32, (rows, 128), 1) + k * 512
            col = ids_col[...]
            hot = jnp.concatenate(
                [(col == lane + q * 128).astype(f32) for q in range(4)], axis=1
            ).astype(bf16)
            block = table_ref[pl.ds(pl.multiple_of(k * 512, 512), 512), :]
            total[...] += dot(hot, block, 1, 0)
            return unused

        lax.fori_loop(0, table_ref.shape[0] // 512, add, 0)
        looked[r] = total[...].astype(bf16)

    def e_copy(hop_at, index):
        if hop_at == 0:
            src, dst, peer = looked.at[2 * index + 1], from_x.at[index], at_x
        elif hop_at == 1:
            src, dst, peer = looked.at[4 * index + 2], from_z1.at[index], at_z1
        else:
            src, dst, peer = looked.at[4], from_z2.at[0], at_z2
        slot = (0, 4, 6)[hop_at] + index
        return remote(src, dst, e_send.at[slot], e_recv.at[slot], peer)

    order = (3, 1, 2, 0)
    todo = []
    for j in range(units):
        todo += [(5 * j + 6 * s + s * s, j, s) for s in (1, 2, 3, 5)]
        if j >= 3:
            todo.append((5 * j, j, 0))
    todo = [(j, s) for unused, j, s in sorted(todo)]
    steps = []
    for s in order:
        steps.append(("odd", s))
    for s in order:
        steps.append(("even", s))
    for s in order:
        steps.append(("merge", s))
    share = -(-len(todo) // (len(steps) + 4))
    for kind, s in steps:
        if kind == "odd":
            look_up(2 * s + 1)
            e_copy(0, s).start()
        elif kind == "even":
            look_up(2 * s)
        else:
            e_copy(0, s).wait_recv()
            looked[2 * s] = looked[2 * s] + from_x[s]
            if s % 2 == 1:
                e_copy(1, s // 2).start()
            else:
                e_copy(1, s // 2).wait_recv()
                looked[2 * s] = looked[2 * s] + from_z1[s // 2]
                if s == 2:
                    e_copy(2, 0).start()
        for j, stage in todo[:share]:
            advance(j, stage)
        todo = todo[share:]
    for j, stage in todo:
        advance(j, stage)
    e_copy(2, 0).wait_recv()
    mine_ref[...] = looked[0] + from_z2[0]
    for j in range(units):
        for stage in range(6):
            copy(j, stage).wait_send()
        for stage in (4, 5):
            copy(j, stage).wait_recv()
    for r in range(1, 8):
        ids_copy(r).wait_send()
    for hop_at, count in ((0, 4), (1, 2), (2, 1)):
        for index in range(count):
            e_copy(hop_at, index).wait_send()


def start_phase(ids, table_low, shards):
    units, slim, columns = shards.shape
    rows, (vocab, width) = ids.shape[1], table_low.shape
    padded = -(-vocab // 512) * 512
    table_low = jnp.pad(table_low, ((0, padded - vocab), (0, 0)))
    any_space = pl.BlockSpec(memory_space=pl.ANY)
    vmem = pl.BlockSpec(memory_space=pltpu.VMEM)
    dma = pltpu.SemaphoreType.DMA
    full, mine = pl.pallas_call(
        functools.partial(start_kernel, units, vocab),
        in_specs=[vmem, vmem, any_space],
        out_specs=[any_space, vmem],
        out_shape=[
            jax.ShapeDtypeStruct((units, 4, 2, 2, 2, slim, columns), bf16),
            jax.ShapeDtypeStruct((rows, width), bf16),
        ],
        scratch_shapes=[
            pltpu.VMEM((8, 1, rows), jnp.int32),
            pltpu.VMEM((rows, 128), jnp.int32),
            pltpu.VMEM((8, rows, width), bf16),
            pltpu.VMEM((4, rows, width), bf16),
            pltpu.VMEM((2, rows, width), bf16),
            pltpu.VMEM((1, rows, width), bf16),
            pltpu.VMEM((rows, width), f32),
            dma((units,)),
            dma((units, 6)),
            dma((units, 6)),
            dma((8,)),
            dma((8,)),
            dma((7,)),
            dma((7,)),
        ],
        compiler_params=pltpu.CompilerParams(
            collective_id=0, has_side_effects=True, vmem_limit_bytes=52 * 2**20
        ),
        cost_estimate=pl.CostEstimate(
            flops=2 * 8 * rows * padded * width, bytes_accessed=2 * 4 * 8 * units * slim * columns,
            transcendentals=0,
        ),
    )(ids, table_low, shards)
    return full.reshape(units, 4, 8 * slim, columns), mine


def body(
    enc_ids, enc_len, tgt_ids, tgt_len, span_mask, buckets,
    attn_in, attn_out, ff_in, ff_out, table, gains, rel,
    mom_attn_in, mom_attn_out, mom_ff_in, mom_ff_out, mom_table, mom_gains, mom_rel,
    avg_attn_in, avg_attn_out, avg_ff_in, avg_ff_out, avg_table, avg_gains, avg_rel,
):
    wide_size = lax.axis_size("wide")
    narrow_size = lax.axis_size("narrow")
    wide_index = lax.axis_index("wide")
    narrow_index = lax.axis_index("narrow")
    micro = narrow_index // 2
    core = narrow_index % 2
    width = table.shape[1]
    vocab = table.shape[0]
    enc_rows = enc_ids.shape[2] // 2
    dec_rows = tgt_ids.shape[2] // 2
    centre = (buckets.shape[0] + 1) // 2 - 1
    lanes = attn_out.shape[1]
    heads_here = lanes // DH
    slim = attn_in.shape[1]

    shards = []
    for layer in range(3):
        packed = attn_in[layer].reshape(slim, heads_here, 3, DH).transpose(0, 2, 1, 3)
        shards.append(jnp.concatenate([packed.reshape(slim, -1), attn_out[layer].T], axis=1))
    for layer in range(2):
        shards.append(ff_in[layer])
        shards.append(ff_out[layer].T)
    shards = jnp.stack(shards).astype(bf16)
    groups = narrow_index ^ jnp.arange(narrow_size)
    small = jnp.concatenate([gains.reshape(-1), rel.reshape(-1)])
    small = lax.all_gather(small, "narrow", axis=0, tiled=False)
    cut = gains.size
    gains_full = small[:, :cut].reshape(narrow_size, *gains.shape).transpose(1, 0, 2)
    gains_full = gains_full.reshape(gains.shape[0], -1)
    rel_full = small[:, cut:].reshape(narrow_size, *rel.shape).transpose(1, 2, 0, 3)
    rel_full = rel_full.reshape(rel.shape[0], rel.shape[1], -1)
    onehot_rev = (buckets[::-1][:, None] == jnp.arange(rel.shape[1])[None, :]).astype(f32)
    onehot_rev = jnp.pad(onehot_rev, ((0, 1), (0, 0)))
    rel_rows = [
        jnp.dot(onehot_rev, rel_full[i], precision=highest)
        .T.reshape(narrow_size, heads_here, 1, -1)[groups]
        .reshape(narrow_size * heads_here, 1, -1)
        for i in range(2)
    ]

    my_enc = lax.dynamic_slice(enc_ids, (micro, 0, core * enc_rows), (1, 1, enc_rows))
    others = wide_index ^ jnp.arange(wide_size)
    targets_micro = lax.dynamic_index_in_dim(tgt_ids, micro, 0, keepdims=False)[others]
    shifted = jnp.concatenate(
        [jnp.zeros((wide_size, 1), jnp.int32), targets_micro[:, :-1]], axis=1
    )
    dec_all = lax.dynamic_slice_in_dim(shifted, core * dec_rows, dec_rows, 1)
    table_low = table.astype(bf16)
    enc_all = gather_direct(my_enc.reshape(enc_rows), "wide")
    tokens = jnp.concatenate([enc_all, dec_all], axis=1)
    local = tokens - wide_index * vocab
    held = (local >= 0) & (local < vocab)
    local = jnp.where(held, local, 0)
    if wide_size == 8 and narrow_size == 4:
        my_ids = jnp.concatenate([my_enc.reshape(enc_rows), dec_all[0]])[None]
        gathered, mine = start_phase(my_ids, table_low, shards)
    else:
        gathered = []
        for shard in shards:
            column = gather_sorted(shard, "wide").reshape(width, -1)
            pair = jnp.stack([column, hop(column, "narrow", 2)])
            pair = jnp.stack([pair, swap(pair)], axis=1)
            gathered.append(pair.reshape(narrow_size, width, -1))
        rows = table_low[local.reshape(-1)]
        rows = jnp.where(held.reshape(-1)[:, None], rows, 0).astype(bf16)
        mine = scatter_relative(rows.reshape(*local.shape, width), "wide", bf16)
    low_in = [gathered[i][:, :, : 3 * lanes] for i in range(3)]
    low_out = [gathered[i][:, :, 3 * lanes :] for i in range(3)]
    low_up = [gathered[3], gathered[5]]
    low_down = [gathered[4], gathered[6]]

    enc0 = mine[:enc_rows].astype(f32)
    dec0 = mine[enc_rows:].astype(f32)

    key_len = lax.dynamic_slice(enc_len, (micro, 0), (1, 1)).reshape(())
    scal = jnp.stack([core, key_len]).astype(jnp.int32)

    def attn_forward(state, gain_row, layer, source, rel_row, causal):
        normed, inverse = rms_forward(state, gain_row)
        kv = project(normed if source is None else source, low_in[layer][:, :, lanes:]).astype(bf16)
        kv_other = swap(kv)
        q = project(normed, low_in[layer][:, :, :lanes]).astype(bf16)
        mixed, lse = attend(scal, q, kv, kv_other, rel_row, centre, causal)
        update = project_back(mixed, low_out[layer])
        return (state + update, (state, inverse, normed, q, kv, kv_other, mixed, lse))

    def attn_backward(saved, upstream, gain_row, layer, source, rel_row, causal):
        state, inverse, normed, q, kv, kv_other, mixed, lse = saved
        up = upstream.astype(bf16)
        out_grad = outer(up, mixed)
        mixed_grad = project(up, low_out[layer]).astype(bf16)
        outs = attend_back(scal, q, kv, kv_other, mixed_grad, lse, rel_row, centre, causal)
        dq, dkv_own, dkv_other = outs[:3]
        dkv = (dkv_own + swap(dkv_other).astype(f32)).astype(bf16)
        q_grad = outer(normed, dq)
        kv_grad = outer(normed if source is None else source, dkv)
        normed_grad = project_back(dq, low_in[layer][:, :, :lanes])
        kv_back = project_back(dkv, low_in[layer][:, :, lanes:])
        if source is None:
            normed_grad = normed_grad + kv_back
        state_grad, gain_grad = rms_backward(state, gain_row, inverse, normed_grad)
        grads = jnp.concatenate([q_grad, kv_grad, out_grad], axis=2).astype(bf16)
        return (upstream + state_grad, gain_grad, grads, kv_back, outs[3] if rel_row is not None else None)

    def ff_forward(state, gain_row, layer):
        normed, inverse = rms_forward(state, gain_row)
        pre = project(normed, low_up[layer])
        hidden = jax.nn.gelu(pre).astype(bf16)
        return (state + project_back(hidden, low_down[layer]), (state, inverse, normed, pre, hidden))

    def ff_backward(saved, upstream, gain_row, layer):
        state, inverse, normed, pre, hidden = saved
        up = upstream.astype(bf16)
        out_grad = outer(up, hidden).astype(bf16)
        hidden_grad = project(up, low_down[layer]).astype(bf16).astype(f32)
        unused, gelu_back = jax.vjp(jax.nn.gelu, pre)
        pre_grad = gelu_back(hidden_grad)[0].astype(bf16)
        in_grad = outer(normed, pre_grad).astype(bf16)
        normed_grad = project_back(pre_grad, low_up[layer])
        state_grad, gain_grad = rms_backward(state, gain_row, inverse, normed_grad)
        return (upstream + state_grad, gain_grad, in_grad, out_grad)

    def scatter(grad):
        pairs = grad.reshape(2, 2, width, -1)
        across = pairs[:, 0].astype(f32) + swap(pairs[:, 1]).astype(f32)
        column = across[0] + hop(across[1].astype(bf16), "narrow", 2).astype(f32)
        return scatter_sorted(column.astype(bf16).reshape(wide_size, slim, -1), "wide")

    enc1, saved_a = attn_forward(enc0, gains_full[0], 0, None, rel_rows[0], 0)
    enc2, saved_b = ff_forward(enc1, gains_full[1], 0)
    encoded, enc_inverse = rms_forward(enc2, gains_full[2])
    dec1, saved_c = attn_forward(dec0, gains_full[3], 1, None, rel_rows[1], dec_rows)
    dec2, saved_d = attn_forward(dec1, gains_full[4], 2, encoded, None, 0)
    dec3, saved_e = ff_forward(dec2, gains_full[5], 1)
    final_gain = gains_full[6] * width ** (-0.5)
    final, final_inverse = rms_forward(dec3, final_gain)

    row_weight = (jnp.arange(2 * dec_rows)[None, None, :] < tgt_len[:, :, None]).astype(
        f32
    ) * span_mask.astype(f32)
    count = jnp.sum(row_weight)
    weights_micro = lax.dynamic_index_in_dim(row_weight, micro, 0, keepdims=False)[others]
    weights = lax.dynamic_slice_in_dim(weights_micro, core * dec_rows, dec_rows, 1).reshape(-1)
    targets = lax.dynamic_slice_in_dim(targets_micro, core * dec_rows, dec_rows, 1).reshape(-1)
    targets = targets - wide_index * vocab
    final_all = gather_relative(final, "wide").reshape(-1, width)
    logits = dot(final_all, table_low, 1, 1)
    target_hot = jnp.arange(vocab)[None, :] == targets[:, None]
    top = jnp.max(logits, axis=-1)
    total = jnp.sum(jnp.exp(logits - top[:, None]), axis=-1)
    hits = jnp.sum(jnp.where(target_hot, logits, 0.0), axis=-1)
    stats = jnp.stack([top, total, hits]).reshape(3, wide_size, dec_rows)
    if wide_size > 8:
        stats = lax.all_gather(stats[:, others], "wide", axis=0, tiled=False)[:, :, others]
    else:
        stats = jnp.stack(
            [stats]
            + [
                hop(stats, "wide", r)[:, [q ^ r for q in range(wide_size)]]
                for r in range(1, wide_size)
            ]
        )
    stats = stats.reshape(wide_size, 3, -1)
    best = jnp.max(stats[:, 0], axis=0)
    log_total = best + jnp.log(jnp.sum(stats[:, 1] * jnp.exp(stats[:, 0] - best[None]), axis=0))
    loss_rows = weights * (log_total - jnp.sum(stats[:, 2], axis=0))
    loss_part = jnp.sum(loss_rows[:dec_rows])
    logit_grad = (
        (weights / count)[:, None]
        * (jnp.exp(logits - log_total[:, None]) - target_hot.astype(f32))
    ).astype(bf16)
    final_grad = scatter_relative(
        dot(logit_grad, table_low, 1, 0).reshape(wide_size, dec_rows, width), "wide", f32
    )

    gain_grads = [None] * 7
    dec_grad, gain_raw = rms_backward(dec3, final_gain, final_inverse, final_grad)
    gain_grads[6] = gain_raw * width ** (-0.5)
    dec_grad, gain_grads[5], up1, down1 = ff_backward(saved_e, dec_grad, gains_full[5], 1)
    dec_grad, gain_grads[4], attn2, source_grad, unused = attn_backward(
        saved_d, dec_grad, gains_full[4], 2, encoded, None, 0
    )
    dec_grad, gain_grads[3], attn1, unused, drel_dec = attn_backward(
        saved_c, dec_grad, gains_full[3], 1, None, rel_rows[1], dec_rows
    )
    enc_grad, gain_grads[2] = rms_backward(enc2, gains_full[2], enc_inverse, source_grad)
    enc_grad, gain_grads[1], up0, down0 = ff_backward(saved_b, enc_grad, gains_full[1], 0)
    enc_grad, gain_grads[0], attn0, unused, drel_enc = attn_backward(
        saved_a, enc_grad, gains_full[0], 0, None, rel_rows[0], 0
    )
    reduced = [scatter(grad) for grad in (attn0, attn1, attn2, up0, down0, up1, down1)]

    row_grads = jnp.concatenate([enc_grad, dec_grad], axis=0).astype(bf16)
    padded = -(-vocab // 64) * 64
    slots = jnp.arange(padded)
    local = jnp.where(held, local, -1).reshape(-1, 2, local.shape[1])
    halves, part_grads = [], []
    half = width // 2
    for start in (0, half):
        rows = row_grads[None, :, start : start + half]
        for bit in list(bits_down("wide"))[:-1]:
            rows = jnp.stack([rows, hop(rows, "wide", bit)], axis=1)
            rows = rows.reshape(-1, *rows.shape[2:])
        far = hop(rows, "wide", 1)
        partial = dot(logit_grad, final_all[:, start : start + half], 0, 0)
        partial = jnp.pad(partial, ((0, padded - vocab), (0, 0)))
        for at, values in ((local[:, 0], rows), (local[:, 1], far)):
            token_hot = (slots[:, None] == at.reshape(-1)[None, :]).astype(bf16)
            partial = partial + dot(token_hot, values.reshape(-1, half), 1, 0)
        quarters = partial.astype(bf16).reshape(narrow_size, padded // narrow_size, half)
        part = scatter_sorted(quarters, "narrow").astype(bf16)
        part_grads.append(part.astype(f32))
        halves.append(gather_sorted(part, "narrow").reshape(padded, half)[:vocab])
    table_grad = jnp.concatenate(halves, axis=1).astype(f32)

    length = onehot_rev.shape[0]
    rel_grad = jnp.stack(
        [
            jnp.dot(rel_grad_rows(drel_enc, core, enc_rows, centre, length), onehot_rev, precision=highest),
            jnp.dot(rel_grad_rows(drel_dec, core, dec_rows, centre, length), onehot_rev, precision=highest),
        ]
    )
    rel_grad = rel_grad.reshape(2, narrow_size, heads_here, -1)[:, groups]
    rel_grad = rel_grad.reshape(2, narrow_size * heads_here, -1)
    gain_total, rel_total, loss_sum = lax.psum(
        (jnp.stack(gain_grads), rel_grad, loss_part), ("wide", "narrow")
    )
    squares = sum(jnp.sum(grad * grad) for grad in reduced + part_grads)
    square_sum = lax.psum(squares, ("wide", "narrow"))
    square_sum = square_sum + jnp.sum(gain_total * gain_total) + jnp.sum(rel_total * rel_total)
    gain_mine = lax.dynamic_slice_in_dim(gain_total, narrow_index * lanes, lanes, 1)
    rel_mine = lax.dynamic_slice_in_dim(
        rel_total, narrow_index * heads_here, heads_here, 1
    ).transpose(0, 2, 1)

    def unpack_in(grad):
        grad = grad[:, : 3 * lanes].reshape(slim, 3, heads_here, DH).transpose(0, 2, 1, 3)
        return grad.reshape(slim, -1)

    grads = (
        jnp.stack([unpack_in(reduced[i]) for i in range(3)]),
        jnp.stack([reduced[i][:, 3 * lanes :].T for i in range(3)]),
        jnp.stack([reduced[3], reduced[5]]),
        jnp.stack([reduced[4].T, reduced[6].T]),
        table_grad,
        gain_mine,
        rel_mine,
    )
    norm = jnp.sqrt(square_sum)
    scale = jnp.minimum(1.0, clip_norm / norm)
    base_rate = math.sqrt(PARAMS) / (3.0 * clip_norm)
    matrix_rate = base_rate / math.sqrt(width)
    rates = (
        matrix_rate, 16.0 * matrix_rate, matrix_rate, matrix_rate,
        base_rate, 0.3 * base_rate, 0.3 * base_rate,
    )
    params = (attn_in, attn_out, ff_in, ff_out, table, gains, rel)
    moms = (mom_attn_in, mom_attn_out, mom_ff_in, mom_ff_out, mom_table, mom_gains, mom_rel)
    avgs = (avg_attn_in, avg_attn_out, avg_ff_in, avg_ff_out, avg_table, avg_gains, avg_rel)
    fresh, scaled_grads, averages = ([], [], [])
    for index in range(7):
        clipped = grads[index] * scale
        moment = momentum_decay * moms[index] + clipped
        weight = params[index] - rates[index] * (clipped + momentum_decay * moment)
        fresh.append(weight)
        scaled_grads.append(clipped)
        averages.append(average_decay * avgs[index] + (1.0 - average_decay) * weight)
    return (loss_sum, count, norm, *fresh, *scaled_grads, *averages)


def solution(mesh):
    weights = (
        P(None, "wide", "narrow"),
        P(None, "narrow", "wide"),
        P(None, "wide", "narrow"),
        P(None, "narrow", "wide"),
        P("wide", None),
        P(None, "narrow"),
        P(None, None, "narrow"),
    )
    in_specs = (P(None, "wide", None), P(None, "wide"), P(), P(), P(), P()) + weights * 3
    out_specs = (P(), P(), P()) + weights * 3
    return jax.shard_map(body, mesh=mesh, in_specs=in_specs, out_specs=out_specs, check_vma=False)
```

```python
import functools
import math

import jax
import jax.numpy as jnp
from jax import lax
from jax.experimental import pallas as pl
from jax.experimental.pallas import tpu as pltpu
from jax.sharding import PartitionSpec as P

DH = 64
PARAMS = 41195520

epsilon = 1e-06
masked_score = -1000000000.0
momentum_decay = 0.9
average_decay = 0.9
clip_norm = 0.02
highest = lax.Precision.HIGHEST
bf16 = jnp.bfloat16
f32 = jnp.float32
CHUNK = 256


def dot(left, right, left_dim, right_dim):
    return lax.dot_general(
        left, right, (((left_dim,), (right_dim,)), ((), ())), preferred_element_type=f32
    )


def hop(values, axis, bit):
    size = lax.axis_size(axis)
    return lax.ppermute(values, axis, [(i, i ^ bit) for i in range(size)])


def swap(values):
    return hop(values, "narrow", 1)


def bits_down(axis):
    bit = lax.axis_size(axis) // 2
    while bit:
        yield bit
        bit //= 2


def bits_up(axis):
    return reversed(list(bits_down(axis)))


def gather_sorted(values, axis):
    index = lax.axis_index(axis)
    values = values[None]
    for bit in bits_down(axis):
        other = hop(values, axis, bit)
        upper = (index & bit) != 0
        values = jnp.stack(
            [jnp.where(upper, other, values), jnp.where(upper, values, other)], axis=1
        ).reshape(-1, *values.shape[1:])
    return values


def scatter_sorted(values, axis):
    index = lax.axis_index(axis)
    for bit in bits_up(axis):
        pairs = values.reshape(-1, 2, *values.shape[1:])
        mine = jnp.where((index & bit) != 0, 1, 0)
        kept = lax.dynamic_index_in_dim(pairs, mine, 1, keepdims=False)
        sent = lax.dynamic_index_in_dim(pairs, 1 - mine, 1, keepdims=False)
        other = hop(sent.astype(bf16), axis, bit)
        values = kept.astype(f32) + other.astype(f32)
        if values.shape[0] > 1:
            values = values.astype(bf16)
    return values[0]


def scatter_relative(values, axis, dtype):
    for bit in bits_up(axis):
        pairs = values.reshape(-1, 2, *values.shape[1:])
        other = hop(pairs[:, 1].astype(bf16), axis, bit)
        values = pairs[:, 0].astype(dtype) + other.astype(dtype)
    return values[0]


def gather_relative(values, axis):
    values = values[None]
    for bit in bits_down(axis):
        values = jnp.stack([values, hop(values, axis, bit)], axis=1)
        values = values.reshape(-1, *values.shape[2:])
    return values


def gather_direct(values, axis):
    size = lax.axis_size(axis)
    if size > 8:
        return gather_relative(values, axis)
    return jnp.stack([values] + [hop(values, axis, r) for r in range(1, size)])


def bias_strip(rel_row, base, width):
    length = rel_row.shape[1]
    row = pltpu.roll(jnp.broadcast_to(rel_row, (8, length)), length - base, 1)[:1]
    rows = jnp.broadcast_to(row, (128, length))
    return pltpu.roll(rows, 0, 1, stride=1, stride_axis=0)[:, :width]


def part_scores(keys, queries_h, strip, col, part, core, key_len, causal):
    scores = dot(keys, queries_h, 1, 1)
    rows, cols = scores.shape
    blocks = rows // 128
    if strip is not None:
        shifts = [(blocks - 1 - j) * 128 + col for j in range(blocks)]
        bias = jnp.concatenate([strip[:, s : s + cols] for s in shifts], axis=0)
        scores = scores + bias
    where_core = core if part == 0 else 1 - core
    key_at = where_core * rows + lax.broadcasted_iota(jnp.int32, (rows, 1), 0)
    if causal:
        query_at = lax.broadcasted_iota(jnp.int32, (1, cols), 1) + col + causal * core
        return jnp.where(key_at <= query_at, scores, masked_score)
    return jnp.where(key_at < key_len, scores, masked_score)


def bases_of(size, rows, core, centre):
    own = centre - (rows // 128 - 1) * 128
    other = own - rows + core * (2 * rows)
    return own, other


def forward_kernel(has_bias, causal, centre, scal, q_ref, kvo_ref, kvt_ref, *rest):
    if has_bias:
        rel_ref, mixed_ref, lse_ref, so_ref, st_ref = rest
    else:
        mixed_ref, lse_ref = rest
    core, key_len, head = scal[0], scal[1], pl.program_id(1)
    q_rows, k_rows = q_ref.shape[1], kvo_ref.shape[1]
    lanes = q_ref.shape[2]
    lane_mask = lax.broadcasted_iota(jnp.int32, (1, lanes), 1) // DH == head
    if has_bias:
        own, other = bases_of(lanes, k_rows, core, centre)
        so_ref[...] = bias_strip(rel_ref[0], own, so_ref.shape[1])
        st_ref[...] = bias_strip(rel_ref[0], other, st_ref.shape[1])
    step = min(CHUNK, q_rows)
    for col in range(0, q_rows, step):
        queries = jnp.where(lane_mask, q_ref[0, col : col + step, :], 0.0).astype(bf16)
        own_s = part_scores(
            kvo_ref[0, :, :lanes], queries, so_ref if has_bias else None,
            col, 0, core, key_len, causal,
        )
        oth_s = part_scores(
            kvt_ref[0, :, :lanes], queries, st_ref if has_bias else None,
            col, 1, core, key_len, causal,
        )
        top = jnp.maximum(
            jnp.max(own_s, axis=0, keepdims=True), jnp.max(oth_s, axis=0, keepdims=True)
        )
        own_e, oth_e = jnp.exp(own_s - top), jnp.exp(oth_s - top)
        total = jnp.sum(own_e, axis=0, keepdims=True) + jnp.sum(oth_e, axis=0, keepdims=True)
        inverse = 1.0 / total
        mixed = dot(kvo_ref[0, :, lanes:], (own_e * inverse).astype(bf16), 0, 0)
        mixed = mixed + dot(kvt_ref[0, :, lanes:], (oth_e * inverse).astype(bf16), 0, 0)
        mixed = mixed.T.astype(bf16)
        mixed_ref[0, col : col + step, :] = jnp.where(
            lane_mask, mixed, mixed_ref[0, col : col + step, :]
        )
        lse_ref[0, 0, :, col : col + step] = top + jnp.log(total)


def turned(i, j):
    return (i + 1 - 2 * (i % 2), 0, 0)


def attend(scal, q, kvo, kvt, rel_rows, centre, causal):
    groups, q_rows, lanes = q.shape
    k_rows = kvo.shape[1]
    heads = lanes // DH
    has_bias = rel_rows is not None
    width = q_rows + (k_rows // 128 - 1) * 128
    in_specs = [
        pl.BlockSpec(memory_space=pltpu.SMEM),
        pl.BlockSpec((1, q_rows, lanes), lambda i, j: (i, 0, 0)),
        pl.BlockSpec((1, k_rows, 2 * lanes), lambda i, j: (i, 0, 0)),
        pl.BlockSpec((1, k_rows, 2 * lanes), turned),
    ]
    args = [scal, q, kvo, kvt]
    scratch = []
    if has_bias:
        in_specs.append(pl.BlockSpec((1, 1, rel_rows.shape[2]), lambda i, j: (i * heads + j, 0, 0)))
        args.append(rel_rows)
        scratch = [pltpu.VMEM((128, width), f32)] * 2
    return pl.pallas_call(
        functools.partial(forward_kernel, has_bias, causal, centre),
        grid=(groups, heads),
        in_specs=in_specs,
        out_specs=[
            pl.BlockSpec((1, q_rows, lanes), lambda i, j: (i, 0, 0)),
            pl.BlockSpec((1, 1, 1, q_rows), lambda i, j: (i, j, 0, 0)),
        ],
        out_shape=[
            jax.ShapeDtypeStruct((groups, q_rows, lanes), bf16),
            jax.ShapeDtypeStruct((groups, heads, 1, q_rows), f32),
        ],
        scratch_shapes=scratch,
        compiler_params=pltpu.CompilerParams(vmem_limit_bytes=40 * 2**20),
    )(*args)


def fold(strip):
    rows, width = strip.shape
    while rows > 8:
        rows //= 2
        strip = strip[:rows] + pltpu.roll(strip[rows:], width - rows, 1)
    return strip


def backward_kernel(has_bias, causal, centre, scal, q_ref, kvo_ref, kvt_ref, up_ref, lse_ref, *rest):
    if has_bias:
        rel_ref, dq_ref, dkvo_ref, dkvt_ref, drel_ref, so_ref, st_ref, go_ref, gt_ref = rest[:9]
        dq_acc, ko_acc, vo_acc, kt_acc, vt_acc = rest[9:]
    else:
        dq_ref, dkvo_ref, dkvt_ref, dq_acc, ko_acc, vo_acc, kt_acc, vt_acc = rest
    core, key_len, head = scal[0], scal[1], pl.program_id(1)
    q_rows, k_rows = q_ref.shape[1], kvo_ref.shape[1]
    lanes = q_ref.shape[2]
    lane_mask = lax.broadcasted_iota(jnp.int32, (1, lanes), 1) // DH == head
    if has_bias:
        own, other = bases_of(lanes, k_rows, core, centre)
        so_ref[...] = bias_strip(rel_ref[0], own, so_ref.shape[1])
        st_ref[...] = bias_strip(rel_ref[0], other, st_ref.shape[1])
        go_ref[...] = jnp.zeros_like(go_ref)
        gt_ref[...] = jnp.zeros_like(gt_ref)

    @pl.when(head == 0)
    def clear():
        for acc in (ko_acc, vo_acc, kt_acc, vt_acc):
            acc[...] = jnp.zeros_like(acc)

    step = min(CHUNK, q_rows)
    for col in range(0, q_rows, step):
        queries = jnp.where(lane_mask, q_ref[0, col : col + step, :], 0.0).astype(bf16)
        ups = jnp.where(lane_mask, up_ref[0, col : col + step, :], 0.0).astype(bf16)
        lse = lse_ref[0, 0, :, col : col + step]
        sides = []
        delta = jnp.zeros((1, step), f32)
        for part, kv_ref, s_ref, k_acc, v_acc in (
            (0, kvo_ref, so_ref if has_bias else None, ko_acc, vo_acc),
            (1, kvt_ref, st_ref if has_bias else None, kt_acc, vt_acc),
        ):
            scores = part_scores(
                kv_ref[0, :, :lanes], queries, s_ref, col, part, core, key_len, causal
            )
            probs = jnp.exp(scores - lse)
            v_acc[...] += dot(probs.astype(bf16), ups, 1, 0)
            dprobs = dot(kv_ref[0, :, lanes:], ups, 1, 1).astype(bf16).astype(f32)
            delta = delta + jnp.sum(probs * dprobs, axis=0, keepdims=True)
            sides.append((probs, dprobs))
        dq = jnp.zeros((lanes, step), f32)
        for (probs, dprobs), kv_ref, g_ref, k_acc in (
            (sides[0], kvo_ref, go_ref if has_bias else None, ko_acc),
            (sides[1], kvt_ref, gt_ref if has_bias else None, kt_acc),
        ):
            ds = (probs * (dprobs - delta)).astype(bf16)
            k_acc[...] += dot(ds, queries, 1, 0)
            dq = dq + dot(kv_ref[0, :, :lanes], ds, 0, 0)
            if has_bias:
                wide_ds = ds.astype(f32)
                blocks = k_rows // 128
                for j in range(blocks):
                    at = (blocks - 1 - j) * 128 + col
                    g_ref[:, at : at + step] += wide_ds[j * 128 : (j + 1) * 128]
        dq_acc[col : col + step, :] = jnp.where(
            lane_mask, dq.T, dq_acc[col : col + step, :]
        )
    if has_bias:
        drel_ref[0, 0, 0] = fold(go_ref[...])
        drel_ref[0, 0, 1] = fold(gt_ref[...])

    @pl.when(head == pl.num_programs(1) - 1)
    def write():
        dq_ref[0] = dq_acc[...].astype(bf16)
        dkvo_ref[0] = jnp.concatenate([ko_acc[...], vo_acc[...]], axis=1)
        dkvt_ref[0] = jnp.concatenate([kt_acc[...], vt_acc[...]], axis=1).astype(bf16)


def attend_back(scal, q, kvo, kvt, up, lse, rel_rows, centre, causal):
    groups, q_rows, lanes = q.shape
    k_rows = kvo.shape[1]
    heads = lanes // DH
    has_bias = rel_rows is not None
    width = q_rows + (k_rows // 128 - 1) * 128
    gwidth = width + 128
    per_group = lambda i, j: (i, 0, 0)
    in_specs = [
        pl.BlockSpec(memory_space=pltpu.SMEM),
        pl.BlockSpec((1, q_rows, lanes), per_group),
        pl.BlockSpec((1, k_rows, 2 * lanes), per_group),
        pl.BlockSpec((1, k_rows, 2 * lanes), turned),
        pl.BlockSpec((1, q_rows, lanes), per_group),
        pl.BlockSpec((1, 1, 1, q_rows), lambda i, j: (i, j, 0, 0)),
    ]
    args = [scal, q, kvo, kvt, up, lse]
    out_specs = [
        pl.BlockSpec((1, q_rows, lanes), per_group),
        pl.BlockSpec((1, k_rows, 2 * lanes), per_group),
        pl.BlockSpec((1, k_rows, 2 * lanes), turned),
    ]
    out_shape = [
        jax.ShapeDtypeStruct((groups, q_rows, lanes), bf16),
        jax.ShapeDtypeStruct((groups, k_rows, 2 * lanes), f32),
        jax.ShapeDtypeStruct((groups, k_rows, 2 * lanes), bf16),
    ]
    scratch = []
    if has_bias:
        in_specs.append(pl.BlockSpec((1, 1, rel_rows.shape[2]), lambda i, j: (i * heads + j, 0, 0)))
        args.append(rel_rows)
        out_specs.append(pl.BlockSpec((1, 1, 2, 8, gwidth), lambda i, j: (i, j, 0, 0, 0)))
        out_shape.append(jax.ShapeDtypeStruct((groups, heads, 2, 8, gwidth), f32))
        scratch = [pltpu.VMEM((128, width), f32)] * 2 + [pltpu.VMEM((128, gwidth), f32)] * 2
    scratch = scratch + [pltpu.VMEM((q_rows, lanes), f32)] + [pltpu.VMEM((k_rows, lanes), f32)] * 4
    return pl.pallas_call(
        functools.partial(backward_kernel, has_bias, causal, centre),
        grid=(groups, heads),
        in_specs=in_specs,
        out_specs=out_specs,
        out_shape=out_shape,
        scratch_shapes=scratch,
        compiler_params=pltpu.CompilerParams(vmem_limit_bytes=40 * 2**20),
    )(*args)


def rel_grad_rows(drel, core, k_rows, centre, length):
    groups, heads, parts, eight, gwidth = drel.shape
    drel = drel.reshape(groups * heads, parts, eight, gwidth)
    line = sum(jnp.roll(drel[:, :, r, :], -r, axis=-1) for r in range(eight))
    line = jnp.roll(line, 127, axis=-1)
    own, other = bases_of(0, k_rows, core, centre)
    total = jnp.zeros((line.shape[0], length + gwidth + 128), f32)
    for part, base in ((0, own), (1, other)):
        old = lax.dynamic_slice_in_dim(total, base + 1, gwidth, 1)
        total = lax.dynamic_update_slice_in_dim(total, old + line[:, part], base + 1, 1)
    return total[:, 128 : 128 + length]


def rms_forward(inputs, gain_row):
    inverse = lax.rsqrt(jnp.mean(inputs * inputs, axis=-1, keepdims=True) + epsilon)
    return ((inputs * inverse * gain_row).astype(bf16), inverse)


def rms_backward(inputs, gain_row, inverse, upstream):
    upstream = upstream.astype(bf16).astype(f32)
    gain_grad = jnp.sum(upstream * inputs * inverse, axis=0)
    inner = jnp.sum(upstream * gain_row * inputs, axis=-1, keepdims=True)
    result = inverse * gain_row * upstream - inputs * (inverse**3 * inner / inputs.shape[-1])
    return (result, gain_grad)


def project(rows, weights):
    return jnp.einsum("rk,nkc->nrc", rows, weights, preferred_element_type=f32)


def project_back(grads, weights):
    return jnp.einsum("nrc,nkc->rk", grads, weights, preferred_element_type=f32)


def outer(rows, grads):
    return jnp.einsum("rk,nrc->nkc", rows, grads, preferred_element_type=f32)


MESH = pl.DeviceIdType.MESH


def greet(peers):
    barrier = pltpu.get_barrier_semaphore()
    for peer in peers:
        pl.semaphore_signal(barrier, inc=1, device_id=peer, device_id_type=MESH)
    pl.semaphore_wait(barrier, len(peers))


def remote(src, dst, send_sem, recv_sem, peer):
    return pltpu.make_async_remote_copy(
        src_ref=src, dst_ref=dst, send_sem=send_sem, recv_sem=recv_sem,
        device_id=peer, device_id_type=MESH,
    )


def start_kernel(
    units, vocab, ids_ref, table_ref, shard_ref, full_ref, mine_ref,
    ids_all, ids_col, looked, from_x, from_z1, from_z2, total,
    own_sem, w_send, w_recv, id_send, id_recv, e_send, e_recv,
):
    wide, narrow = lax.axis_index("wide"), lax.axis_index("narrow")
    flip = lambda bit: wide + bit - 2 * bit * (wide // bit % 2)
    z2, z1, x = wide // 4, wide // 2 % 2, wide % 2
    at_x, at_z1, at_z2 = (flip(1), narrow), (flip(2), narrow), (flip(4), narrow)
    at_core = (wide, narrow + 1 - 2 * (narrow % 2))
    at_y = (wide, narrow + 2 - 4 * (narrow // 2))
    others = []
    for r in range(1, 8):
        there = wide
        for bit in (1, 2, 4):
            if r & bit:
                there = there + bit - 2 * bit * (wide // bit % 2)
        others.append((there, narrow))
    greet(others + [at_core, at_y])

    def own(j):
        return pltpu.make_async_copy(shard_ref.at[j], full_ref.at[j, 0, z2, z1, x], own_sem.at[j])

    def copy(j, stage):
        if stage == 0:
            src, dst, peer = shard_ref.at[j], full_ref.at[j, 0, z2, z1, x], at_z2
        elif stage == 1:
            src = dst = full_ref.at[j, 0, :, z1, x]
            peer = at_z1
        elif stage == 2:
            src = dst = full_ref.at[j, 0, :, :, x]
            peer = at_x
        elif stage == 3:
            src, dst, peer = full_ref.at[j, 0], full_ref.at[j, 2], at_y
        elif stage == 4:
            src, dst, peer = full_ref.at[j, 0], full_ref.at[j, 1], at_core
        else:
            src, dst, peer = full_ref.at[j, 2], full_ref.at[j, 3], at_core
        return remote(src, dst, w_send.at[j, stage], w_recv.at[j, stage], peer)

    def advance(j, stage):
        if stage == 1:
            own(j).wait()
        if stage > 0:
            copy(j, {5: 3}.get(stage, stage - 1)).wait_recv()
        copy(j, stage).start()
        if stage == 3:
            copy(j, 4).start()

    def ids_copy(r):
        return remote(
            ids_all.at[0], ids_all.at[r], id_send.at[r], id_recv.at[r], others[r - 1]
        )

    ids_all[0] = ids_ref[...]
    for r in range(1, 8):
        ids_copy(r).start()
    for j in range(units):
        own(j).start()
    for j in range(min(3, units)):
        advance(j, 0)

    rows = ids_ref.shape[1]
    cut = total.shape[0]

    def look_up(r):
        if r > 0:
            ids_copy(r).wait_recv()
        ids = ids_all[r] - wide * vocab
        for t in range(rows // 128):
            ids_col[t * 128 : (t + 1) * 128] = jnp.broadcast_to(
                ids[:, t * 128 : (t + 1) * 128], (128, 128)
            ).T
        total[...] = jnp.zeros_like(total)

        def add(k, unused):
            lane = lax.broadcasted_iota(jnp.int32, (rows, 128), 1) + k * 512
            col = ids_col[...]
            hot = jnp.concatenate(
                [(col == lane + q * 128).astype(f32) for q in range(4)], axis=1
            ).astype(bf16)
            block = table_ref[pl.ds(pl.multiple_of(k * 512, 512), 512), :]
            total[...] += dot(hot, block, 1, 0)
            return unused

        lax.fori_loop(0, table_ref.shape[0] // 512, add, 0)
        looked[r] = total[...].astype(bf16)

    def e_copy(hop_at, index):
        if hop_at == 0:
            src, dst, peer = looked.at[2 * index + 1], from_x.at[index], at_x
        elif hop_at == 1:
            src, dst, peer = looked.at[4 * index + 2], from_z1.at[index], at_z1
        else:
            src, dst, peer = looked.at[4], from_z2.at[0], at_z2
        slot = (0, 4, 6)[hop_at] + index
        return remote(src, dst, e_send.at[slot], e_recv.at[slot], peer)

    order = (3, 1, 2, 0)
    todo = []
    for j in range(units):
        todo += [(5 * j + 6 * s + s * s, j, s) for s in (1, 2, 3, 5)]
        if j >= 3:
            todo.append((5 * j, j, 0))
    todo = [(j, s) for unused, j, s in sorted(todo)]
    steps = []
    for s in order:
        steps.append(("odd", s))
    for s in order:
        steps.append(("even", s))
    for s in order:
        steps.append(("merge", s))
    share = -(-len(todo) // (len(steps) + 4))
    for kind, s in steps:
        if kind == "odd":
            look_up(2 * s + 1)
            e_copy(0, s).start()
        elif kind == "even":
            look_up(2 * s)
        else:
            e_copy(0, s).wait_recv()
            looked[2 * s] = looked[2 * s] + from_x[s]
            if s % 2 == 1:
                e_copy(1, s // 2).start()
            else:
                e_copy(1, s // 2).wait_recv()
                looked[2 * s] = looked[2 * s] + from_z1[s // 2]
                if s == 2:
                    e_copy(2, 0).start()
        for j, stage in todo[:share]:
            advance(j, stage)
        todo = todo[share:]
    for j, stage in todo:
        advance(j, stage)
    e_copy(2, 0).wait_recv()
    mine_ref[...] = looked[0] + from_z2[0]
    for j in range(units):
        for stage in range(6):
            copy(j, stage).wait_send()
        for stage in (4, 5):
            copy(j, stage).wait_recv()
    for r in range(1, 8):
        ids_copy(r).wait_send()
    for hop_at, count in ((0, 4), (1, 2), (2, 1)):
        for index in range(count):
            e_copy(hop_at, index).wait_send()


def start_phase(ids, table_low, shards):
    units, slim, columns = shards.shape
    rows, (vocab, width) = ids.shape[1], table_low.shape
    padded = -(-vocab // 512) * 512
    table_low = jnp.pad(table_low, ((0, padded - vocab), (0, 0)))
    any_space = pl.BlockSpec(memory_space=pl.ANY)
    vmem = pl.BlockSpec(memory_space=pltpu.VMEM)
    dma = pltpu.SemaphoreType.DMA
    full, mine = pl.pallas_call(
        functools.partial(start_kernel, units, vocab),
        in_specs=[vmem, vmem, any_space],
        out_specs=[any_space, vmem],
        out_shape=[
            jax.ShapeDtypeStruct((units, 4, 2, 2, 2, slim, columns), bf16),
            jax.ShapeDtypeStruct((rows, width), bf16),
        ],
        scratch_shapes=[
            pltpu.VMEM((8, 1, rows), jnp.int32),
            pltpu.VMEM((rows, 128), jnp.int32),
            pltpu.VMEM((8, rows, width), bf16),
            pltpu.VMEM((4, rows, width), bf16),
            pltpu.VMEM((2, rows, width), bf16),
            pltpu.VMEM((1, rows, width), bf16),
            pltpu.VMEM((rows, width), f32),
            dma((units,)),
            dma((units, 6)),
            dma((units, 6)),
            dma((8,)),
            dma((8,)),
            dma((7,)),
            dma((7,)),
        ],
        compiler_params=pltpu.CompilerParams(
            collective_id=0, has_side_effects=True, vmem_limit_bytes=52 * 2**20
        ),
        cost_estimate=pl.CostEstimate(
            flops=2 * 8 * rows * padded * width, bytes_accessed=2 * 4 * 8 * units * slim * columns,
            transcendentals=0,
        ),
    )(ids, table_low, shards)
    return full.reshape(units, 4, 8 * slim, columns), mine


def end_kernel(kinds, *refs):
    units = len(kinds)
    lefts = sorted({left for kind in kinds for left, unused in kind})
    rights = sorted({right for kind in kinds for unused, right in kind})
    count = len(lefts) + len(rights)
    inputs = refs[:count]
    left_refs = {name: inputs[i] for i, name in enumerate(lefts)}
    right_refs = {name: inputs[len(lefts) + i] for i, name in enumerate(rights)}
    ids_ref, rows_ref, head_ref, small_ref = refs[count : count + 4]
    out_ref, table_out, small_out, square_out, c_in, y_in = refs[count + 4 : count + 10]
    (
        left_vm, right_a, right_b, right_c, right_d, left_t, send_c, stage, held, x_in, z1_in, z2_in,
        gathered, table_vm, table_c, table_y, small_all, small_next, square_all, square_next,
        load_sem, stage_sem, w_send, w_recv, l_send, l_recv, t_send, t_recv, s_send, s_recv, own_sem,
    ) = refs[count + 10 :]
    wide, narrow = lax.axis_index("wide"), lax.axis_index("narrow")
    z2, z1, x = wide // 4, wide // 2 % 2, wide % 2
    y, core = narrow // 2, narrow % 2

    def flipped(index, bits, r):
        for bit in bits:
            if r & bit:
                index = index + bit - 2 * bit * (index // bit % 2)
        return index

    wide_peer = lambda r: (flipped(wide, (1, 2, 4), r), narrow)
    narrow_peer = lambda g: (wide, flipped(narrow, (1, 2), g))
    greet([wide_peer(r) for r in range(1, 8)] + [narrow_peer(g) for g in range(1, 4)])

    slim, columns = out_ref.shape[1:]
    width = 8 * slim

    def small_copy(base, src, dst, index, peer):
        return remote(src, dst, s_send.at[base + index], s_recv.at[base + index], peer)

    def spread(base, value_ref, all_ref):
        all_ref[0] = value_ref[...]
        for r in range(1, 8):
            small_copy(base, all_ref.at[0], all_ref.at[r], r, wide_peer(r)).start()

    def spread_next(base, all_ref, next_ref):
        for r in range(1, 8):
            small_copy(base, all_ref.at[0], all_ref.at[r], r, wide_peer(r)).wait()
        next_ref[0] = jnp.sum(all_ref[...], axis=0)
        for g in range(1, 4):
            small_copy(base + 7, next_ref.at[0], next_ref.at[g], g, narrow_peer(g)).start()

    def collect(base, next_ref, result_ref):
        for g in range(1, 4):
            small_copy(base + 7, next_ref.at[0], next_ref.at[g], g, narrow_peer(g)).wait()
        result_ref[...] = jnp.sum(next_ref[...], axis=0)

    def row_copy(r):
        bit = 1 if r % 2 else (2 if r % 4 else 4)
        return remote(gathered.at[r - bit], gathered.at[r], l_send.at[r], l_recv.at[r], wide_peer(bit))

    right_space = {}

    def loads(j):
        copies = []
        for at, (left, right) in enumerate(kinds[j]):
            src = left_refs[left]
            copies.append((src, left_vm.at[at, : src.shape[0]]))
            src = right_refs[right]
            cols = src.shape[2]
            if cols == columns:
                space = right_d
            else:
                space = (right_a, right_b, right_c)[at]
            copies.append((src, space.at[:, : src.shape[1]]))
        return [
            pltpu.make_async_copy(src, dst, load_sem.at[i]) for i, (src, dst) in enumerate(copies)
        ]

    def product(j, group):
        parts = []
        for at, (left, right) in enumerate(kinds[j]):
            rows = left_refs[left].shape[0]
            cols = right_refs[right].shape[2]
            space = right_d if cols == columns else (right_a, right_b, right_c)[at]
            parts.append(dot(left_t[at, :, :rows], space[group, :rows, :], 1, 0).astype(bf16))
        whole = parts[0] if len(parts) == 1 else jnp.concatenate(parts, axis=1)
        return whole

    def w_copy(j, hop_at):
        slot = j % 3
        if hop_at == 0:
            src, dst, peer = send_c, c_in.at[j], narrow_peer(1)
        elif hop_at == 1:
            src, dst, peer = held.at[slot, 1], y_in.at[j], narrow_peer(2)
        elif hop_at == 2:
            src, dst, peer = held.at[slot, 0, :, :, 1 - x], x_in.at[j], wide_peer(1)
        elif hop_at == 3:
            src, dst, peer = x_in.at[j, :, 1 - z1], z1_in.at[j], wide_peer(2)
        else:
            src, dst, peer = z1_in.at[j, 1 - z2], z2_in.at[j], wide_peer(4)
        return remote(src, dst, w_send.at[j, hop_at], w_recv.at[j, hop_at], peer)

    def multiply(j):
        for copy in loads(j):
            copy.wait()
        for at, (left, unused) in enumerate(kinds[j]):
            rows = left_refs[left].shape[0]
            left_t[at, :, :rows] = left_vm[at, :rows, :].T
        if j > 0:
            w_copy(j - 1, 0).wait_send()
        for side in range(2):
            send_c[side] = product(j, 2 * side + 1).reshape(send_c.shape[1:])
        w_copy(j, 0).start()
        for side in range(2):
            held[j % 3, side] = product(j, 2 * side).reshape(held.shape[2:])
        if j + 1 < units:
            for copy in loads(j + 1):
                copy.start()

    def added(a, b):
        return (a.astype(f32) + b.astype(f32)).astype(bf16)

    def after_core(j):
        w_copy(j, 0).wait_recv()
        copy = pltpu.make_async_copy(c_in.at[j], stage, stage_sem.at[0])
        copy.start()
        copy.wait()
        for side in (1, 0):
            held[j % 3, side] = added(held[j % 3, side], stage[side])
            if side == 1:
                w_copy(j, 1).start()

    def after_y(j):
        w_copy(j, 1).wait()
        copy = pltpu.make_async_copy(y_in.at[j], stage.at[0], stage_sem.at[0])
        copy.start()
        copy.wait()
        held[j % 3, 0] = added(held[j % 3, 0], stage[0])
        w_copy(j, 2).start()

    def after_x(j):
        w_copy(j, 2).wait()
        x_in[j] = added(x_in[j], held[j % 3, 0, :, :, x])
        w_copy(j, 3).start()

    def after_z1(j):
        w_copy(j, 3).wait()
        z1_in[j] = added(z1_in[j], x_in[j, :, z1])
        w_copy(j, 4).start()

    def after_z2(j):
        w_copy(j, 4).wait()
        total = z2_in[j].astype(f32) + z1_in[j, z2].astype(f32)
        out_ref[j] = total
        note(total)

    def note(values):
        rows = values.shape[0]
        squares = jnp.sum((values * values).reshape(rows // 8, 8, values.shape[1]), axis=0)
        for at in range(0, values.shape[1], 128):
            square_all[0] += squares[:, at : at + 128]

    quarter = table_vm.shape[1]
    tokens = gathered.shape[1]
    step = 512

    def scatter_rows():
        def chunk(k, unused):
            per = quarter // step
            at = pl.ds(pl.multiple_of(k % per * step, step), step)
            slot = lax.broadcasted_iota(jnp.int32, (step, 1), 0) + k * step

            def one(r, total):
                hot = (slot == ids_ref[r]).astype(f32).astype(bf16)
                return total + dot(hot, gathered[r], 1, 0)

            total = lax.fori_loop(0, 8, one, table_vm[k // per, at, :].astype(f32))
            table_vm[k // per, at, :] = total.astype(bf16)
            return unused

        lax.fori_loop(0, 4 * quarter // step, chunk, 0)

    def t_copy(at):
        if at == 0:
            src, dst, peer = table_vm.at[1 - core], table_c.at[0], narrow_peer(1)
        elif at == 1:
            src, dst, peer = table_vm.at[3 - core], table_c.at[1], narrow_peer(1)
        elif at == 2:
            src, dst, peer = table_vm.at[2 * (1 - y) + core], table_y, narrow_peer(2)
        elif at == 3:
            src, dst, peer = table_vm.at[narrow], table_out.at[narrow], narrow_peer(2)
        elif at == 4:
            src, dst, peer = table_vm.at[narrow], table_out.at[narrow], narrow_peer(1)
        else:
            there = 2 * (1 - y) + core
            src, dst, peer = table_out.at[there], table_out.at[there], narrow_peer(1)
        return remote(src, dst, t_send.at[at], t_recv.at[at], peer)

    def own_quarter():
        return pltpu.make_async_copy(table_vm.at[narrow], table_out.at[narrow], own_sem.at[0])

    def head_load():
        return pltpu.make_async_copy(head_ref, table_vm, own_sem.at[1])

    def rows_load():
        return pltpu.make_async_copy(rows_ref, gathered.at[0], own_sem.at[2])

    rows_load().start()
    head_load().start()
    for copy in loads(0):
        copy.start()
    square_all[0] = jnp.zeros_like(square_all[0])
    spread(0, small_ref, small_all)
    rows_load().wait()
    for r in (1, 4, 2):
        row_copy(r).start()

    def extra(t):
        if t == 0:
            spread_next(0, small_all, small_next)
        elif t == 1:
            collect(0, small_next, small_out)
            row_copy(2).wait_recv()
            row_copy(3).start()
            row_copy(4).wait_recv()
            row_copy(6).start()
            row_copy(5).start()
        elif t == 2:
            row_copy(6).wait_recv()
            row_copy(7).start()
            head_load().wait()
        elif t == 4:
            for r in (1, 3, 5, 7):
                row_copy(r).wait_recv()
            scatter_rows()
            t_copy(0).start()
            t_copy(1).start()
        elif t == 5:
            for side in range(2):
                t_copy(side).wait_recv()
            there = 2 * (1 - y) + core
            table_vm[there] = added(table_vm[there], table_c[1 - y])
            t_copy(2).start()
            table_vm[narrow] = added(table_vm[narrow], table_c[y])
        elif t == 7:
            t_copy(2).wait()
            part = added(table_vm[narrow], table_y[...])
            table_vm[narrow] = part
            t_copy(3).start()
            t_copy(4).start()
            own_quarter().start()
            note(part.astype(f32))

    for t in range(units + 4):
        if t < units:
            multiply(t)
            after_core(t)
        extra(t)
        for lag, act in ((1, after_y), (2, after_x), (3, after_z1), (4, after_z2)):
            if 0 <= t - lag < units:
                act(t - lag)
    for r in range(1, 8):
        small_copy(16, square_all.at[0], square_all.at[r], r, wide_peer(r)).start()
    spread_next(16, square_all, square_next)
    t_copy(3).wait_recv()
    t_copy(5).start()
    collect(16, square_next, square_out)
    t_copy(4).wait_recv()
    t_copy(5).wait_recv()
    for at in (0, 1, 3, 4, 5):
        t_copy(at).wait_send()
    own_quarter().wait()
    w_copy(units - 1, 0).wait_send()
    for r in range(1, 8):
        row_copy(r).wait_send()


def end_phase(kinds, lefts, rights, ids, rows, head, small):
    units = len(kinds)
    names = sorted({left for kind in kinds for left, unused in kind})
    right_names = sorted({right for kind in kinds for unused, right in kind})
    tokens, width = rows.shape
    slim = width // 8
    quarter = head.shape[1]
    most = max(value.shape[0] for value in lefts.values())
    any_space = pl.BlockSpec(memory_space=pl.ANY)
    vmem = pl.BlockSpec(memory_space=pltpu.VMEM)
    dma = pltpu.SemaphoreType.DMA
    narrow_cols = [rights[right].shape[2] for unused, right in max(kinds, key=len)]
    args = [lefts[name] for name in names] + [rights[name] for name in right_names]
    outs = pl.pallas_call(
        functools.partial(end_kernel, kinds),
        in_specs=[any_space] * len(args) + [vmem, any_space, any_space, vmem],
        out_specs=[vmem, any_space, vmem, vmem, any_space, any_space],
        out_shape=[
            jax.ShapeDtypeStruct((units, slim, width), f32),
            jax.ShapeDtypeStruct((4, quarter, width), bf16),
            jax.ShapeDtypeStruct(small.shape, f32),
            jax.ShapeDtypeStruct((8, 128), f32),
            jax.ShapeDtypeStruct((units, 2, 2, 2, 2, slim, width), bf16),
            jax.ShapeDtypeStruct((units, 2, 2, 2, slim, width), bf16),
        ],
        scratch_shapes=[
            pltpu.VMEM((3, most, width), bf16),
            pltpu.VMEM((4, most, narrow_cols[0]), bf16),
            pltpu.VMEM((4, most, narrow_cols[1]), bf16),
            pltpu.VMEM((4, most, narrow_cols[2]), bf16),
            pltpu.VMEM((4, most, width), bf16),
            pltpu.VMEM((3, width, most), bf16),
            pltpu.VMEM((2, 2, 2, 2, slim, width), bf16),
            pltpu.VMEM((2, 2, 2, 2, slim, width), bf16),
            pltpu.VMEM((3, 2, 2, 2, 2, slim, width), bf16),
            pltpu.VMEM((units, 2, 2, slim, width), bf16),
            pltpu.VMEM((units, 2, slim, width), bf16),
            pltpu.VMEM((units, slim, width), bf16),
            pltpu.VMEM((8, tokens, width), bf16),
            pltpu.VMEM((4, quarter, width), bf16),
            pltpu.VMEM((2, quarter, width), bf16),
            pltpu.VMEM((quarter, width), bf16),
            pltpu.VMEM((8, *small.shape), f32),
            pltpu.VMEM((4, *small.shape), f32),
            pltpu.VMEM((8, 8, 128), f32),
            pltpu.VMEM((4, 8, 128), f32),
            dma((6,)),
            dma((1,)),
            dma((units, 5)),
            dma((units, 5)),
            dma((8,)),
            dma((8,)),
            dma((6,)),
            dma((6,)),
            dma((32,)),
            dma((32,)),
            dma((3,)),
        ],
        compiler_params=pltpu.CompilerParams(
            collective_id=1, has_side_effects=True, vmem_limit_bytes=62 * 2**20
        ),
        cost_estimate=pl.CostEstimate(
            flops=2 * 8 * tokens * 4 * quarter * width, bytes_accessed=100 * 2**20, transcendentals=0
        ),
    )(*args, ids, rows, head, small)
    return outs[:4]


def body(
    enc_ids, enc_len, tgt_ids, tgt_len, span_mask, buckets,
    attn_in, attn_out, ff_in, ff_out, table, gains, rel,
    mom_attn_in, mom_attn_out, mom_ff_in, mom_ff_out, mom_table, mom_gains, mom_rel,
    avg_attn_in, avg_attn_out, avg_ff_in, avg_ff_out, avg_table, avg_gains, avg_rel,
):
    wide_size = lax.axis_size("wide")
    narrow_size = lax.axis_size("narrow")
    wide_index = lax.axis_index("wide")
    narrow_index = lax.axis_index("narrow")
    micro = narrow_index // 2
    core = narrow_index % 2
    width = table.shape[1]
    vocab = table.shape[0]
    enc_rows = enc_ids.shape[2] // 2
    dec_rows = tgt_ids.shape[2] // 2
    centre = (buckets.shape[0] + 1) // 2 - 1
    lanes = attn_out.shape[1]
    heads_here = lanes // DH
    slim = attn_in.shape[1]

    shards = []
    for layer in range(3):
        packed = attn_in[layer].reshape(slim, heads_here, 3, DH).transpose(0, 2, 1, 3)
        shards.append(jnp.concatenate([packed.reshape(slim, -1), attn_out[layer].T], axis=1))
    for layer in range(2):
        shards.append(ff_in[layer])
        shards.append(ff_out[layer].T)
    shards = jnp.stack(shards).astype(bf16)
    groups = narrow_index ^ jnp.arange(narrow_size)
    small = jnp.concatenate([gains.reshape(-1), rel.reshape(-1)])
    small = lax.all_gather(small, "narrow", axis=0, tiled=False)
    cut = gains.size
    gains_full = small[:, :cut].reshape(narrow_size, *gains.shape).transpose(1, 0, 2)
    gains_full = gains_full.reshape(gains.shape[0], -1)
    rel_full = small[:, cut:].reshape(narrow_size, *rel.shape).transpose(1, 2, 0, 3)
    rel_full = rel_full.reshape(rel.shape[0], rel.shape[1], -1)
    onehot_rev = (buckets[::-1][:, None] == jnp.arange(rel.shape[1])[None, :]).astype(f32)
    onehot_rev = jnp.pad(onehot_rev, ((0, 1), (0, 0)))
    rel_rows = [
        jnp.dot(onehot_rev, rel_full[i], precision=highest)
        .T.reshape(narrow_size, heads_here, 1, -1)[groups]
        .reshape(narrow_size * heads_here, 1, -1)
        for i in range(2)
    ]

    my_enc = lax.dynamic_slice(enc_ids, (micro, 0, core * enc_rows), (1, 1, enc_rows))
    others = wide_index ^ jnp.arange(wide_size)
    targets_micro = lax.dynamic_index_in_dim(tgt_ids, micro, 0, keepdims=False)[others]
    shifted = jnp.concatenate(
        [jnp.zeros((wide_size, 1), jnp.int32), targets_micro[:, :-1]], axis=1
    )
    dec_all = lax.dynamic_slice_in_dim(shifted, core * dec_rows, dec_rows, 1)
    table_low = table.astype(bf16)
    enc_all = gather_direct(my_enc.reshape(enc_rows), "wide")
    tokens = jnp.concatenate([enc_all, dec_all], axis=1)
    local = tokens - wide_index * vocab
    held = (local >= 0) & (local < vocab)
    local = jnp.where(held, local, 0)
    if wide_size == 8 and narrow_size == 4:
        my_ids = jnp.concatenate([my_enc.reshape(enc_rows), dec_all[0]])[None]
        gathered, mine = start_phase(my_ids, table_low, shards)
    else:
        gathered = []
        for shard in shards:
            column = gather_sorted(shard, "wide").reshape(width, -1)
            pair = jnp.stack([column, hop(column, "narrow", 2)])
            pair = jnp.stack([pair, swap(pair)], axis=1)
            gathered.append(pair.reshape(narrow_size, width, -1))
        rows = table_low[local.reshape(-1)]
        rows = jnp.where(held.reshape(-1)[:, None], rows, 0).astype(bf16)
        mine = scatter_relative(rows.reshape(*local.shape, width), "wide", bf16)
    low_in = [gathered[i][:, :, : 3 * lanes] for i in range(3)]
    low_out = [gathered[i][:, :, 3 * lanes :] for i in range(3)]
    low_up = [gathered[3], gathered[5]]
    low_down = [gathered[4], gathered[6]]

    enc0 = mine[:enc_rows].astype(f32)
    dec0 = mine[enc_rows:].astype(f32)

    key_len = lax.dynamic_slice(enc_len, (micro, 0), (1, 1)).reshape(())
    scal = jnp.stack([core, key_len]).astype(jnp.int32)

    def attn_forward(state, gain_row, layer, source, rel_row, causal):
        normed, inverse = rms_forward(state, gain_row)
        kv = project(normed if source is None else source, low_in[layer][:, :, lanes:]).astype(bf16)
        kv_other = swap(kv)
        q = project(normed, low_in[layer][:, :, :lanes]).astype(bf16)
        mixed, lse = attend(scal, q, kv, kv_other, rel_row, centre, causal)
        update = project_back(mixed, low_out[layer])
        return (state + update, (state, inverse, normed, q, kv, kv_other, mixed, lse))

    def attn_backward(saved, upstream, gain_row, layer, source, rel_row, causal):
        state, inverse, normed, q, kv, kv_other, mixed, lse = saved
        up = upstream.astype(bf16)
        mixed_grad = project(up, low_out[layer]).astype(bf16)
        outs = attend_back(scal, q, kv, kv_other, mixed_grad, lse, rel_row, centre, causal)
        dq, dkv_own, dkv_other = outs[:3]
        dkv = (dkv_own + swap(dkv_other).astype(f32)).astype(bf16)
        normed_grad = project_back(dq, low_in[layer][:, :, :lanes])
        kv_back = project_back(dkv, low_in[layer][:, :, lanes:])
        if source is None:
            normed_grad = normed_grad + kv_back
        state_grad, gain_grad = rms_backward(state, gain_row, inverse, normed_grad)
        pieces = ((normed, dq), (normed if source is None else source, dkv), (up, mixed))
        return (upstream + state_grad, gain_grad, pieces, kv_back, outs[3] if rel_row is not None else None)

    def ff_forward(state, gain_row, layer):
        normed, inverse = rms_forward(state, gain_row)
        pre = project(normed, low_up[layer])
        hidden = jax.nn.gelu(pre).astype(bf16)
        return (state + project_back(hidden, low_down[layer]), (state, inverse, normed, pre, hidden))

    def ff_backward(saved, upstream, gain_row, layer):
        state, inverse, normed, pre, hidden = saved
        up = upstream.astype(bf16)
        hidden_grad = project(up, low_down[layer]).astype(bf16).astype(f32)
        unused, gelu_back = jax.vjp(jax.nn.gelu, pre)
        pre_grad = gelu_back(hidden_grad)[0].astype(bf16)
        normed_grad = project_back(pre_grad, low_up[layer])
        state_grad, gain_grad = rms_backward(state, gain_row, inverse, normed_grad)
        return (upstream + state_grad, gain_grad, ((normed, pre_grad),), ((up, hidden),))

    def scatter(pieces):
        grad = jnp.concatenate([outer(*piece) for piece in pieces], axis=2).astype(bf16)
        return spread(grad)

    def spread(grad):
        pairs = grad.reshape(2, 2, width, -1)
        across = pairs[:, 0].astype(f32) + swap(pairs[:, 1]).astype(f32)
        column = across[0] + hop(across[1].astype(bf16), "narrow", 2).astype(f32)
        return scatter_sorted(column.astype(bf16).reshape(wide_size, slim, -1), "wide")

    enc1, saved_a = attn_forward(enc0, gains_full[0], 0, None, rel_rows[0], 0)
    enc2, saved_b = ff_forward(enc1, gains_full[1], 0)
    encoded, enc_inverse = rms_forward(enc2, gains_full[2])
    dec1, saved_c = attn_forward(dec0, gains_full[3], 1, None, rel_rows[1], dec_rows)
    dec2, saved_d = attn_forward(dec1, gains_full[4], 2, encoded, None, 0)
    dec3, saved_e = ff_forward(dec2, gains_full[5], 1)
    final_gain = gains_full[6] * width ** (-0.5)
    final, final_inverse = rms_forward(dec3, final_gain)

    row_weight = (jnp.arange(2 * dec_rows)[None, None, :] < tgt_len[:, :, None]).astype(
        f32
    ) * span_mask.astype(f32)
    count = jnp.sum(row_weight)
    weights_micro = lax.dynamic_index_in_dim(row_weight, micro, 0, keepdims=False)[others]
    weights = lax.dynamic_slice_in_dim(weights_micro, core * dec_rows, dec_rows, 1).reshape(-1)
    targets = lax.dynamic_slice_in_dim(targets_micro, core * dec_rows, dec_rows, 1).reshape(-1)
    targets = targets - wide_index * vocab
    final_all = gather_relative(final, "wide").reshape(-1, width)
    logits = dot(final_all, table_low, 1, 1)
    target_hot = jnp.arange(vocab)[None, :] == targets[:, None]
    top = jnp.max(logits, axis=-1)
    total = jnp.sum(jnp.exp(logits - top[:, None]), axis=-1)
    hits = jnp.sum(jnp.where(target_hot, logits, 0.0), axis=-1)
    stats = jnp.stack([top, total, hits]).reshape(3, wide_size, dec_rows)
    if wide_size > 8:
        stats = lax.all_gather(stats[:, others], "wide", axis=0, tiled=False)[:, :, others]
    else:
        stats = jnp.stack(
            [stats]
            + [
                hop(stats, "wide", r)[:, [q ^ r for q in range(wide_size)]]
                for r in range(1, wide_size)
            ]
        )
    stats = stats.reshape(wide_size, 3, -1)
    best = jnp.max(stats[:, 0], axis=0)
    log_total = best + jnp.log(jnp.sum(stats[:, 1] * jnp.exp(stats[:, 0] - best[None]), axis=0))
    loss_rows = weights * (log_total - jnp.sum(stats[:, 2], axis=0))
    loss_part = jnp.sum(loss_rows[:dec_rows])
    logit_grad = (
        (weights / count)[:, None]
        * (jnp.exp(logits - log_total[:, None]) - target_hot.astype(f32))
    ).astype(bf16)
    final_grad = scatter_relative(
        dot(logit_grad, table_low, 1, 0).reshape(wide_size, dec_rows, width), "wide", f32
    )

    gain_grads = [None] * 7
    dec_grad, gain_raw = rms_backward(dec3, final_gain, final_inverse, final_grad)
    gain_grads[6] = gain_raw * width ** (-0.5)
    dec_grad, gain_grads[5], up1, down1 = ff_backward(saved_e, dec_grad, gains_full[5], 1)
    dec_grad, gain_grads[4], attn2, source_grad, unused = attn_backward(
        saved_d, dec_grad, gains_full[4], 2, encoded, None, 0
    )
    dec_grad, gain_grads[3], attn1, unused, drel_dec = attn_backward(
        saved_c, dec_grad, gains_full[3], 1, None, rel_rows[1], dec_rows
    )
    enc_grad, gain_grads[2] = rms_backward(enc2, gains_full[2], enc_inverse, source_grad)
    enc_grad, gain_grads[1], up0, down0 = ff_backward(saved_b, enc_grad, gains_full[1], 0)
    enc_grad, gain_grads[0], attn0, unused, drel_enc = attn_backward(
        saved_a, enc_grad, gains_full[0], 0, None, rel_rows[0], 0
    )
    length = onehot_rev.shape[0]
    rel_grad = jnp.stack(
        [
            jnp.dot(rel_grad_rows(drel_enc, core, enc_rows, centre, length), onehot_rev, precision=highest),
            jnp.dot(rel_grad_rows(drel_dec, core, dec_rows, centre, length), onehot_rev, precision=highest),
        ]
    )
    rel_grad = rel_grad.reshape(2, narrow_size, heads_here, -1)[:, groups]
    rel_grad = rel_grad.reshape(2, narrow_size * heads_here, -1)
    row_grads = jnp.concatenate([enc_grad, dec_grad], axis=0).astype(bf16)
    local = jnp.where(held, local, -1)
    if wide_size == 8 and narrow_size == 4:
        order = (up1, down1, attn2, attn1, up0, down0, attn0)
        kinds, lefts, rights = [], {}, {}
        names = {}
        for unit in order:
            kind = []
            for left, right in unit:
                name = names.setdefault(id(left), "l%02d" % len(names))
                lefts[name] = left
                rights["r%02d" % len(rights)] = right
                kind.append((name, "r%02d" % (len(rights) - 1)))
            kinds.append(tuple(kind))
        quarter = -(-vocab // 2048) * 512
        head_part = dot(logit_grad, final_all, 0, 0).astype(bf16)
        head_part = jnp.pad(head_part, ((0, 4 * quarter - vocab), (0, 0)))
        flat = jnp.concatenate(
            [jnp.stack(gain_grads).reshape(-1), rel_grad.reshape(-1), loss_part[None]]
        )
        small_rows = -(-flat.size // 1024) * 8
        small_in = jnp.pad(flat, (0, small_rows * 128 - flat.size)).reshape(small_rows, 128)
        summed, table_grad, small_sum, square_rows = end_phase(
            tuple(kinds), lefts, rights, local[:, None, :], row_grads,
            head_part.reshape(4, quarter, width), small_in,
        )
        reduced = [summed[i] for i in (6, 3, 2, 4, 5, 0, 1)]
        table_grad = table_grad.reshape(4 * quarter, width)[:vocab].astype(f32)
        small_sum = small_sum.reshape(-1)
        cut = 7 * width
        gain_total = small_sum[:cut].reshape(7, width)
        rel_total = small_sum[cut : cut + rel_grad.size].reshape(rel_grad.shape)
        loss_sum = small_sum[cut + rel_grad.size]
        square_sum = jnp.sum(square_rows)
    else:
        reduced = [scatter(grad) for grad in (attn0, attn1, attn2, up0, down0, up1, down1)]

        padded = -(-vocab // 64) * 64
        slots = jnp.arange(padded)
        local = local.reshape(-1, 2, local.shape[1])
        halves, part_grads = [], []
        half = width // 2
        for start in (0, half):
            rows = row_grads[None, :, start : start + half]
            for bit in list(bits_down("wide"))[:-1]:
                rows = jnp.stack([rows, hop(rows, "wide", bit)], axis=1)
                rows = rows.reshape(-1, *rows.shape[2:])
            far = hop(rows, "wide", 1)
            partial = dot(logit_grad, final_all[:, start : start + half], 0, 0)
            partial = jnp.pad(partial, ((0, padded - vocab), (0, 0)))
            for at, values in ((local[:, 0], rows), (local[:, 1], far)):
                token_hot = (slots[:, None] == at.reshape(-1)[None, :]).astype(bf16)
                partial = partial + dot(token_hot, values.reshape(-1, half), 1, 0)
            quarters = partial.astype(bf16).reshape(narrow_size, padded // narrow_size, half)
            part = scatter_sorted(quarters, "narrow").astype(bf16)
            part_grads.append(part.astype(f32))
            halves.append(gather_sorted(part, "narrow").reshape(padded, half)[:vocab])
        table_grad = jnp.concatenate(halves, axis=1).astype(f32)

        gain_total, rel_total, loss_sum = lax.psum(
            (jnp.stack(gain_grads), rel_grad, loss_part), ("wide", "narrow")
        )
        squares = sum(jnp.sum(grad * grad) for grad in reduced + part_grads)
        square_sum = lax.psum(squares, ("wide", "narrow"))
    square_sum = square_sum + jnp.sum(gain_total * gain_total) + jnp.sum(rel_total * rel_total)
    gain_mine = lax.dynamic_slice_in_dim(gain_total, narrow_index * lanes, lanes, 1)
    rel_mine = lax.dynamic_slice_in_dim(
        rel_total, narrow_index * heads_here, heads_here, 1
    ).transpose(0, 2, 1)

    def unpack_in(grad):
        grad = grad[:, : 3 * lanes].reshape(slim, 3, heads_here, DH).transpose(0, 2, 1, 3)
        return grad.reshape(slim, -1)

    grads = (
        jnp.stack([unpack_in(reduced[i]) for i in range(3)]),
        jnp.stack([reduced[i][:, 3 * lanes :].T for i in range(3)]),
        jnp.stack([reduced[3], reduced[5]]),
        jnp.stack([reduced[4].T, reduced[6].T]),
        table_grad,
        gain_mine,
        rel_mine,
    )
    norm = jnp.sqrt(square_sum)
    scale = jnp.minimum(1.0, clip_norm / norm)
    base_rate = math.sqrt(PARAMS) / (3.0 * clip_norm)
    matrix_rate = base_rate / math.sqrt(width)
    rates = (
        matrix_rate, 16.0 * matrix_rate, matrix_rate, matrix_rate,
        base_rate, 0.3 * base_rate, 0.3 * base_rate,
    )
    params = (attn_in, attn_out, ff_in, ff_out, table, gains, rel)
    moms = (mom_attn_in, mom_attn_out, mom_ff_in, mom_ff_out, mom_table, mom_gains, mom_rel)
    avgs = (avg_attn_in, avg_attn_out, avg_ff_in, avg_ff_out, avg_table, avg_gains, avg_rel)
    fresh, scaled_grads, averages = ([], [], [])
    for index in range(7):
        clipped = grads[index] * scale
        moment = momentum_decay * moms[index] + clipped
        weight = params[index] - rates[index] * (clipped + momentum_decay * moment)
        fresh.append(weight)
        scaled_grads.append(clipped)
        averages.append(average_decay * avgs[index] + (1.0 - average_decay) * weight)
    return (loss_sum, count, norm, *fresh, *scaled_grads, *averages)


def solution(mesh):
    weights = (
        P(None, "wide", "narrow"),
        P(None, "narrow", "wide"),
        P(None, "wide", "narrow"),
        P(None, "narrow", "wide"),
        P("wide", None),
        P(None, "narrow"),
        P(None, None, "narrow"),
    )
    in_specs = (P(None, "wide", None), P(None, "wide"), P(), P(), P(), P()) + weights * 3
    out_specs = (P(), P(), P()) + weights * 3
    return jax.shard_map(body, mesh=mesh, in_specs=in_specs, out_specs=out_specs, check_vma=False)
```

```python
import functools
import math

import jax
import jax.numpy as jnp
from jax import lax
from jax.experimental import pallas as pl
from jax.experimental.pallas import tpu as pltpu
from jax.sharding import PartitionSpec as P

DH = 64
PARAMS = 41195520

epsilon = 1e-06
masked_score = -1000000000.0
momentum_decay = 0.9
average_decay = 0.9
clip_norm = 0.02
highest = lax.Precision.HIGHEST
bf16 = jnp.bfloat16
f32 = jnp.float32
CHUNK = 256


def dot(left, right, left_dim, right_dim):
    return lax.dot_general(
        left, right, (((left_dim,), (right_dim,)), ((), ())), preferred_element_type=f32
    )


def hop(values, axis, bit):
    size = lax.axis_size(axis)
    return lax.ppermute(values, axis, [(i, i ^ bit) for i in range(size)])


def swap(values):
    return hop(values, "narrow", 1)


def bits_down(axis):
    bit = lax.axis_size(axis) // 2
    while bit:
        yield bit
        bit //= 2


def bits_up(axis):
    return reversed(list(bits_down(axis)))


def gather_sorted(values, axis):
    index = lax.axis_index(axis)
    values = values[None]
    for bit in bits_down(axis):
        other = hop(values, axis, bit)
        upper = (index & bit) != 0
        values = jnp.stack(
            [jnp.where(upper, other, values), jnp.where(upper, values, other)], axis=1
        ).reshape(-1, *values.shape[1:])
    return values


def scatter_sorted(values, axis):
    index = lax.axis_index(axis)
    for bit in bits_up(axis):
        pairs = values.reshape(-1, 2, *values.shape[1:])
        mine = jnp.where((index & bit) != 0, 1, 0)
        kept = lax.dynamic_index_in_dim(pairs, mine, 1, keepdims=False)
        sent = lax.dynamic_index_in_dim(pairs, 1 - mine, 1, keepdims=False)
        other = hop(sent.astype(bf16), axis, bit)
        values = kept.astype(f32) + other.astype(f32)
        if values.shape[0] > 1:
            values = values.astype(bf16)
    return values[0]


def scatter_relative(values, axis, dtype):
    for bit in bits_up(axis):
        pairs = values.reshape(-1, 2, *values.shape[1:])
        other = hop(pairs[:, 1].astype(bf16), axis, bit)
        values = pairs[:, 0].astype(dtype) + other.astype(dtype)
    return values[0]


def gather_relative(values, axis):
    values = values[None]
    for bit in bits_down(axis):
        values = jnp.stack([values, hop(values, axis, bit)], axis=1)
        values = values.reshape(-1, *values.shape[2:])
    return values


def gather_direct(values, axis):
    size = lax.axis_size(axis)
    if size > 8:
        return gather_relative(values, axis)
    return jnp.stack([values] + [hop(values, axis, r) for r in range(1, size)])


def bias_strip(rel_row, base, width):
    length = rel_row.shape[1]
    row = pltpu.roll(jnp.broadcast_to(rel_row, (8, length)), length + 128 - base, 1)
    rows = jnp.broadcast_to(row[:1, : width + 128], (128, width + 128))
    return pltpu.roll(rows, 0, 1, stride=1, stride_axis=0)[:, 128:]


def part_scores(keys, queries_h, strip, col, part, core, key_len, causal):
    scores = dot(keys, queries_h, 1, 1)
    rows, cols = scores.shape
    blocks = rows // 128
    if strip is not None:
        shifts = [(blocks - 1 - j) * 128 + col for j in range(blocks)]
        bias = jnp.concatenate([strip[:, s : s + cols] for s in shifts], axis=0)
        scores = scores + bias
    where_core = core if part == 0 else 1 - core
    key_at = where_core * rows + lax.broadcasted_iota(jnp.int32, (rows, 1), 0)
    if causal:
        query_at = lax.broadcasted_iota(jnp.int32, (1, cols), 1) + col + causal * core
        return jnp.where(key_at <= query_at, scores, masked_score)
    return jnp.where(key_at < key_len, scores, masked_score)


def bases_of(size, rows, core, centre):
    own = centre - (rows // 128 - 1) * 128
    other = own - rows + core * (2 * rows)
    return own, other


def forward_kernel(has_bias, causal, centre, scal, q_ref, kvo_ref, kvt_ref, *rest):
    if has_bias:
        rel_ref, mixed_ref, lse_ref, so_ref, st_ref = rest
    else:
        mixed_ref, lse_ref = rest
    core, key_len, head = scal[0], scal[1], pl.program_id(1)
    q_rows, k_rows = q_ref.shape[1], kvo_ref.shape[1]
    lanes = q_ref.shape[2]
    lane_mask = lax.broadcasted_iota(jnp.int32, (1, lanes), 1) // DH == head
    if has_bias:
        own, other = bases_of(lanes, k_rows, core, centre)
        so_ref[...] = bias_strip(rel_ref[0], own, so_ref.shape[1])
        st_ref[...] = bias_strip(rel_ref[0], other, st_ref.shape[1])
    step = min(CHUNK, q_rows)
    for col in range(0, q_rows, step):
        queries = jnp.where(lane_mask, q_ref[0, col : col + step, :], 0.0).astype(bf16)
        own_s = part_scores(
            kvo_ref[0, :, :lanes], queries, so_ref if has_bias else None,
            col, 0, core, key_len, causal,
        )
        oth_s = part_scores(
            kvt_ref[0, :, :lanes], queries, st_ref if has_bias else None,
            col, 1, core, key_len, causal,
        )
        top = jnp.maximum(
            jnp.max(own_s, axis=0, keepdims=True), jnp.max(oth_s, axis=0, keepdims=True)
        )
        own_e, oth_e = jnp.exp(own_s - top), jnp.exp(oth_s - top)
        total = jnp.sum(own_e, axis=0, keepdims=True) + jnp.sum(oth_e, axis=0, keepdims=True)
        inverse = 1.0 / total
        mixed = dot(kvo_ref[0, :, lanes:], (own_e * inverse).astype(bf16), 0, 0)
        mixed = mixed + dot(kvt_ref[0, :, lanes:], (oth_e * inverse).astype(bf16), 0, 0)
        mixed = mixed.T.astype(bf16)
        mixed_ref[0, col : col + step, :] = jnp.where(
            lane_mask, mixed, mixed_ref[0, col : col + step, :]
        )
        lse_ref[0, 0, :, col : col + step] = top + jnp.log(total)


def turned(i, j):
    return (i + 1 - 2 * (i % 2), 0, 0)


def attend(scal, q, kvo, kvt, rel_rows, centre, causal):
    groups, q_rows, lanes = q.shape
    k_rows = kvo.shape[1]
    heads = lanes // DH
    has_bias = rel_rows is not None
    width = q_rows + (k_rows // 128 - 1) * 128
    in_specs = [
        pl.BlockSpec(memory_space=pltpu.SMEM),
        pl.BlockSpec((1, q_rows, lanes), lambda i, j: (i, 0, 0)),
        pl.BlockSpec((1, k_rows, 2 * lanes), lambda i, j: (i, 0, 0)),
        pl.BlockSpec((1, k_rows, 2 * lanes), turned),
    ]
    args = [scal, q, kvo, kvt]
    scratch = []
    if has_bias:
        in_specs.append(pl.BlockSpec((1, 1, rel_rows.shape[2]), lambda i, j: (i * heads + j, 0, 0)))
        args.append(rel_rows)
        scratch = [pltpu.VMEM((128, width), f32)] * 2
    return pl.pallas_call(
        functools.partial(forward_kernel, has_bias, causal, centre),
        grid=(groups, heads),
        in_specs=in_specs,
        out_specs=[
            pl.BlockSpec((1, q_rows, lanes), lambda i, j: (i, 0, 0)),
            pl.BlockSpec((1, 1, 1, q_rows), lambda i, j: (i, j, 0, 0)),
        ],
        out_shape=[
            jax.ShapeDtypeStruct((groups, q_rows, lanes), bf16),
            jax.ShapeDtypeStruct((groups, heads, 1, q_rows), f32),
        ],
        scratch_shapes=scratch,
        compiler_params=pltpu.CompilerParams(vmem_limit_bytes=40 * 2**20),
    )(*args)


def fold(strip):
    rows, width = strip.shape
    while rows > 8:
        rows //= 2
        strip = strip[:rows] + pltpu.roll(strip[rows:], width - rows, 1)
    return strip


def backward_kernel(has_bias, causal, centre, scal, q_ref, kvo_ref, kvt_ref, up_ref, lse_ref, *rest):
    if has_bias:
        rel_ref, dq_ref, dkvo_ref, dkvt_ref, drel_ref, so_ref, st_ref, go_ref, gt_ref = rest[:9]
        dq_acc, ko_acc, vo_acc, kt_acc, vt_acc = rest[9:]
    else:
        dq_ref, dkvo_ref, dkvt_ref, dq_acc, ko_acc, vo_acc, kt_acc, vt_acc = rest
    core, key_len, head = scal[0], scal[1], pl.program_id(1)
    q_rows, k_rows = q_ref.shape[1], kvo_ref.shape[1]
    lanes = q_ref.shape[2]
    lane_mask = lax.broadcasted_iota(jnp.int32, (1, lanes), 1) // DH == head
    if has_bias:
        own, other = bases_of(lanes, k_rows, core, centre)
        so_ref[...] = bias_strip(rel_ref[0], own, so_ref.shape[1])
        st_ref[...] = bias_strip(rel_ref[0], other, st_ref.shape[1])
        go_ref[...] = jnp.zeros_like(go_ref)
        gt_ref[...] = jnp.zeros_like(gt_ref)

    @pl.when(head == 0)
    def clear():
        for acc in (ko_acc, vo_acc, kt_acc, vt_acc):
            acc[...] = jnp.zeros_like(acc)

    step = min(CHUNK, q_rows)
    for col in range(0, q_rows, step):
        queries = jnp.where(lane_mask, q_ref[0, col : col + step, :], 0.0).astype(bf16)
        ups = jnp.where(lane_mask, up_ref[0, col : col + step, :], 0.0).astype(bf16)
        lse = lse_ref[0, 0, :, col : col + step]
        sides = []
        delta = jnp.zeros((1, step), f32)
        for part, kv_ref, s_ref, k_acc, v_acc in (
            (0, kvo_ref, so_ref if has_bias else None, ko_acc, vo_acc),
            (1, kvt_ref, st_ref if has_bias else None, kt_acc, vt_acc),
        ):
            scores = part_scores(
                kv_ref[0, :, :lanes], queries, s_ref, col, part, core, key_len, causal
            )
            probs = jnp.exp(scores - lse)
            v_acc[...] += dot(probs.astype(bf16), ups, 1, 0)
            dprobs = dot(kv_ref[0, :, lanes:], ups, 1, 1).astype(bf16).astype(f32)
            delta = delta + jnp.sum(probs * dprobs, axis=0, keepdims=True)
            sides.append((probs, dprobs))
        dq = jnp.zeros((lanes, step), f32)
        for (probs, dprobs), kv_ref, g_ref, k_acc in (
            (sides[0], kvo_ref, go_ref if has_bias else None, ko_acc),
            (sides[1], kvt_ref, gt_ref if has_bias else None, kt_acc),
        ):
            ds = (probs * (dprobs - delta)).astype(bf16)
            k_acc[...] += dot(ds, queries, 1, 0)
            dq = dq + dot(kv_ref[0, :, :lanes], ds, 0, 0)
            if has_bias:
                wide_ds = ds.astype(f32)
                blocks = k_rows // 128
                for j in range(blocks):
                    at = (blocks - 1 - j) * 128 + col
                    g_ref[:, at : at + step] += wide_ds[j * 128 : (j + 1) * 128]
        dq_acc[col : col + step, :] = jnp.where(
            lane_mask, dq.T, dq_acc[col : col + step, :]
        )
    if has_bias:
        drel_ref[0, 0, 0] = fold(go_ref[...])
        drel_ref[0, 0, 1] = fold(gt_ref[...])

    @pl.when(head == pl.num_programs(1) - 1)
    def write():
        dq_ref[0] = dq_acc[...].astype(bf16)
        dkvo_ref[0] = jnp.concatenate([ko_acc[...], vo_acc[...]], axis=1)
        dkvt_ref[0] = jnp.concatenate([kt_acc[...], vt_acc[...]], axis=1).astype(bf16)


def attend_back(scal, q, kvo, kvt, up, lse, rel_rows, centre, causal):
    groups, q_rows, lanes = q.shape
    k_rows = kvo.shape[1]
    heads = lanes // DH
    has_bias = rel_rows is not None
    width = q_rows + (k_rows // 128 - 1) * 128
    gwidth = width + 128
    per_group = lambda i, j: (i, 0, 0)
    in_specs = [
        pl.BlockSpec(memory_space=pltpu.SMEM),
        pl.BlockSpec((1, q_rows, lanes), per_group),
        pl.BlockSpec((1, k_rows, 2 * lanes), per_group),
        pl.BlockSpec((1, k_rows, 2 * lanes), turned),
        pl.BlockSpec((1, q_rows, lanes), per_group),
        pl.BlockSpec((1, 1, 1, q_rows), lambda i, j: (i, j, 0, 0)),
    ]
    args = [scal, q, kvo, kvt, up, lse]
    out_specs = [
        pl.BlockSpec((1, q_rows, lanes), per_group),
        pl.BlockSpec((1, k_rows, 2 * lanes), per_group),
        pl.BlockSpec((1, k_rows, 2 * lanes), turned),
    ]
    out_shape = [
        jax.ShapeDtypeStruct((groups, q_rows, lanes), bf16),
        jax.ShapeDtypeStruct((groups, k_rows, 2 * lanes), f32),
        jax.ShapeDtypeStruct((groups, k_rows, 2 * lanes), bf16),
    ]
    scratch = []
    if has_bias:
        in_specs.append(pl.BlockSpec((1, 1, rel_rows.shape[2]), lambda i, j: (i * heads + j, 0, 0)))
        args.append(rel_rows)
        out_specs.append(pl.BlockSpec((1, 1, 2, 8, gwidth), lambda i, j: (i, j, 0, 0, 0)))
        out_shape.append(jax.ShapeDtypeStruct((groups, heads, 2, 8, gwidth), f32))
        scratch = [pltpu.VMEM((128, width), f32)] * 2 + [pltpu.VMEM((128, gwidth), f32)] * 2
    scratch = scratch + [pltpu.VMEM((q_rows, lanes), f32)] + [pltpu.VMEM((k_rows, lanes), f32)] * 4
    return pl.pallas_call(
        functools.partial(backward_kernel, has_bias, causal, centre),
        grid=(groups, heads),
        in_specs=in_specs,
        out_specs=out_specs,
        out_shape=out_shape,
        scratch_shapes=scratch,
        compiler_params=pltpu.CompilerParams(vmem_limit_bytes=40 * 2**20),
    )(*args)


def rel_grad_rows(drel, core, k_rows, centre, length):
    groups, heads, parts, eight, gwidth = drel.shape
    drel = drel.reshape(groups * heads, parts, eight, gwidth)
    line = sum(jnp.roll(drel[:, :, r, :], -r, axis=-1) for r in range(eight))
    line = jnp.roll(line, 127, axis=-1)
    own, other = bases_of(0, k_rows, core, centre)
    total = jnp.zeros((line.shape[0], length + gwidth + 128), f32)
    for part, base in ((0, own), (1, other)):
        old = lax.dynamic_slice_in_dim(total, base + 1, gwidth, 1)
        total = lax.dynamic_update_slice_in_dim(total, old + line[:, part], base + 1, 1)
    return total[:, 128 : 128 + length]


def rms_forward(inputs, gain_row):
    inverse = lax.rsqrt(jnp.mean(inputs * inputs, axis=-1, keepdims=True) + epsilon)
    return ((inputs * inverse * gain_row).astype(bf16), inverse)


def rms_backward(inputs, gain_row, inverse, upstream):
    upstream = upstream.astype(bf16).astype(f32)
    gain_grad = jnp.sum(upstream * inputs * inverse, axis=0)
    inner = jnp.sum(upstream * gain_row * inputs, axis=-1, keepdims=True)
    result = inverse * gain_row * upstream - inputs * (inverse**3 * inner / inputs.shape[-1])
    return (result, gain_grad)


def project(rows, weights):
    return jnp.einsum("rk,nkc->nrc", rows, weights, preferred_element_type=f32)


def project_back(grads, weights):
    return jnp.einsum("nrc,nkc->rk", grads, weights, preferred_element_type=f32)


def outer(rows, grads):
    return jnp.einsum("rk,nrc->nkc", rows, grads, preferred_element_type=f32)


MESH = pl.DeviceIdType.MESH


def greet(peers):
    barrier = pltpu.get_barrier_semaphore()
    for peer in peers:
        pl.semaphore_signal(barrier, inc=1, device_id=peer, device_id_type=MESH)
    pl.semaphore_wait(barrier, len(peers))


def remote(src, dst, send_sem, recv_sem, peer):
    return pltpu.make_async_remote_copy(
        src_ref=src, dst_ref=dst, send_sem=send_sem, recv_sem=recv_sem,
        device_id=peer, device_id_type=MESH,
    )


START_ORDER = (
    (0, 1), (1, 0), (2, 0), (0, 2), (9, 7), (1, 1), (5, 0),
    (0, 3), (1, 2), (2, 1), (3, 0), (2, 2), (4, 0), (9, 3), (9, 5),
    (3, 1), (9, 1), (5, 1), (1, 3), (8, 1), (9, 6), (3, 2), (2, 3),
    (4, 1), (6, 0), (4, 2), (1, 5), (8, 3), (3, 3), (6, 1), (0, 5),
    (4, 3), (7, 3), (8, 2), (5, 2), (9, 2), (7, 1), (3, 5), (5, 3),
    (6, 2), (9, 4), (7, 2), (4, 5), (8, 0), (6, 3), (9, 0), (7, 0),
    (2, 5), (5, 5), (6, 5),
)


def start_kernel(
    units, ids_ref, small_ref, table_in, shard_ref, *refs
):
    full_refs, refs = refs[:units], refs[units:]
    (
        mine_ref, table_ref, ids_out, small_out, small_sorted,
        ids_all, small_all, chunks, chunk_sem, small_send, small_recv, ids_col, looked,
        from_x, from_z1, from_z2,
        own_sem, w_send, w_recv, id_send, id_recv, e_send, e_recv,
    ) = refs
    wide, narrow = lax.axis_index("wide"), lax.axis_index("narrow")
    flip = lambda bit: wide + bit - 2 * bit * (wide // bit % 2)
    z2, z1, x = wide // 4, wide // 2 % 2, wide % 2
    at_x, at_z1, at_z2 = (flip(1), narrow), (flip(2), narrow), (flip(4), narrow)
    at_core = (wide, narrow + 1 - 2 * (narrow % 2))
    at_y = (wide, narrow + 2 - 4 * (narrow // 2))
    others = []
    for r in range(1, 8):
        there = wide
        for bit in (1, 2, 4):
            if r & bit:
                there = there + bit - 2 * bit * (wide // bit % 2)
        others.append((there, narrow))
    at_both = (wide, 3 - narrow)
    greet(others + [at_core, at_y, at_both])
    vocab = table_in.shape[0]

    def own(j):
        return pltpu.make_async_copy(shard_ref.at[j], full_refs[j].at[0, z2, z1, x], own_sem.at[j])

    def copy(j, stage):
        if stage == 0:
            src, dst, peer = shard_ref.at[j], full_refs[j].at[0, z2, z1, x], at_z2
        elif stage == 1:
            src = dst = full_refs[j].at[0, :, z1, x]
            peer = at_z1
        elif stage == 2:
            src = dst = full_refs[j].at[0, :, :, x]
            peer = at_x
        elif stage == 3:
            src, dst, peer = full_refs[j].at[0], full_refs[j].at[2], at_y
        elif stage == 4:
            src, dst, peer = full_refs[j].at[0], full_refs[j].at[1], at_core
        else:
            src, dst, peer = full_refs[j].at[2], full_refs[j].at[3], at_core
        return remote(src, dst, w_send.at[j, stage], w_recv.at[j, stage], peer)

    def advance(j, stage):
        if stage == 1:
            own(j).wait()
        if stage > 0:
            copy(j, {5: 3}.get(stage, stage - 1)).wait_recv()
        copy(j, stage).start()
        if stage == 3:
            copy(j, 4).start()

    def ids_copy(r):
        return remote(
            ids_all.at[0], ids_all.at[r], id_send.at[r], id_recv.at[r], others[r - 1]
        )

    def small_copy(g):
        peer = (None, at_core, at_y, at_both)[g]
        return remote(small_all.at[0], small_all.at[g], small_send.at[g], small_recv.at[g], peer)

    size = chunks.shape[1]
    spans = [(at, min(size, vocab - at)) for at in range(0, vocab, size)]

    def chunk_copy(k):
        at, count = spans[k]
        return pltpu.make_async_copy(
            table_in.at[at : at + count], chunks.at[k % 2, :count], chunk_sem.at[k % 2]
        )

    chunk_copy(0).start()
    ids_all[0] = ids_ref[...]
    small_all[0] = small_ref[...]
    for j in range(units):
        own(j).start()
    advance(0, 0)
    for r in range(1, 8):
        ids_copy(r).start()
    for g in range(1, 4):
        small_copy(g).start()
    for k, (at, count) in enumerate(spans):
        if k + 1 < len(spans):
            chunk_copy(k + 1).start()
        chunk_copy(k).wait()
        table_ref[at : at + count, :] = chunks[k % 2, :count, :].astype(bf16)
    table_ref[vocab:, :] = jnp.zeros((table_ref.shape[0] - vocab, table_ref.shape[1]), bf16)

    rows = ids_ref.shape[1]

    def look_up(r):
        if r > 0:
            ids_copy(r).wait_recv()
        ids = ids_all[r] - wide * vocab
        for t in range(rows // 128):
            ids_col[t * 128 : (t + 1) * 128] = jnp.broadcast_to(
                ids[:, t * 128 : (t + 1) * 128], (128, 128)
            ).T
        col = ids_col[...]
        lane = lax.broadcasted_iota(jnp.int32, (rows, 128), 1)
        hot = jnp.concatenate(
            [
                (col == lane + at).astype(f32).astype(bf16)
                for at in range(0, table_ref.shape[0], 128)
            ],
            axis=1,
        )
        looked[r] = dot(hot, table_ref[...], 1, 0).astype(bf16)

    def e_copy(hop_at, index):
        if hop_at == 0:
            src, dst, peer = looked.at[2 * index + 1], from_x.at[index], at_x
        elif hop_at == 1:
            src, dst, peer = looked.at[4 * index + 2], from_z1.at[index], at_z1
        else:
            src, dst, peer = looked.at[4], from_z2.at[0], at_z2
        slot = (0, 4, 6)[hop_at] + index
        return remote(src, dst, e_send.at[slot], e_recv.at[slot], peer)

    for what, index in START_ORDER:
        if what < 7:
            advance(what, index)
        elif what == 9:
            look_up(index)
        elif what == 8:
            e_copy(0, index).start()
        else:
            e_copy(0, index).wait_recv()
            looked[2 * index] = looked[2 * index] + from_x[index]
            if index % 2 == 1:
                e_copy(1, index // 2).start()
            else:
                e_copy(1, index // 2).wait_recv()
                looked[2 * index] = looked[2 * index] + from_z1[index // 2]
                if index == 2:
                    e_copy(2, 0).start()
    e_copy(2, 0).wait_recv()
    mine_ref[...] = looked[0] + from_z2[0]
    for g in range(1, 4):
        small_copy(g).wait()
    ids_out[...] = ids_all[...]
    small_out[...] = small_all[...]
    for g, index in enumerate((narrow, at_core[1], at_y[1], at_both[1])):
        small_sorted[index] = small_all[g]
    for j in range(units):
        for stage in range(6):
            copy(j, stage).wait_send()
        for stage in (4, 5):
            copy(j, stage).wait_recv()
    for r in range(1, 8):
        ids_copy(r).wait_send()
    for hop_at, count in ((0, 4), (1, 2), (2, 1)):
        for index in range(count):
            e_copy(hop_at, index).wait_send()


def start_phase(ids, small, table, shards):
    units, slim, columns = shards.shape
    rows, (vocab, width) = ids.shape[1], table.shape
    padded = -(-vocab // 2048) * 2048
    any_space = pl.BlockSpec(memory_space=pl.ANY)
    vmem = pl.BlockSpec(memory_space=pltpu.VMEM)
    dma = pltpu.SemaphoreType.DMA
    *full, mine, table_pad, ids_all, small_all, small_sorted = pl.pallas_call(
        functools.partial(start_kernel, units),
        in_specs=[vmem, vmem, any_space, any_space],
        out_specs=[any_space] * units + [vmem] * 5,
        out_shape=[jax.ShapeDtypeStruct((4, 2, 2, 2, slim, columns), bf16)] * units
        + [
            jax.ShapeDtypeStruct((rows, width), bf16),
            jax.ShapeDtypeStruct((padded, width), bf16),
            jax.ShapeDtypeStruct((8, 1, rows), jnp.int32),
            jax.ShapeDtypeStruct((4, *small.shape), f32),
            jax.ShapeDtypeStruct((4, *small.shape), f32),
        ],
        scratch_shapes=[
            pltpu.VMEM((8, 1, rows), jnp.int32),
            pltpu.VMEM((4, *small.shape), f32),
            pltpu.VMEM((2, 512, width), f32),
            dma((2,)),
            dma((4,)),
            dma((4,)),
            pltpu.VMEM((rows, 128), jnp.int32),
            pltpu.VMEM((8, rows, width), bf16),
            pltpu.VMEM((4, rows, width), bf16),
            pltpu.VMEM((2, rows, width), bf16),
            pltpu.VMEM((1, rows, width), bf16),
            dma((units,)),
            dma((units, 6)),
            dma((units, 6)),
            dma((8,)),
            dma((8,)),
            dma((7,)),
            dma((7,)),
        ],
        compiler_params=pltpu.CompilerParams(
            collective_id=0, has_side_effects=True, vmem_limit_bytes=52 * 2**20
        ),
        cost_estimate=pl.CostEstimate(
            flops=2 * 8 * rows * padded * width, bytes_accessed=2 * 4 * 8 * units * slim * columns,
            transcendentals=0,
        ),
    )(ids, small, table, shards)
    full = [one.reshape(4, 8 * slim, columns) for one in full]
    return full, mine, table_pad, ids_all[:, 0], small_all, small_sorted


def head_kernel(
    vocab, final_ref, table_ref, target_ref, weight_ref, scaled_ref,
    grad_ref, part_ref, loss_ref,
    finals, table_t, logits, slopes, stats, log_total, partial, from_x, from_z1, from_z2,
    f_send, f_recv, s_send, s_recv, g_send, g_recv,
):
    wide, narrow = lax.axis_index("wide"), lax.axis_index("narrow")

    def peer(r):
        index = wide
        for bit in (1, 2, 4):
            if r & bit:
                index = index + bit - 2 * bit * (wide // bit % 2)
        return (index, narrow)

    greet([peer(r) for r in range(1, 8)])
    rows, width = final_ref.shape
    padded = table_ref.shape[0]
    step = 512
    steps = padded // step

    def f_copy(r):
        bit = 1 if r % 2 else (2 if r % 4 else 4)
        return remote(finals.at[r - bit], finals.at[r], f_send.at[r], f_recv.at[r], peer(bit))

    finals[0] = final_ref[...]
    for r in (4, 2, 1):
        f_copy(r).start()

    def chunk_at(k):
        return pl.ds(pl.multiple_of(k * step, step), step)

    def slots(k):
        return lax.broadcasted_iota(jnp.int32, (step, 1), 0) + k * step

    def pair_of(ref, p):
        return jnp.concatenate([ref[2 * p : 2 * p + 1, :], ref[2 * p + 1 : 2 * p + 2, :]], axis=1)

    def forward(p):
        both = jnp.concatenate([finals[2 * p], finals[2 * p + 1]], axis=0)
        target = pair_of(target_ref, p)

        def first(k, top):
            scores = dot(table_ref[chunk_at(k), :], both, 1, 1)
            scores = jnp.where(slots(k) < vocab, scores, -1e30)
            logits[p, chunk_at(k), :] = scores
            return jnp.maximum(top, jnp.max(scores, axis=0, keepdims=True))

        top = lax.fori_loop(0, steps, first, jnp.full((1, 2 * rows), -1e30, f32))

        def second(k, carry):
            total, hits = carry
            scores = logits[p, chunk_at(k), :]
            total = total + jnp.sum(jnp.exp(scores - top), axis=0, keepdims=True)
            hot = jnp.where(slots(k) == target, scores, 0.0)
            return total, hits + jnp.sum(hot, axis=0, keepdims=True)

        zero = jnp.zeros((1, 2 * rows), f32)
        total, hits = lax.fori_loop(0, steps, second, (zero, zero))
        for side in range(2):
            for at, value in enumerate((top, total, hits)):
                stats[0, 2 * p + side, at : at + 1, :] = value[:, side * rows : (side + 1) * rows]

    def turn(k, unused):
        at = pl.ds(pl.multiple_of(k * step, step), step)
        table_t[:, at] = table_ref[at, :].T
        return unused

    lax.fori_loop(0, steps, turn, 0)
    f_copy(2).wait_recv()
    f_copy(3).start()
    f_copy(1).wait_recv()
    forward(0)
    f_copy(4).wait_recv()
    f_copy(6).start()
    f_copy(5).start()
    f_copy(3).wait_recv()
    forward(1)
    f_copy(6).wait_recv()
    f_copy(7).start()
    f_copy(5).wait_recv()
    forward(2)
    f_copy(7).wait_recv()
    forward(3)

    def s_copy(r):
        return remote(stats.at[0], stats.at[r], s_send.at[r], s_recv.at[r], peer(r))

    for r in range(1, 8):
        s_copy(r).start()
    for r in range(1, 8):
        s_copy(r).wait()
    for q in range(8):
        tops = [stats[r, q ^ r, 0:1, :] for r in range(8)]
        best = functools.reduce(jnp.maximum, tops)
        total = sum(stats[r, q ^ r, 1:2, :] * jnp.exp(tops[r] - best) for r in range(8))
        log_total[q : q + 1, :] = best + jnp.log(total)
    hits = sum(stats[r, r, 2:3, :] for r in range(8))
    loss_ref[...] = weight_ref[...] * (log_total[0:1, :] - hits)

    def backward(p):
        target, scaled, minus = pair_of(target_ref, p), pair_of(scaled_ref, p), pair_of(log_total, p)

        def one(k, unused):
            probs = jnp.exp(logits[p, chunk_at(k), :] - minus)
            slope = scaled * (probs - (slots(k) == target).astype(f32))
            slopes[p, chunk_at(k), :] = slope.astype(bf16)
            return unused

        lax.fori_loop(0, steps, one, 0)
        down = dot(table_t[...], slopes[p], 1, 0).T.astype(bf16)
        partial[2 * p] = down[:rows]
        partial[2 * p + 1] = down[rows:]

    def g_copy(hop_at, index):
        if hop_at == 0:
            src, dst, bit = partial.at[2 * index + 1], from_x.at[index], 1
        elif hop_at == 1:
            src, dst, bit = partial.at[4 * index + 2], from_z1.at[index], 2
        else:
            src, dst, bit = partial.at[4], from_z2.at[0], 4
        slot = (0, 4, 6)[hop_at] + index
        return remote(src, dst, g_send.at[slot], g_recv.at[slot], peer(bit))

    def added(a, b):
        return (a.astype(f32) + b.astype(f32)).astype(bf16)

    def parts(start, stop):
        def one(k, unused):
            total = jnp.zeros((step, width), f32)
            for p in range(4):
                both = jnp.concatenate([finals[2 * p], finals[2 * p + 1]], axis=0)
                total = total + dot(slopes[p, chunk_at(k), :], both, 1, 0)
            part_ref[chunk_at(k), :] = total.astype(bf16)
            return unused

        lax.fori_loop(start, stop, one, 0)

    def merge(s):
        g_copy(0, s).wait_recv()
        partial[2 * s] = added(partial[2 * s], from_x[s])

    for p in (3, 1, 2, 0):
        backward(p)
        g_copy(0, p).start()
    for s in (3, 1):
        merge(s)
        g_copy(1, s // 2).start()
    parts(0, steps // 2)
    merge(2)
    g_copy(1, 1).wait_recv()
    partial[4] = added(partial[4], from_z1[1])
    g_copy(2, 0).start()
    parts(steps // 2, steps)
    merge(0)
    g_copy(1, 0).wait_recv()
    partial[0] = added(partial[0], from_z1[0])
    g_copy(2, 0).wait_recv()
    grad_ref[...] = partial[0].astype(f32) + from_z2[0].astype(f32)
    for r in range(1, 8):
        f_copy(r).wait_send()
    for hop_at, count in ((0, 4), (1, 2), (2, 1)):
        for index in range(count):
            g_copy(hop_at, index).wait_send()


def head_phase(vocab, final, table_pad, targets, weights, scaled):
    rows, width = final.shape
    padded = table_pad.shape[0]
    vmem = pl.BlockSpec(memory_space=pltpu.VMEM)
    dma = pltpu.SemaphoreType.DMA
    return pl.pallas_call(
        functools.partial(head_kernel, vocab),
        in_specs=[vmem] * 5,
        out_specs=[vmem] * 3,
        out_shape=[
            jax.ShapeDtypeStruct((rows, width), f32),
            jax.ShapeDtypeStruct((padded, width), bf16),
            jax.ShapeDtypeStruct((1, rows), f32),
        ],
        scratch_shapes=[
            pltpu.VMEM((8, rows, width), bf16),
            pltpu.VMEM((width, padded), bf16),
            pltpu.VMEM((4, padded, 2 * rows), f32),
            pltpu.VMEM((4, padded, 2 * rows), bf16),
            pltpu.VMEM((8, 8, 8, rows), f32),
            pltpu.VMEM((8, rows), f32),
            pltpu.VMEM((8, rows, width), bf16),
            pltpu.VMEM((4, rows, width), bf16),
            pltpu.VMEM((2, rows, width), bf16),
            pltpu.VMEM((1, rows, width), bf16),
            dma((8,)),
            dma((8,)),
            dma((8,)),
            dma((8,)),
            dma((7,)),
            dma((7,)),
        ],
        compiler_params=pltpu.CompilerParams(
            collective_id=2, has_side_effects=True, vmem_limit_bytes=60 * 2**20
        ),
        cost_estimate=pl.CostEstimate(
            flops=6 * 8 * rows * padded * width, bytes_accessed=20 * 2**20,
            transcendentals=2 * 8 * rows * padded,
        ),
    )(final, table_pad, targets, weights, scaled)


HELD = 4
X_FIRST = (5, 6, )
END_ORDER = (
    (0, 0), (1, 0), (0, 1), (6, 3), (1, 1), (6, 5), (9, 0), (0, 2),
    (1, 2), (2, 0), (0, 3), (6, 6), (1, 3), (2, 1), (3, 0), (9, 1),
    (0, 4), (6, 7), (1, 4), (3, 1), (0, 5), (1, 5), (7, 0), (7, 1),
    (2, 2), (7, 2), (7, 3), (2, 5), (8, 0), (2, 3), (3, 2), (0, 6),
    (4, 1), (8, 1), (4, 0), (1, 6), (3, 5), (2, 6), (3, 3), (4, 5),
    (5, 5), (8, 2), (5, 1), (4, 3), (3, 6), (4, 2), (2, 4), (4, 6),
    (5, 3), (3, 4), (5, 6), (5, 2), (4, 4), (8, 3), (5, 4), (5, 0),
)


def end_kernel(kinds, places, *refs):
    units = len(kinds)
    lefts = sorted({left for kind in kinds for left, unused in kind})
    rights = sorted({right for kind in kinds for unused, right in kind})
    count = len(lefts) + len(rights)
    inputs = refs[:count]
    left_refs = {name: inputs[i] for i, name in enumerate(lefts)}
    right_refs = {name: inputs[len(lefts) + i] for i, name in enumerate(rights)}
    ids_ref, rows_ref, head_ref, small_ref = refs[count : count + 4]
    attn_in_out, attn_out_out, ff_in_out, ff_out_out = refs[count + 4 : count + 8]
    table_out, small_out, square_out, c_in, y_in = refs[count + 8 : count + 13]
    (
        left_vm, right_a, right_b, right_c, right_d, left_t, send_c, stage, held, x_in, z1_in, z2_in,
        gathered, table_vm, table_c, table_y, small_all, small_next, square_all, square_next,
        load_sem, stage_sem, w_send, w_recv, l_send, l_recv, t_send, t_recv, s_send, s_recv, own_sem,
    ) = refs[count + 13 :]
    wide, narrow = lax.axis_index("wide"), lax.axis_index("narrow")
    z2, z1, x = wide // 4, wide // 2 % 2, wide % 2
    y, core = narrow // 2, narrow % 2

    def flipped(index, bits, r):
        for bit in bits:
            if r & bit:
                index = index + bit - 2 * bit * (index // bit % 2)
        return index

    wide_peer = lambda r: (flipped(wide, (1, 2, 4), r), narrow)
    narrow_peer = lambda g: (wide, flipped(narrow, (1, 2), g))
    greet([wide_peer(r) for r in range(1, 8)] + [narrow_peer(g) for g in range(1, 4)])

    slim, columns = ff_in_out.shape[1:]
    width = 8 * slim

    def small_copy(base, src, dst, index, peer):
        return remote(src, dst, s_send.at[base + index], s_recv.at[base + index], peer)

    def spread(base, value_ref, all_ref):
        all_ref[0] = value_ref[...]
        for r in range(1, 8):
            small_copy(base, all_ref.at[0], all_ref.at[r], r, wide_peer(r)).start()

    def spread_next(base, all_ref, next_ref):
        for r in range(1, 8):
            small_copy(base, all_ref.at[0], all_ref.at[r], r, wide_peer(r)).wait()
        next_ref[0] = jnp.sum(all_ref[...], axis=0)
        for g in range(1, 4):
            small_copy(base + 7, next_ref.at[0], next_ref.at[g], g, narrow_peer(g)).start()

    def collect(base, next_ref, result_ref):
        for g in range(1, 4):
            small_copy(base + 7, next_ref.at[0], next_ref.at[g], g, narrow_peer(g)).wait()
        result_ref[...] = jnp.sum(next_ref[...], axis=0)

    def row_copy(r):
        bit = 1 if r % 2 else (2 if r % 4 else 4)
        return remote(gathered.at[r - bit], gathered.at[r], l_send.at[r], l_recv.at[r], wide_peer(bit))

    right_space = {}

    def loads(j):
        copies = []
        for at, (left, right) in enumerate(kinds[j]):
            src = left_refs[left]
            copies.append((src, left_vm.at[at, : src.shape[0]]))
            src = right_refs[right]
            cols = src.shape[2]
            if cols == columns:
                space = right_d
            else:
                space = (right_a, right_b, right_c)[at]
            copies.append((src, space.at[:, : src.shape[1]]))
        return [
            pltpu.make_async_copy(src, dst, load_sem.at[i]) for i, (src, dst) in enumerate(copies)
        ]

    def product(j, group):
        parts = []
        for at, (left, right) in enumerate(kinds[j]):
            rows = left_refs[left].shape[0]
            cols = right_refs[right].shape[2]
            space = right_d if cols == columns else (right_a, right_b, right_c)[at]
            parts.append(dot(left_t[at, :, :rows], space[group, :rows, :], 1, 0).astype(bf16))
        whole = parts[0] if len(parts) == 1 else jnp.concatenate(parts, axis=1)
        return whole

    def w_copy(j, hop_at):
        slot = j % HELD
        if hop_at == 0:
            src, dst, peer = send_c, c_in.at[j], narrow_peer(1)
        elif hop_at == 1 and j in X_FIRST:
            src, dst, peer = held.at[slot, :, :, :, 1 - x], y_in.at[j], wide_peer(1)
        elif hop_at == 1:
            src, dst, peer = held.at[slot, 1], y_in.at[j], narrow_peer(2)
        elif hop_at == 2 and j in X_FIRST:
            src, dst, peer = held.at[slot, 1, :, :, x], x_in.at[j], narrow_peer(2)
        elif hop_at == 2:
            src, dst, peer = held.at[slot, 0, :, :, 1 - x], x_in.at[j], wide_peer(1)
        elif hop_at == 3:
            src, dst, peer = x_in.at[j, :, 1 - z1], z1_in.at[j], wide_peer(2)
        else:
            src, dst, peer = z1_in.at[j, 1 - z2], z2_in.at[j], wide_peer(4)
        return remote(src, dst, w_send.at[j, hop_at], w_recv.at[j, hop_at], peer)

    def multiply(j):
        for copy in loads(j):
            copy.wait()
        for at, (left, unused) in enumerate(kinds[j]):
            rows = left_refs[left].shape[0]
            left_t[at, :, :rows] = left_vm[at, :rows, :].T
        if j > 0:
            w_copy(j - 1, 0).wait_send()
        for side in range(2):
            send_c[side] = product(j, 2 * side + 1).reshape(send_c.shape[1:])
        w_copy(j, 0).start()
        for side in range(2):
            held[j % HELD, side] = product(j, 2 * side).reshape(held.shape[2:])
        if j + 1 < units:
            for copy in loads(j + 1):
                copy.start()

    def added(a, b):
        return (a.astype(f32) + b.astype(f32)).astype(bf16)

    def staged(src, dst):
        copy = pltpu.make_async_copy(src, dst, stage_sem.at[0])
        copy.start()
        copy.wait()

    def after_core(j):
        w_copy(j, 0).wait_recv()
        staged(c_in.at[j], stage)
        for side in (1, 0):
            held[j % HELD, side] = added(held[j % HELD, side], stage[side])
            if side == 1 and j not in X_FIRST:
                w_copy(j, 1).start()
        if j in X_FIRST:
            w_copy(j, 1).start()

    def after_first(j):
        w_copy(j, 1).wait()
        staged(y_in.at[j], stage.at[0])
        if j in X_FIRST:
            for side in (1, 0):
                held[j % HELD, side, :, :, x] = added(held[j % HELD, side, :, :, x], stage[0, side])
                if side == 1:
                    w_copy(j, 2).start()
        else:
            held[j % HELD, 0] = added(held[j % HELD, 0], stage[0])
            w_copy(j, 2).start()

    def after_second(j):
        w_copy(j, 2).wait()
        x_in[j] = added(x_in[j], held[j % HELD, 0, :, :, x])
        w_copy(j, 3).start()

    def after_z1(j):
        w_copy(j, 3).wait()
        z1_in[j] = added(z1_in[j], x_in[j, :, z1])
        w_copy(j, 4).start()

    def after_z2(j):
        w_copy(j, 4).wait()
        total = z2_in[j].astype(f32) + z1_in[j, z2].astype(f32)
        note(total)
        what, layer = places[j]
        if what == 0:
            lanes = attn_out_out.shape[1]
            parts = []
            for head in range(lanes // DH):
                for which in range(3):
                    at = which * lanes + head * DH
                    parts.append(total[:, at : at + DH])
            attn_in_out[layer] = jnp.concatenate(parts, axis=1)
            attn_out_out[layer] = total[:, 3 * lanes :].T
        elif what == 1:
            ff_in_out[layer] = total
        else:
            ff_out_out[layer] = total.T

    def note(values):
        rows = values.shape[0]
        squares = jnp.sum((values * values).reshape(rows // 8, 8, values.shape[1]), axis=0)
        for at in range(0, values.shape[1], 128):
            square_all[0] += squares[:, at : at + 128]

    quarter = table_vm.shape[1]
    tokens = gathered.shape[1]
    step = 256

    def scatter_rows(part):
        def chunk(k, unused):
            per = quarter // step
            at = pl.ds(pl.multiple_of(k % per * step, step), step)
            slot = lax.broadcasted_iota(jnp.int32, (step, 1), 0) + k * step
            hot = jnp.concatenate(
                [(slot == ids_ref[r]).astype(f32).astype(bf16) for r in range(8)], axis=1
            )
            total = table_vm[k // per, at, :].astype(f32)
            total = total + dot(hot, gathered[...].reshape(8 * tokens, width), 1, 0)
            table_vm[k // per, at, :] = total.astype(bf16)
            return unused

        count = quarter // step
        lax.fori_loop(part * count, (part + 1) * count, chunk, 0)

    def t_copy(at):
        if at == 0:
            src, dst, peer = table_vm.at[1 - core], table_c.at[0], narrow_peer(1)
        elif at == 1:
            src, dst, peer = table_vm.at[3 - core], table_c.at[1], narrow_peer(1)
        elif at == 2:
            src, dst, peer = table_vm.at[2 * (1 - y) + core], table_y, narrow_peer(2)
        elif at == 3:
            src, dst, peer = table_vm.at[narrow], table_out.at[narrow], narrow_peer(2)
        elif at == 4:
            src, dst, peer = table_vm.at[narrow], table_out.at[narrow], narrow_peer(1)
        else:
            there = 2 * (1 - y) + core
            src, dst, peer = table_out.at[there], table_out.at[there], narrow_peer(1)
        return remote(src, dst, t_send.at[at], t_recv.at[at], peer)

    def own_quarter():
        return pltpu.make_async_copy(table_vm.at[narrow], table_out.at[narrow], own_sem.at[0])

    def head_load():
        return pltpu.make_async_copy(head_ref, table_vm, own_sem.at[1])

    def rows_load():
        return pltpu.make_async_copy(rows_ref, gathered.at[0], own_sem.at[2])

    rows_load().start()
    head_load().start()
    for copy in loads(0):
        copy.start()
    square_all[0] = jnp.zeros_like(square_all[0])
    spread(0, small_ref, small_all)
    rows_load().wait()
    for r in (1, 4, 2):
        row_copy(r).start()

    def table_step(at):
        there = 2 * (1 - y) + core
        if at == 0:
            t_copy(0).start()
            t_copy(1).start()
        elif at == 1:
            for side in range(2):
                t_copy(side).wait_recv()
            table_vm[there] = added(table_vm[there], table_c[1 - y])
            t_copy(2).start()
            table_vm[narrow] = added(table_vm[narrow], table_c[y])
        elif at == 2:
            t_copy(2).wait()
            part = added(table_vm[narrow], table_y[...])
            table_vm[narrow] = part
            t_copy(3).start()
            t_copy(4).start()
            own_quarter().start()
            note(part.astype(f32))
        else:
            t_copy(3).wait_recv()
            t_copy(5).start()

    arrived = []

    def rows_step(r):
        needed = {3: 2, 5: 4, 6: 4, 7: 6}[r]
        if needed not in arrived:
            arrived.append(needed)
            row_copy(needed).wait_recv()
        row_copy(r).start()

    def scatter_step(part):
        if part == 0:
            head_load().wait()
            for r in (1, 3, 5, 7):
                row_copy(r).wait_recv()
        scatter_rows(part)

    def small_step(at):
        if at == 0:
            spread_next(0, small_all, small_next)
        else:
            collect(0, small_next, small_out)

    acts = (
        multiply, after_core, after_first, after_second, after_z1, after_z2,
        rows_step, scatter_step, table_step, small_step,
    )
    for what, index in END_ORDER:
        acts[what](index)
    for r in range(1, 8):
        small_copy(16, square_all.at[0], square_all.at[r], r, wide_peer(r)).start()
    spread_next(16, square_all, square_next)
    collect(16, square_next, square_out)
    t_copy(4).wait_recv()
    t_copy(5).wait_recv()
    for at in (0, 1, 3, 4, 5):
        t_copy(at).wait_send()
    own_quarter().wait()
    w_copy(units - 1, 0).wait_send()
    for r in range(1, 8):
        row_copy(r).wait_send()


def end_phase(kinds, places, lefts, rights, ids, rows, head, small):
    units = len(kinds)
    names = sorted({left for kind in kinds for left, unused in kind})
    right_names = sorted({right for kind in kinds for unused, right in kind})
    tokens, width = rows.shape
    slim = width // 8
    quarter = head.shape[1]
    most = max(value.shape[0] for value in lefts.values())
    any_space = pl.BlockSpec(memory_space=pl.ANY)
    vmem = pl.BlockSpec(memory_space=pltpu.VMEM)
    dma = pltpu.SemaphoreType.DMA
    narrow_cols = [rights[right].shape[2] for unused, right in max(kinds, key=len)]
    args = [lefts[name] for name in names] + [rights[name] for name in right_names]
    outs = pl.pallas_call(
        functools.partial(end_kernel, kinds, places),
        in_specs=[any_space] * len(args) + [vmem, any_space, any_space, vmem],
        out_specs=[vmem] * 4 + [any_space, vmem, vmem, any_space, any_space],
        out_shape=[
            jax.ShapeDtypeStruct((3, slim, 3 * (width // 4)), f32),
            jax.ShapeDtypeStruct((3, width // 4, slim), f32),
            jax.ShapeDtypeStruct((2, slim, width), f32),
            jax.ShapeDtypeStruct((2, width, slim), f32),
            jax.ShapeDtypeStruct((4, quarter, width), bf16),
            jax.ShapeDtypeStruct(small.shape, f32),
            jax.ShapeDtypeStruct((8, 128), f32),
            jax.ShapeDtypeStruct((units, 2, 2, 2, 2, slim, width), bf16),
            jax.ShapeDtypeStruct((units, 2, 2, 2, slim, width), bf16),
        ],
        scratch_shapes=[
            pltpu.VMEM((3, most, width), bf16),
            pltpu.VMEM((4, most, narrow_cols[0]), bf16),
            pltpu.VMEM((4, most, narrow_cols[1]), bf16),
            pltpu.VMEM((4, most, narrow_cols[2]), bf16),
            pltpu.VMEM((4, most, width), bf16),
            pltpu.VMEM((3, width, most), bf16),
            pltpu.VMEM((2, 2, 2, 2, slim, width), bf16),
            pltpu.VMEM((2, 2, 2, 2, slim, width), bf16),
            pltpu.VMEM((HELD, 2, 2, 2, 2, slim, width), bf16),
            pltpu.VMEM((units, 2, 2, slim, width), bf16),
            pltpu.VMEM((units, 2, slim, width), bf16),
            pltpu.VMEM((units, slim, width), bf16),
            pltpu.VMEM((8, tokens, width), bf16),
            pltpu.VMEM((4, quarter, width), bf16),
            pltpu.VMEM((2, quarter, width), bf16),
            pltpu.VMEM((quarter, width), bf16),
            pltpu.VMEM((8, *small.shape), f32),
            pltpu.VMEM((4, *small.shape), f32),
            pltpu.VMEM((8, 8, 128), f32),
            pltpu.VMEM((4, 8, 128), f32),
            dma((6,)),
            dma((1,)),
            dma((units, 5)),
            dma((units, 5)),
            dma((8,)),
            dma((8,)),
            dma((6,)),
            dma((6,)),
            dma((32,)),
            dma((32,)),
            dma((3,)),
        ],
        compiler_params=pltpu.CompilerParams(
            collective_id=1, has_side_effects=True, vmem_limit_bytes=62 * 2**20
        ),
        cost_estimate=pl.CostEstimate(
            flops=2 * 8 * tokens * 4 * quarter * width, bytes_accessed=100 * 2**20, transcendentals=0
        ),
    )(*args, ids, rows, head, small)
    return outs[:4], *outs[4:7]


def body(
    enc_ids, enc_len, tgt_ids, tgt_len, span_mask, buckets,
    attn_in, attn_out, ff_in, ff_out, table, gains, rel,
    mom_attn_in, mom_attn_out, mom_ff_in, mom_ff_out, mom_table, mom_gains, mom_rel,
    avg_attn_in, avg_attn_out, avg_ff_in, avg_ff_out, avg_table, avg_gains, avg_rel,
):
    wide_size = lax.axis_size("wide")
    narrow_size = lax.axis_size("narrow")
    wide_index = lax.axis_index("wide")
    narrow_index = lax.axis_index("narrow")
    micro = narrow_index // 2
    core = narrow_index % 2
    width = table.shape[1]
    vocab = table.shape[0]
    enc_rows = enc_ids.shape[2] // 2
    dec_rows = tgt_ids.shape[2] // 2
    centre = (buckets.shape[0] + 1) // 2 - 1
    lanes = attn_out.shape[1]
    heads_here = lanes // DH
    slim = attn_in.shape[1]

    shards = []
    for layer in range(3):
        packed = attn_in[layer].reshape(slim, heads_here, 3, DH).transpose(0, 2, 1, 3)
        shards.append(jnp.concatenate([packed.reshape(slim, -1), attn_out[layer].T], axis=1))
    for layer in range(2):
        shards.append(ff_in[layer])
        shards.append(ff_out[layer].T)
    shards = jnp.stack(shards).astype(bf16)
    groups = narrow_index ^ jnp.arange(narrow_size)
    small = jnp.concatenate([gains.reshape(-1), rel.reshape(-1)])
    cut = gains.size
    onehot_rev = (buckets[::-1][:, None] == jnp.arange(rel.shape[1])[None, :]).astype(f32)
    onehot_rev = jnp.pad(onehot_rev, ((0, 1), (0, 0)))
    my_enc = lax.dynamic_slice(enc_ids, (micro, 0, core * enc_rows), (1, 1, enc_rows))
    others = wide_index ^ jnp.arange(wide_size)
    targets_micro = lax.dynamic_index_in_dim(tgt_ids, micro, 0, keepdims=False)[others]
    shifted = jnp.concatenate(
        [jnp.zeros((wide_size, 1), jnp.int32), targets_micro[:, :-1]], axis=1
    )
    dec_all = lax.dynamic_slice_in_dim(shifted, core * dec_rows, dec_rows, 1)
    if wide_size == 8 and narrow_size == 4:
        my_ids = jnp.concatenate([my_enc.reshape(enc_rows), dec_all[0]])[None]
        gathered, mine, table_pad, tokens, small, small_sorted = start_phase(
            my_ids, small.reshape(-1, 128), table, shards
        )
        small = small.reshape(narrow_size, -1)
        small_sorted = small_sorted.reshape(narrow_size, -1)
        local = tokens - wide_index * vocab
        held = (local >= 0) & (local < vocab)
    else:
        small_sorted = lax.all_gather(small, "narrow", axis=0, tiled=False)
        small = small_sorted[groups]
        enc_all = gather_direct(my_enc.reshape(enc_rows), "wide")
        tokens = jnp.concatenate([enc_all, dec_all], axis=1)
        local = tokens - wide_index * vocab
        held = (local >= 0) & (local < vocab)
        gathered = []
        for shard in shards:
            column = gather_sorted(shard, "wide").reshape(width, -1)
            pair = jnp.stack([column, hop(column, "narrow", 2)])
            pair = jnp.stack([pair, swap(pair)], axis=1)
            gathered.append(pair.reshape(narrow_size, width, -1))
        table_low = table.astype(bf16)
        rows = table_low[jnp.where(held, local, 0).reshape(-1)]
        rows = jnp.where(held.reshape(-1)[:, None], rows, 0).astype(bf16)
        mine = scatter_relative(rows.reshape(*local.shape, width), "wide", bf16)
    gains_full = small_sorted[:, :cut].reshape(narrow_size, *gains.shape).transpose(1, 0, 2)
    gains_full = gains_full.reshape(gains.shape[0], -1)
    rel_full = small[:, cut:].reshape(narrow_size, *rel.shape).transpose(1, 2, 0, 3)
    rel_full = rel_full.reshape(rel.shape[0], rel.shape[1], -1)
    rel_rows = [
        jnp.dot(onehot_rev, rel_full[i], precision=highest).T[:, None, :] for i in range(2)
    ]
    low_in = [gathered[i][:, :, : 3 * lanes] for i in range(3)]
    low_out = [gathered[i][:, :, 3 * lanes :] for i in range(3)]
    low_up = [gathered[3], gathered[5]]
    low_down = [gathered[4], gathered[6]]

    enc0 = mine[:enc_rows].astype(f32)
    dec0 = mine[enc_rows:].astype(f32)

    key_len = lax.dynamic_slice(enc_len, (micro, 0), (1, 1)).reshape(())
    scal = jnp.stack([core, key_len]).astype(jnp.int32)

    def attn_forward(state, gain_row, layer, source, rel_row, causal):
        normed, inverse = rms_forward(state, gain_row)
        kv = project(normed if source is None else source, low_in[layer][:, :, lanes:]).astype(bf16)
        kv_other = swap(kv)
        q = project(normed, low_in[layer][:, :, :lanes]).astype(bf16)
        mixed, lse = attend(scal, q, kv, kv_other, rel_row, centre, causal)
        update = project_back(mixed, low_out[layer])
        return (state + update, (state, inverse, normed, q, kv, kv_other, mixed, lse))

    def attn_backward(saved, upstream, gain_row, layer, source, rel_row, causal):
        state, inverse, normed, q, kv, kv_other, mixed, lse = saved
        up = upstream.astype(bf16)
        mixed_grad = project(up, low_out[layer]).astype(bf16)
        outs = attend_back(scal, q, kv, kv_other, mixed_grad, lse, rel_row, centre, causal)
        dq, dkv_own, dkv_other = outs[:3]
        dkv = (dkv_own + swap(dkv_other).astype(f32)).astype(bf16)
        normed_grad = project_back(dq, low_in[layer][:, :, :lanes])
        kv_back = project_back(dkv, low_in[layer][:, :, lanes:])
        if source is None:
            normed_grad = normed_grad + kv_back
        state_grad, gain_grad = rms_backward(state, gain_row, inverse, normed_grad)
        pieces = ((normed, dq), (normed if source is None else source, dkv), (up, mixed))
        return (upstream + state_grad, gain_grad, pieces, kv_back, outs[3] if rel_row is not None else None)

    def ff_forward(state, gain_row, layer):
        normed, inverse = rms_forward(state, gain_row)
        pre = project(normed, low_up[layer])
        hidden = jax.nn.gelu(pre).astype(bf16)
        return (state + project_back(hidden, low_down[layer]), (state, inverse, normed, pre, hidden))

    def ff_backward(saved, upstream, gain_row, layer):
        state, inverse, normed, pre, hidden = saved
        up = upstream.astype(bf16)
        hidden_grad = project(up, low_down[layer]).astype(bf16).astype(f32)
        unused, gelu_back = jax.vjp(jax.nn.gelu, pre)
        pre_grad = gelu_back(hidden_grad)[0].astype(bf16)
        normed_grad = project_back(pre_grad, low_up[layer])
        state_grad, gain_grad = rms_backward(state, gain_row, inverse, normed_grad)
        return (upstream + state_grad, gain_grad, ((normed, pre_grad),), ((up, hidden),))

    def scatter(pieces):
        grad = jnp.concatenate([outer(*piece) for piece in pieces], axis=2).astype(bf16)
        return spread(grad)

    def spread(grad):
        pairs = grad.reshape(2, 2, width, -1)
        across = pairs[:, 0].astype(f32) + swap(pairs[:, 1]).astype(f32)
        column = across[0] + hop(across[1].astype(bf16), "narrow", 2).astype(f32)
        return scatter_sorted(column.astype(bf16).reshape(wide_size, slim, -1), "wide")

    enc1, saved_a = attn_forward(enc0, gains_full[0], 0, None, rel_rows[0], 0)
    enc2, saved_b = ff_forward(enc1, gains_full[1], 0)
    encoded, enc_inverse = rms_forward(enc2, gains_full[2])
    dec1, saved_c = attn_forward(dec0, gains_full[3], 1, None, rel_rows[1], dec_rows)
    dec2, saved_d = attn_forward(dec1, gains_full[4], 2, encoded, None, 0)
    dec3, saved_e = ff_forward(dec2, gains_full[5], 1)
    final_gain = gains_full[6] * width ** (-0.5)
    final, final_inverse = rms_forward(dec3, final_gain)

    row_weight = (jnp.arange(2 * dec_rows)[None, None, :] < tgt_len[:, :, None]).astype(
        f32
    ) * span_mask.astype(f32)
    count = jnp.sum(row_weight)
    weights_micro = lax.dynamic_index_in_dim(row_weight, micro, 0, keepdims=False)[others]
    weights = lax.dynamic_slice_in_dim(weights_micro, core * dec_rows, dec_rows, 1).reshape(-1)
    targets = lax.dynamic_slice_in_dim(targets_micro, core * dec_rows, dec_rows, 1).reshape(-1)
    targets = targets - wide_index * vocab
    if wide_size == 8 and narrow_size == 4:
        own_weights = weights[None, :dec_rows]
        shape = (wide_size, dec_rows)
        final_grad, head_part, loss_row = head_phase(
            vocab, final, table_pad,
            jnp.where(targets < vocab, targets, -1).reshape(shape), own_weights,
            (weights / count).reshape(shape),
        )
        loss_part = jnp.sum(loss_row)
    else:
        final_all = gather_relative(final, "wide").reshape(-1, width)
        logits = dot(final_all, table_low, 1, 1)
        target_hot = jnp.arange(vocab)[None, :] == targets[:, None]
        top = jnp.max(logits, axis=-1)
        total = jnp.sum(jnp.exp(logits - top[:, None]), axis=-1)
        hits = jnp.sum(jnp.where(target_hot, logits, 0.0), axis=-1)
        stats = jnp.stack([top, total, hits]).reshape(3, wide_size, dec_rows)
        if wide_size > 8:
            stats = lax.all_gather(stats[:, others], "wide", axis=0, tiled=False)[:, :, others]
        else:
            stats = jnp.stack(
                [stats]
                + [
                    hop(stats, "wide", r)[:, [q ^ r for q in range(wide_size)]]
                    for r in range(1, wide_size)
                ]
            )
        stats = stats.reshape(wide_size, 3, -1)
        best = jnp.max(stats[:, 0], axis=0)
        log_total = best + jnp.log(jnp.sum(stats[:, 1] * jnp.exp(stats[:, 0] - best[None]), axis=0))
        loss_rows = weights * (log_total - jnp.sum(stats[:, 2], axis=0))
        loss_part = jnp.sum(loss_rows[:dec_rows])
        logit_grad = (
            (weights / count)[:, None]
            * (jnp.exp(logits - log_total[:, None]) - target_hot.astype(f32))
        ).astype(bf16)
        final_grad = scatter_relative(
            dot(logit_grad, table_low, 1, 0).reshape(wide_size, dec_rows, width), "wide", f32
        )

    gain_grads = [None] * 7
    dec_grad, gain_raw = rms_backward(dec3, final_gain, final_inverse, final_grad)
    gain_grads[6] = gain_raw * width ** (-0.5)
    dec_grad, gain_grads[5], up1, down1 = ff_backward(saved_e, dec_grad, gains_full[5], 1)
    dec_grad, gain_grads[4], attn2, source_grad, unused = attn_backward(
        saved_d, dec_grad, gains_full[4], 2, encoded, None, 0
    )
    dec_grad, gain_grads[3], attn1, unused, drel_dec = attn_backward(
        saved_c, dec_grad, gains_full[3], 1, None, rel_rows[1], dec_rows
    )
    enc_grad, gain_grads[2] = rms_backward(enc2, gains_full[2], enc_inverse, source_grad)
    enc_grad, gain_grads[1], up0, down0 = ff_backward(saved_b, enc_grad, gains_full[1], 0)
    enc_grad, gain_grads[0], attn0, unused, drel_enc = attn_backward(
        saved_a, enc_grad, gains_full[0], 0, None, rel_rows[0], 0
    )
    length = onehot_rev.shape[0]
    rel_grad = jnp.stack(
        [
            jnp.dot(rel_grad_rows(drel_enc, core, enc_rows, centre, length), onehot_rev, precision=highest),
            jnp.dot(rel_grad_rows(drel_dec, core, dec_rows, centre, length), onehot_rev, precision=highest),
        ]
    )
    rel_grad = rel_grad.reshape(2, narrow_size, heads_here, -1)[:, groups]
    rel_grad = rel_grad.reshape(2, narrow_size * heads_here, -1)
    row_grads = jnp.concatenate([enc_grad, dec_grad], axis=0).astype(bf16)
    local = jnp.where(held, local, -1)
    if wide_size == 8 and narrow_size == 4:
        order = (up1, down1, attn2, attn1, up0, down0, attn0)
        kinds, lefts, rights = [], {}, {}
        names = {}
        for unit in order:
            kind = []
            for left, right in unit:
                name = names.setdefault(id(left), "l%02d" % len(names))
                lefts[name] = left
                rights["r%02d" % len(rights)] = right
                kind.append((name, "r%02d" % (len(rights) - 1)))
            kinds.append(tuple(kind))
        quarter = head_part.shape[0] // 4
        flat = jnp.concatenate(
            [jnp.stack(gain_grads).reshape(-1), rel_grad.reshape(-1), loss_part[None]]
        )
        small_rows = -(-flat.size // 1024) * 8
        small_in = jnp.pad(flat, (0, small_rows * 128 - flat.size)).reshape(small_rows, 128)
        matrix_grads, table_grad, small_sum, square_rows = end_phase(
            tuple(kinds), ((1, 1), (2, 1), (0, 2), (0, 1), (1, 0), (2, 0), (0, 0)), lefts, rights, local[:, None, :], row_grads,
            head_part.reshape(4, quarter, width), small_in,
        )
        table_grad = table_grad.reshape(4 * quarter, width)[:vocab].astype(f32)
        small_sum = small_sum.reshape(-1)
        cut = 7 * width
        gain_total = small_sum[:cut].reshape(7, width)
        rel_total = small_sum[cut : cut + rel_grad.size].reshape(rel_grad.shape)
        loss_sum = small_sum[cut + rel_grad.size]
        square_sum = jnp.sum(square_rows)
    else:
        reduced = [scatter(grad) for grad in (attn0, attn1, attn2, up0, down0, up1, down1)]

        padded = -(-vocab // 64) * 64
        slots = jnp.arange(padded)
        local = local.reshape(-1, 2, local.shape[1])
        halves, part_grads = [], []
        half = width // 2
        for start in (0, half):
            rows = row_grads[None, :, start : start + half]
            for bit in list(bits_down("wide"))[:-1]:
                rows = jnp.stack([rows, hop(rows, "wide", bit)], axis=1)
                rows = rows.reshape(-1, *rows.shape[2:])
            far = hop(rows, "wide", 1)
            partial = dot(logit_grad, final_all[:, start : start + half], 0, 0)
            partial = jnp.pad(partial, ((0, padded - vocab), (0, 0)))
            for at, values in ((local[:, 0], rows), (local[:, 1], far)):
                token_hot = (slots[:, None] == at.reshape(-1)[None, :]).astype(bf16)
                partial = partial + dot(token_hot, values.reshape(-1, half), 1, 0)
            quarters = partial.astype(bf16).reshape(narrow_size, padded // narrow_size, half)
            part = scatter_sorted(quarters, "narrow").astype(bf16)
            part_grads.append(part.astype(f32))
            halves.append(gather_sorted(part, "narrow").reshape(padded, half)[:vocab])
        table_grad = jnp.concatenate(halves, axis=1).astype(f32)

        gain_total, rel_total, loss_sum = lax.psum(
            (jnp.stack(gain_grads), rel_grad, loss_part), ("wide", "narrow")
        )
        unpack = lambda grad: (
            grad[:, : 3 * lanes].reshape(slim, 3, heads_here, DH).transpose(0, 2, 1, 3)
        ).reshape(slim, -1)
        matrix_grads = (
            jnp.stack([unpack(reduced[i]) for i in range(3)]),
            jnp.stack([reduced[i][:, 3 * lanes :].T for i in range(3)]),
            jnp.stack([reduced[3], reduced[5]]),
            jnp.stack([reduced[4].T, reduced[6].T]),
        )
        squares = sum(jnp.sum(grad * grad) for grad in reduced + part_grads)
        square_sum = lax.psum(squares, ("wide", "narrow"))
    square_sum = square_sum + jnp.sum(gain_total * gain_total) + jnp.sum(rel_total * rel_total)
    gain_mine = lax.dynamic_slice_in_dim(gain_total, narrow_index * lanes, lanes, 1)
    rel_mine = lax.dynamic_slice_in_dim(
        rel_total, narrow_index * heads_here, heads_here, 1
    ).transpose(0, 2, 1)

    grads = (*matrix_grads, table_grad, gain_mine, rel_mine)
    norm = jnp.sqrt(square_sum)
    scale = jnp.minimum(1.0, clip_norm / norm)
    base_rate = math.sqrt(PARAMS) / (3.0 * clip_norm)
    matrix_rate = base_rate / math.sqrt(width)
    rates = (
        matrix_rate, 16.0 * matrix_rate, matrix_rate, matrix_rate,
        base_rate, 0.3 * base_rate, 0.3 * base_rate,
    )
    params = (attn_in, attn_out, ff_in, ff_out, table, gains, rel)
    moms = (mom_attn_in, mom_attn_out, mom_ff_in, mom_ff_out, mom_table, mom_gains, mom_rel)
    avgs = (avg_attn_in, avg_attn_out, avg_ff_in, avg_ff_out, avg_table, avg_gains, avg_rel)
    fresh, scaled_grads, averages = ([], [], [])
    for index in range(7):
        clipped = grads[index] * scale
        moment = momentum_decay * moms[index] + clipped
        weight = params[index] - rates[index] * (clipped + momentum_decay * moment)
        fresh.append(weight)
        scaled_grads.append(clipped)
        averages.append(average_decay * avgs[index] + (1.0 - average_decay) * weight)
    return (loss_sum, count, norm, *fresh, *scaled_grads, *averages)


def solution(mesh):
    weights = (
        P(None, "wide", "narrow"),
        P(None, "narrow", "wide"),
        P(None, "wide", "narrow"),
        P(None, "narrow", "wide"),
        P("wide", None),
        P(None, "narrow"),
        P(None, None, "narrow"),
    )
    in_specs = (P(None, "wide", None), P(None, "wide"), P(), P(), P(), P()) + weights * 3
    out_specs = (P(), P(), P()) + weights * 3
    return jax.shard_map(body, mesh=mesh, in_specs=in_specs, out_specs=out_specs, check_vma=False)
```

```python
import functools
import math

import jax
import jax.numpy as jnp
from jax import lax
from jax.experimental import pallas as pl
from jax.experimental.pallas import tpu as pltpu
from jax.sharding import PartitionSpec as P

DH = 64
PARAMS = 41195520

epsilon = 1e-06
masked_score = -1000000000.0
momentum_decay = 0.9
average_decay = 0.9
clip_norm = 0.02
highest = lax.Precision.HIGHEST
bf16 = jnp.bfloat16
f32 = jnp.float32
CHUNK = 256


def dot(left, right, left_dim, right_dim):
    return lax.dot_general(
        left, right, (((left_dim,), (right_dim,)), ((), ())), preferred_element_type=f32
    )


def hop(values, axis, bit):
    size = lax.axis_size(axis)
    return lax.ppermute(values, axis, [(i, i ^ bit) for i in range(size)])


def swap(values):
    return hop(values, "narrow", 1)


def bits_down(axis):
    bit = lax.axis_size(axis) // 2
    while bit:
        yield bit
        bit //= 2


def bits_up(axis):
    return reversed(list(bits_down(axis)))


def gather_sorted(values, axis):
    index = lax.axis_index(axis)
    values = values[None]
    for bit in bits_down(axis):
        other = hop(values, axis, bit)
        upper = (index & bit) != 0
        values = jnp.stack(
            [jnp.where(upper, other, values), jnp.where(upper, values, other)], axis=1
        ).reshape(-1, *values.shape[1:])
    return values


def scatter_sorted(values, axis):
    index = lax.axis_index(axis)
    for bit in bits_up(axis):
        pairs = values.reshape(-1, 2, *values.shape[1:])
        mine = jnp.where((index & bit) != 0, 1, 0)
        kept = lax.dynamic_index_in_dim(pairs, mine, 1, keepdims=False)
        sent = lax.dynamic_index_in_dim(pairs, 1 - mine, 1, keepdims=False)
        other = hop(sent.astype(bf16), axis, bit)
        values = kept.astype(f32) + other.astype(f32)
        if values.shape[0] > 1:
            values = values.astype(bf16)
    return values[0]


def scatter_relative(values, axis, dtype):
    for bit in bits_up(axis):
        pairs = values.reshape(-1, 2, *values.shape[1:])
        other = hop(pairs[:, 1].astype(bf16), axis, bit)
        values = pairs[:, 0].astype(dtype) + other.astype(dtype)
    return values[0]


def gather_relative(values, axis):
    values = values[None]
    for bit in bits_down(axis):
        values = jnp.stack([values, hop(values, axis, bit)], axis=1)
        values = values.reshape(-1, *values.shape[2:])
    return values


def gather_direct(values, axis):
    size = lax.axis_size(axis)
    if size > 8:
        return gather_relative(values, axis)
    return jnp.stack([values] + [hop(values, axis, r) for r in range(1, size)])


def bias_strip(rel_row, base, width):
    length = rel_row.shape[1]
    row = pltpu.roll(jnp.broadcast_to(rel_row, (8, length)), length + 128 - base, 1)
    rows = jnp.broadcast_to(row[:1, : width + 128], (128, width + 128))
    return pltpu.roll(rows, 0, 1, stride=1, stride_axis=0)[:, 128:]


def part_scores(keys, queries_h, strip, col, part, core, key_len, causal):
    scores = dot(keys, queries_h, 1, 1)
    rows, cols = scores.shape
    blocks = rows // 128
    if strip is not None:
        shifts = [(blocks - 1 - j) * 128 + col for j in range(blocks)]
        bias = jnp.concatenate([strip[:, s : s + cols] for s in shifts], axis=0)
        scores = scores + bias
    where_core = core if part == 0 else 1 - core
    key_at = where_core * rows + lax.broadcasted_iota(jnp.int32, (rows, 1), 0)
    if causal:
        query_at = lax.broadcasted_iota(jnp.int32, (1, cols), 1) + col + causal * core
        return jnp.where(key_at <= query_at, scores, masked_score)
    return jnp.where(key_at < key_len, scores, masked_score)


def bases_of(size, rows, core, centre):
    own = centre - (rows // 128 - 1) * 128
    other = own - rows + core * (2 * rows)
    return own, other


def head_mask(lanes, head):
    return lax.broadcasted_iota(jnp.int32, (1, lanes), 1) // DH == head


def forward_kernel(has_bias, causal, centre, scal, q_ref, kvo_ref, kvt_ref, *rest):
    if has_bias:
        rel_ref, mixed_ref, lse_ref, so_ref, st_ref = rest
    else:
        mixed_ref, lse_ref = rest
    core, key_len = scal[0], scal[1]
    q_rows, k_rows = q_ref.shape[1], kvo_ref.shape[1]
    lanes = q_ref.shape[2]
    heads = lanes // DH
    if has_bias:
        own, other = bases_of(lanes, k_rows, core, centre)
        for head in range(heads):
            so_ref[head] = bias_strip(rel_ref[head], own, so_ref.shape[2])
            st_ref[head] = bias_strip(rel_ref[head], other, st_ref.shape[2])
    own_values, oth_values = kvo_ref[0, :, lanes:].T, kvt_ref[0, :, lanes:].T
    step = min(CHUNK, q_rows)
    for col in range(0, q_rows, step):
        mixed = []
        for head in range(heads):
            mask = head_mask(lanes, head)
            queries = jnp.where(mask, q_ref[0, col : col + step, :], 0.0).astype(bf16)
            own_s = part_scores(
                kvo_ref[0, :, :lanes], queries, so_ref.at[head] if has_bias else None,
                col, 0, core, key_len, causal,
            )
            oth_s = part_scores(
                kvt_ref[0, :, :lanes], queries, st_ref.at[head] if has_bias else None,
                col, 1, core, key_len, causal,
            )
            top = jnp.maximum(
                jnp.max(own_s, axis=0, keepdims=True), jnp.max(oth_s, axis=0, keepdims=True)
            )
            own_e, oth_e = jnp.exp(own_s - top), jnp.exp(oth_s - top)
            total = jnp.sum(own_e, axis=0, keepdims=True) + jnp.sum(oth_e, axis=0, keepdims=True)
            inverse = 1.0 / total
            rows = slice(head * DH, (head + 1) * DH)
            mixed.append(
                dot(own_values[rows], (own_e * inverse).astype(bf16), 1, 0)
                + dot(oth_values[rows], (oth_e * inverse).astype(bf16), 1, 0)
            )
            lse_ref[0, head, :, col : col + step] = top + jnp.log(total)
        mixed_ref[0, col : col + step, :] = jnp.concatenate(mixed, axis=0).T.astype(bf16)


def turned(i):
    return (i + 1 - 2 * (i % 2), 0, 0)


def attend(scal, q, kvo, kvt, rel_rows, centre, causal):
    groups, q_rows, lanes = q.shape
    k_rows = kvo.shape[1]
    heads = lanes // DH
    has_bias = rel_rows is not None
    width = q_rows + (k_rows // 128 - 1) * 128
    in_specs = [
        pl.BlockSpec(memory_space=pltpu.SMEM),
        pl.BlockSpec((1, q_rows, lanes), lambda i: (i, 0, 0)),
        pl.BlockSpec((1, k_rows, 2 * lanes), lambda i: (i, 0, 0)),
        pl.BlockSpec((1, k_rows, 2 * lanes), turned),
    ]
    args = [scal, q, kvo, kvt]
    scratch = []
    if has_bias:
        in_specs.append(pl.BlockSpec((heads, 1, rel_rows.shape[2]), lambda i: (i, 0, 0)))
        args.append(rel_rows)
        scratch = [pltpu.VMEM((heads, 128, width), f32)] * 2
    return pl.pallas_call(
        functools.partial(forward_kernel, has_bias, causal, centre),
        grid=(groups,),
        in_specs=in_specs,
        out_specs=[
            pl.BlockSpec((1, q_rows, lanes), lambda i: (i, 0, 0)),
            pl.BlockSpec((1, heads, 1, q_rows), lambda i: (i, 0, 0, 0)),
        ],
        out_shape=[
            jax.ShapeDtypeStruct((groups, q_rows, lanes), bf16),
            jax.ShapeDtypeStruct((groups, heads, 1, q_rows), f32),
        ],
        scratch_shapes=scratch,
        compiler_params=pltpu.CompilerParams(vmem_limit_bytes=40 * 2**20),
    )(*args)


def fold(strip):
    rows, width = strip.shape
    while rows > 8:
        rows //= 2
        strip = strip[:rows] + pltpu.roll(strip[rows:], width - rows, 1)
    return strip


def backward_kernel(has_bias, causal, centre, scal, q_ref, kvo_ref, kvt_ref, up_ref, lse_ref, *rest):
    if has_bias:
        rel_ref, dq_ref, dkvo_ref, dkvt_ref, drel_ref, so_ref, st_ref, go_ref, gt_ref = rest[:9]
        ko_acc, vo_acc, kt_acc, vt_acc = rest[9:]
    else:
        dq_ref, dkvo_ref, dkvt_ref, ko_acc, vo_acc, kt_acc, vt_acc = rest
    core, key_len = scal[0], scal[1]
    q_rows, k_rows = q_ref.shape[1], kvo_ref.shape[1]
    lanes = q_ref.shape[2]
    heads = lanes // DH
    if has_bias:
        own, other = bases_of(lanes, k_rows, core, centre)
        for head in range(heads):
            so_ref[head] = bias_strip(rel_ref[head], own, so_ref.shape[2])
            st_ref[head] = bias_strip(rel_ref[head], other, st_ref.shape[2])
        go_ref[...] = jnp.zeros_like(go_ref)
        gt_ref[...] = jnp.zeros_like(gt_ref)
    for acc in (ko_acc, vo_acc, kt_acc, vt_acc):
        acc[...] = jnp.zeros_like(acc)
    own_keys, oth_keys = kvo_ref[0, :, :lanes].T, kvt_ref[0, :, :lanes].T
    step = min(CHUNK, q_rows)
    for col in range(0, q_rows, step):
        all_dq = []
        for head in range(heads):
            mask = head_mask(lanes, head)
            queries = jnp.where(mask, q_ref[0, col : col + step, :], 0.0).astype(bf16)
            ups = jnp.where(mask, up_ref[0, col : col + step, :], 0.0).astype(bf16)
            lse = lse_ref[0, head, :, col : col + step]
            sides = []
            delta = jnp.zeros((1, step), f32)
            for part, kv_ref, s_ref, v_acc in (
                (0, kvo_ref, so_ref.at[head] if has_bias else None, vo_acc),
                (1, kvt_ref, st_ref.at[head] if has_bias else None, vt_acc),
            ):
                scores = part_scores(
                    kv_ref[0, :, :lanes], queries, s_ref, col, part, core, key_len, causal
                )
                probs = jnp.exp(scores - lse)
                v_acc[...] += dot(probs.astype(bf16), ups, 1, 0)
                dprobs = dot(kv_ref[0, :, lanes:], ups, 1, 1).astype(bf16).astype(f32)
                delta = delta + jnp.sum(probs * dprobs, axis=0, keepdims=True)
                sides.append((probs, dprobs))
            dq = jnp.zeros((DH, step), f32)
            for (probs, dprobs), keys, g_ref, k_acc in (
                (sides[0], own_keys, go_ref if has_bias else None, ko_acc),
                (sides[1], oth_keys, gt_ref if has_bias else None, kt_acc),
            ):
                ds = (probs * (dprobs - delta)).astype(bf16)
                k_acc[...] += dot(ds, queries, 1, 0)
                dq = dq + dot(keys[head * DH : (head + 1) * DH], ds, 1, 0)
                if has_bias:
                    wide_ds = ds.astype(f32)
                    blocks = k_rows // 128
                    for j in range(blocks):
                        at = (blocks - 1 - j) * 128 + col
                        g_ref[head, :, at : at + step] += wide_ds[j * 128 : (j + 1) * 128]
            all_dq.append(dq)
        dq_ref[0, col : col + step, :] = jnp.concatenate(all_dq, axis=0).T.astype(bf16)
    if has_bias:
        for head in range(heads):
            drel_ref[0, head, 0] = fold(go_ref[head])
            drel_ref[0, head, 1] = fold(gt_ref[head])
    dkvo_ref[0] = jnp.concatenate([ko_acc[...], vo_acc[...]], axis=1)
    dkvt_ref[0] = jnp.concatenate([kt_acc[...], vt_acc[...]], axis=1).astype(bf16)


def attend_back(scal, q, kvo, kvt, up, lse, rel_rows, centre, causal):
    groups, q_rows, lanes = q.shape
    k_rows = kvo.shape[1]
    heads = lanes // DH
    has_bias = rel_rows is not None
    width = q_rows + (k_rows // 128 - 1) * 128
    gwidth = width + 128
    per_group = lambda i: (i, 0, 0)
    in_specs = [
        pl.BlockSpec(memory_space=pltpu.SMEM),
        pl.BlockSpec((1, q_rows, lanes), per_group),
        pl.BlockSpec((1, k_rows, 2 * lanes), per_group),
        pl.BlockSpec((1, k_rows, 2 * lanes), turned),
        pl.BlockSpec((1, q_rows, lanes), per_group),
        pl.BlockSpec((1, heads, 1, q_rows), lambda i: (i, 0, 0, 0)),
    ]
    args = [scal, q, kvo, kvt, up, lse]
    out_specs = [
        pl.BlockSpec((1, q_rows, lanes), per_group),
        pl.BlockSpec((1, k_rows, 2 * lanes), per_group),
        pl.BlockSpec((1, k_rows, 2 * lanes), turned),
    ]
    out_shape = [
        jax.ShapeDtypeStruct((groups, q_rows, lanes), bf16),
        jax.ShapeDtypeStruct((groups, k_rows, 2 * lanes), f32),
        jax.ShapeDtypeStruct((groups, k_rows, 2 * lanes), bf16),
    ]
    scratch = []
    if has_bias:
        in_specs.append(pl.BlockSpec((heads, 1, rel_rows.shape[2]), lambda i: (i, 0, 0)))
        args.append(rel_rows)
        out_specs.append(pl.BlockSpec((1, heads, 2, 8, gwidth), lambda i: (i, 0, 0, 0, 0)))
        out_shape.append(jax.ShapeDtypeStruct((groups, heads, 2, 8, gwidth), f32))
        scratch = [pltpu.VMEM((heads, 128, width), f32)] * 2
        scratch = scratch + [pltpu.VMEM((heads, 128, gwidth), f32)] * 2
    scratch = scratch + [pltpu.VMEM((k_rows, lanes), f32)] * 4
    return pl.pallas_call(
        functools.partial(backward_kernel, has_bias, causal, centre),
        grid=(groups,),
        in_specs=in_specs,
        out_specs=out_specs,
        out_shape=out_shape,
        scratch_shapes=scratch,
        compiler_params=pltpu.CompilerParams(vmem_limit_bytes=40 * 2**20),
    )(*args)


def rel_grad_rows(drel, core, k_rows, centre, length):
    groups, heads, parts, eight, gwidth = drel.shape
    drel = drel.reshape(groups * heads, parts, eight, gwidth)
    line = sum(jnp.roll(drel[:, :, r, :], -r, axis=-1) for r in range(eight))
    line = jnp.roll(line, 127, axis=-1)
    own, other = bases_of(0, k_rows, core, centre)
    total = jnp.zeros((line.shape[0], length + gwidth + 128), f32)
    for part, base in ((0, own), (1, other)):
        old = lax.dynamic_slice_in_dim(total, base + 1, gwidth, 1)
        total = lax.dynamic_update_slice_in_dim(total, old + line[:, part], base + 1, 1)
    return total[:, 128 : 128 + length]


def rms_forward(inputs, gain_row):
    inverse = lax.rsqrt(jnp.mean(inputs * inputs, axis=-1, keepdims=True) + epsilon)
    return ((inputs * inverse * gain_row).astype(bf16), inverse)


def rms_backward(inputs, gain_row, inverse, upstream):
    upstream = upstream.astype(bf16).astype(f32)
    gain_grad = jnp.sum(upstream * inputs * inverse, axis=0)
    inner = jnp.sum(upstream * gain_row * inputs, axis=-1, keepdims=True)
    result = inverse * gain_row * upstream - inputs * (inverse**3 * inner / inputs.shape[-1])
    return (result, gain_grad)


def project(rows, weights):
    return jnp.einsum("rk,nkc->nrc", rows, weights, preferred_element_type=f32)


def project_back(grads, weights):
    return jnp.einsum("nrc,nkc->rk", grads, weights, preferred_element_type=f32)


def outer(rows, grads):
    return jnp.einsum("rk,nrc->nkc", rows, grads, preferred_element_type=f32)


MESH = pl.DeviceIdType.MESH


def greet(peers):
    barrier = pltpu.get_barrier_semaphore()
    for peer in peers:
        pl.semaphore_signal(barrier, inc=1, device_id=peer, device_id_type=MESH)
    pl.semaphore_wait(barrier, len(peers))


def remote(src, dst, send_sem, recv_sem, peer):
    return pltpu.make_async_remote_copy(
        src_ref=src, dst_ref=dst, send_sem=send_sem, recv_sem=recv_sem,
        device_id=peer, device_id_type=MESH,
    )


START_ORDER = (
    (9, 7), (0, 1), (1, 0), (0, 2), (9, 3), (2, 0), (1, 1), (6, 1),
    (1, 2), (0, 3), (4, 0), (2, 1), (3, 0), (2, 2), (1, 3), (3, 1),
    (6, 2), (5, 0), (8, 3), (3, 2), (0, 5), (9, 5), (4, 1), (9, 1),
    (2, 3), (9, 6), (8, 1), (9, 2), (4, 2), (8, 2), (9, 4), (3, 3),
    (6, 3), (1, 5), (5, 1), (7, 3), (4, 3), (9, 0), (7, 1), (5, 2),
    (7, 2), (5, 3), (2, 5), (3, 5), (4, 5), (8, 0), (6, 5), (5, 5),
    (7, 0),
)
OTHER_WAY = 6


def start_kernel(
    units, ids_ref, small_ref, table_in, shard_ref, *refs
):
    full_refs, refs = refs[:units], refs[units:]
    (
        mine_ref, table_ref, ids_out, small_out, small_sorted,
        ids_all, small_all, chunks, chunk_sem, small_send, small_recv, ids_col, looked,
        from_x, from_z1, from_z2,
        own_sem, w_send, w_recv, id_send, id_recv, e_send, e_recv,
    ) = refs
    wide, narrow = lax.axis_index("wide"), lax.axis_index("narrow")
    flip = lambda bit: wide + bit - 2 * bit * (wide // bit % 2)
    z2, z1, x = wide // 4, wide // 2 % 2, wide % 2
    at_x, at_z1, at_z2 = (flip(1), narrow), (flip(2), narrow), (flip(4), narrow)
    at_core = (wide, narrow + 1 - 2 * (narrow % 2))
    at_y = (wide, narrow + 2 - 4 * (narrow // 2))
    others = []
    for r in range(1, 8):
        there = wide
        for bit in (1, 2, 4):
            if r & bit:
                there = there + bit - 2 * bit * (wide // bit % 2)
        others.append((there, narrow))
    at_both = (wide, 3 - narrow)
    greet(others + [at_core, at_y, at_both])
    vocab = table_in.shape[0]

    def own(j):
        return pltpu.make_async_copy(
            shard_ref.at[j], full_refs[j].at[0, 0, z2, z1, x], own_sem.at[j]
        )

    def copy(j, stage):
        full, shard = full_refs[j], shard_ref.at[j]
        mine = full.at[0, 0, z2, z1, x]
        if j == OTHER_WAY:
            src, dst, peer = (
                (shard, mine, at_x),
                (full.at[0, 0, z2, z1], full.at[1, 0, z2, z1], at_y),
                (full.at[:, 0, z2, z1], full.at[:, 0, z2, z1], at_z1),
                (full.at[:, 0, z2], full.at[:, 0, z2], at_z2),
                None,
                (full.at[:, 0], full.at[:, 1], at_core),
            )[stage]
        else:
            src, dst, peer = (
                (shard, mine, at_z2),
                (full.at[0, 0, :, z1, x], full.at[0, 0, :, z1, x], at_z1),
                (full.at[0, 0, :, :, x], full.at[0, 0, :, :, x], at_x),
                (full.at[0, 0], full.at[1, 0], at_y),
                (full.at[0, 0], full.at[0, 1], at_core),
                (full.at[1, 0], full.at[1, 1], at_core),
            )[stage]
        return remote(src, dst, w_send.at[j, stage], w_recv.at[j, stage], peer)

    def advance(j, stage):
        if stage == 1:
            own(j).wait()
        if stage > 0:
            copy(j, {5: 3}.get(stage, stage - 1)).wait_recv()
        copy(j, stage).start()
        if stage == 3 and j != OTHER_WAY:
            copy(j, 4).start()

    def ids_copy(r):
        return remote(
            ids_all.at[0], ids_all.at[r], id_send.at[r], id_recv.at[r], others[r - 1]
        )

    def small_copy(g):
        peer = (None, at_core, at_y, at_both)[g]
        return remote(small_all.at[0], small_all.at[g], small_send.at[g], small_recv.at[g], peer)

    size = chunks.shape[1]
    spans = [(at, min(size, vocab - at)) for at in range(0, vocab, size)]

    def chunk_copy(k):
        at, count = spans[k]
        return pltpu.make_async_copy(
            table_in.at[at : at + count], chunks.at[k % 2, :count], chunk_sem.at[k % 2]
        )

    chunk_copy(0).start()
    ids_all[0] = ids_ref[...]
    small_all[0] = small_ref[...]
    for j in range(units):
        own(j).start()
    advance(0, 0)
    advance(6, 0)
    for r in range(1, 8):
        ids_copy(r).start()
    for g in range(1, 4):
        small_copy(g).start()
    for k, (at, count) in enumerate(spans):
        if k + 1 < len(spans):
            chunk_copy(k + 1).start()
        chunk_copy(k).wait()
        table_ref[at : at + count, :] = chunks[k % 2, :count, :].astype(bf16)
    table_ref[vocab:, :] = jnp.zeros((table_ref.shape[0] - vocab, table_ref.shape[1]), bf16)

    rows = ids_ref.shape[1]

    def look_up(r):
        if r > 0:
            ids_copy(r).wait_recv()
        ids = ids_all[r] - wide * vocab
        for t in range(rows // 128):
            ids_col[t * 128 : (t + 1) * 128] = jnp.broadcast_to(
                ids[:, t * 128 : (t + 1) * 128], (128, 128)
            ).T
        col = ids_col[...]
        lane = lax.broadcasted_iota(jnp.int32, (rows, 128), 1)
        hot = jnp.concatenate(
            [
                (col == lane + at).astype(f32).astype(bf16)
                for at in range(0, table_ref.shape[0], 128)
            ],
            axis=1,
        )
        looked[r] = dot(hot, table_ref[...], 1, 0).astype(bf16)

    def e_copy(hop_at, index):
        if hop_at == 0:
            src, dst, peer = looked.at[2 * index + 1], from_x.at[index], at_x
        elif hop_at == 1:
            src, dst, peer = looked.at[4 * index + 2], from_z1.at[index], at_z1
        else:
            src, dst, peer = looked.at[4], from_z2.at[0], at_z2
        slot = (0, 4, 6)[hop_at] + index
        return remote(src, dst, e_send.at[slot], e_recv.at[slot], peer)

    for what, index in START_ORDER:
        if what < 7:
            advance(what, index)
        elif what == 9:
            look_up(index)
        elif what == 8:
            e_copy(0, index).start()
        else:
            e_copy(0, index).wait_recv()
            looked[2 * index] = looked[2 * index] + from_x[index]
            if index % 2 == 1:
                e_copy(1, index // 2).start()
            else:
                e_copy(1, index // 2).wait_recv()
                looked[2 * index] = looked[2 * index] + from_z1[index // 2]
                if index == 2:
                    e_copy(2, 0).start()
    e_copy(2, 0).wait_recv()
    mine_ref[...] = looked[0] + from_z2[0]
    for g in range(1, 4):
        small_copy(g).wait()
    ids_out[...] = ids_all[...]
    small_out[...] = small_all[...]
    for g, index in enumerate((narrow, at_core[1], at_y[1], at_both[1])):
        small_sorted[index] = small_all[g]
    for j in range(units):
        core_stages = (5,) if j == OTHER_WAY else (4, 5)
        for stage in (0, 1, 2, 3, *core_stages):
            copy(j, stage).wait_send()
        for stage in core_stages:
            copy(j, stage).wait_recv()
    for r in range(1, 8):
        ids_copy(r).wait_send()
    for hop_at, count in ((0, 4), (1, 2), (2, 1)):
        for index in range(count):
            e_copy(hop_at, index).wait_send()


def start_phase(ids, small, table, shards):
    units, slim, columns = shards.shape
    rows, (vocab, width) = ids.shape[1], table.shape
    padded = -(-vocab // 2048) * 2048
    any_space = pl.BlockSpec(memory_space=pl.ANY)
    vmem = pl.BlockSpec(memory_space=pltpu.VMEM)
    dma = pltpu.SemaphoreType.DMA
    *full, mine, table_pad, ids_all, small_all, small_sorted = pl.pallas_call(
        functools.partial(start_kernel, units),
        in_specs=[vmem, vmem, any_space, any_space],
        out_specs=[any_space] * units + [vmem] * 5,
        out_shape=[jax.ShapeDtypeStruct((2, 2, 2, 2, 2, slim, columns), bf16)] * units
        + [
            jax.ShapeDtypeStruct((rows, width), bf16),
            jax.ShapeDtypeStruct((padded, width), bf16),
            jax.ShapeDtypeStruct((8, 1, rows), jnp.int32),
            jax.ShapeDtypeStruct((4, *small.shape), f32),
            jax.ShapeDtypeStruct((4, *small.shape), f32),
        ],
        scratch_shapes=[
            pltpu.VMEM((8, 1, rows), jnp.int32),
            pltpu.VMEM((4, *small.shape), f32),
            pltpu.VMEM((2, 512, width), f32),
            dma((2,)),
            dma((4,)),
            dma((4,)),
            pltpu.VMEM((rows, 128), jnp.int32),
            pltpu.VMEM((8, rows, width), bf16),
            pltpu.VMEM((4, rows, width), bf16),
            pltpu.VMEM((2, rows, width), bf16),
            pltpu.VMEM((1, rows, width), bf16),
            dma((units,)),
            dma((units, 6)),
            dma((units, 6)),
            dma((8,)),
            dma((8,)),
            dma((7,)),
            dma((7,)),
        ],
        compiler_params=pltpu.CompilerParams(
            collective_id=0, has_side_effects=True, vmem_limit_bytes=52 * 2**20
        ),
        cost_estimate=pl.CostEstimate(
            flops=2 * 8 * rows * padded * width, bytes_accessed=2 * 4 * 8 * units * slim * columns,
            transcendentals=0,
        ),
    )(ids, small, table, shards)
    full = [one.reshape(4, 8 * slim, columns) for one in full]
    return full, mine, table_pad, ids_all[:, 0], small_all, small_sorted


def head_kernel(
    vocab, final_ref, table_ref, target_ref, weight_ref, scaled_ref,
    grad_ref, part_ref, loss_ref,
    finals, table_t, logits, slopes, stats, log_total, partial, from_x, from_z1, from_z2,
    f_send, f_recv, s_send, s_recv, g_send, g_recv,
):
    wide, narrow = lax.axis_index("wide"), lax.axis_index("narrow")

    def peer(r):
        index = wide
        for bit in (1, 2, 4):
            if r & bit:
                index = index + bit - 2 * bit * (wide // bit % 2)
        return (index, narrow)

    greet([peer(r) for r in range(1, 8)])
    rows, width = final_ref.shape
    padded = table_ref.shape[0]
    step = 512
    steps = padded // step

    def f_copy(r):
        bit = 1 if r % 2 else (2 if r % 4 else 4)
        return remote(finals.at[r - bit], finals.at[r], f_send.at[r], f_recv.at[r], peer(bit))

    finals[0] = final_ref[...]
    for r in (4, 2, 1):
        f_copy(r).start()

    def chunk_at(k):
        return pl.ds(pl.multiple_of(k * step, step), step)

    def slots(k):
        return lax.broadcasted_iota(jnp.int32, (step, 1), 0) + k * step

    def pair_of(ref, p):
        return jnp.concatenate([ref[2 * p : 2 * p + 1, :], ref[2 * p + 1 : 2 * p + 2, :]], axis=1)

    def forward(p):
        both = jnp.concatenate([finals[2 * p], finals[2 * p + 1]], axis=0)
        target = pair_of(target_ref, p)

        def first(k, top):
            scores = dot(table_ref[chunk_at(k), :], both, 1, 1)
            scores = jnp.where(slots(k) < vocab, scores, -1e30)
            logits[p, chunk_at(k), :] = scores
            return jnp.maximum(top, jnp.max(scores, axis=0, keepdims=True))

        top = lax.fori_loop(0, steps, first, jnp.full((1, 2 * rows), -1e30, f32))

        def second(k, carry):
            total, hits = carry
            scores = logits[p, chunk_at(k), :]
            total = total + jnp.sum(jnp.exp(scores - top), axis=0, keepdims=True)
            hot = jnp.where(slots(k) == target, scores, 0.0)
            return total, hits + jnp.sum(hot, axis=0, keepdims=True)

        zero = jnp.zeros((1, 2 * rows), f32)
        total, hits = lax.fori_loop(0, steps, second, (zero, zero))
        for side in range(2):
            for at, value in enumerate((top, total, hits)):
                stats[0, 2 * p + side, at : at + 1, :] = value[:, side * rows : (side + 1) * rows]

    def turn(k, unused):
        at = pl.ds(pl.multiple_of(k * step, step), step)
        table_t[:, at] = table_ref[at, :].T
        return unused

    lax.fori_loop(0, steps, turn, 0)
    f_copy(2).wait_recv()
    f_copy(3).start()
    f_copy(1).wait_recv()
    forward(0)
    f_copy(4).wait_recv()
    f_copy(6).start()
    f_copy(5).start()
    f_copy(3).wait_recv()
    forward(1)
    f_copy(6).wait_recv()
    f_copy(7).start()
    f_copy(5).wait_recv()
    forward(2)
    f_copy(7).wait_recv()
    forward(3)

    def s_copy(r):
        return remote(stats.at[0], stats.at[r], s_send.at[r], s_recv.at[r], peer(r))

    for r in range(1, 8):
        s_copy(r).start()
    for r in range(1, 8):
        s_copy(r).wait()
    for q in range(8):
        tops = [stats[r, q ^ r, 0:1, :] for r in range(8)]
        best = functools.reduce(jnp.maximum, tops)
        total = sum(stats[r, q ^ r, 1:2, :] * jnp.exp(tops[r] - best) for r in range(8))
        log_total[q : q + 1, :] = best + jnp.log(total)
    hits = sum(stats[r, r, 2:3, :] for r in range(8))
    loss_ref[...] = weight_ref[...] * (log_total[0:1, :] - hits)

    def backward(p):
        target, scaled, minus = pair_of(target_ref, p), pair_of(scaled_ref, p), pair_of(log_total, p)

        def one(k, unused):
            probs = jnp.exp(logits[p, chunk_at(k), :] - minus)
            slope = scaled * (probs - (slots(k) == target).astype(f32))
            slopes[p, chunk_at(k), :] = slope.astype(bf16)
            return unused

        lax.fori_loop(0, steps, one, 0)
        down = dot(table_t[...], slopes[p], 1, 0).T.astype(bf16)
        partial[2 * p] = down[:rows]
        partial[2 * p + 1] = down[rows:]

    def g_copy(hop_at, index):
        if hop_at == 0:
            src, dst, bit = partial.at[2 * index + 1], from_x.at[index], 1
        elif hop_at == 1:
            src, dst, bit = partial.at[4 * index + 2], from_z1.at[index], 2
        else:
            src, dst, bit = partial.at[4], from_z2.at[0], 4
        slot = (0, 4, 6)[hop_at] + index
        return remote(src, dst, g_send.at[slot], g_recv.at[slot], peer(bit))

    def added(a, b):
        return (a.astype(f32) + b.astype(f32)).astype(bf16)

    def parts(start, stop):
        def one(k, unused):
            total = jnp.zeros((step, width), f32)
            for p in range(4):
                both = jnp.concatenate([finals[2 * p], finals[2 * p + 1]], axis=0)
                total = total + dot(slopes[p, chunk_at(k), :], both, 1, 0)
            part_ref[chunk_at(k), :] = total.astype(bf16)
            return unused

        lax.fori_loop(start, stop, one, 0)

    def merge(s):
        g_copy(0, s).wait_recv()
        partial[2 * s] = added(partial[2 * s], from_x[s])

    for p in (3, 1, 2, 0):
        backward(p)
        g_copy(0, p).start()
    for s in (3, 1):
        merge(s)
        g_copy(1, s // 2).start()
    parts(0, steps // 2)
    merge(2)
    g_copy(1, 1).wait_recv()
    partial[4] = added(partial[4], from_z1[1])
    g_copy(2, 0).start()
    parts(steps // 2, steps)
    merge(0)
    g_copy(1, 0).wait_recv()
    partial[0] = added(partial[0], from_z1[0])
    g_copy(2, 0).wait_recv()
    grad_ref[...] = partial[0].astype(f32) + from_z2[0].astype(f32)
    for r in range(1, 8):
        f_copy(r).wait_send()
    for hop_at, count in ((0, 4), (1, 2), (2, 1)):
        for index in range(count):
            g_copy(hop_at, index).wait_send()


def head_phase(vocab, final, table_pad, targets, weights, scaled):
    rows, width = final.shape
    padded = table_pad.shape[0]
    vmem = pl.BlockSpec(memory_space=pltpu.VMEM)
    dma = pltpu.SemaphoreType.DMA
    return pl.pallas_call(
        functools.partial(head_kernel, vocab),
        in_specs=[vmem] * 5,
        out_specs=[vmem] * 3,
        out_shape=[
            jax.ShapeDtypeStruct((rows, width), f32),
            jax.ShapeDtypeStruct((padded, width), bf16),
            jax.ShapeDtypeStruct((1, rows), f32),
        ],
        scratch_shapes=[
            pltpu.VMEM((8, rows, width), bf16),
            pltpu.VMEM((width, padded), bf16),
            pltpu.VMEM((4, padded, 2 * rows), f32),
            pltpu.VMEM((4, padded, 2 * rows), bf16),
            pltpu.VMEM((8, 8, 8, rows), f32),
            pltpu.VMEM((8, rows), f32),
            pltpu.VMEM((8, rows, width), bf16),
            pltpu.VMEM((4, rows, width), bf16),
            pltpu.VMEM((2, rows, width), bf16),
            pltpu.VMEM((1, rows, width), bf16),
            dma((8,)),
            dma((8,)),
            dma((8,)),
            dma((8,)),
            dma((7,)),
            dma((7,)),
        ],
        compiler_params=pltpu.CompilerParams(
            collective_id=2, has_side_effects=True, vmem_limit_bytes=60 * 2**20
        ),
        cost_estimate=pl.CostEstimate(
            flops=6 * 8 * rows * padded * width, bytes_accessed=20 * 2**20,
            transcendentals=2 * 8 * rows * padded,
        ),
    )(final, table_pad, targets, weights, scaled)


HELD = 4
X_FIRST = (5, 6, )
END_ORDER = (
    (0, 0), (1, 0), (0, 1), (6, 3), (1, 1), (6, 5), (9, 0), (0, 2),
    (1, 2), (2, 0), (0, 3), (6, 6), (1, 3), (2, 1), (3, 0), (9, 1),
    (0, 4), (6, 7), (1, 4), (3, 1), (0, 5), (1, 5), (7, 0), (7, 1),
    (2, 2), (7, 2), (7, 3), (2, 5), (8, 0), (2, 3), (3, 2), (0, 6),
    (4, 1), (8, 1), (4, 0), (1, 6), (3, 5), (2, 6), (3, 3), (4, 5),
    (5, 5), (8, 2), (5, 1), (4, 3), (3, 6), (4, 2), (2, 4), (4, 6),
    (5, 3), (3, 4), (5, 6), (5, 2), (4, 4), (8, 3), (5, 4), (5, 0),
)


def end_kernel(kinds, places, *refs):
    units = len(kinds)
    lefts = sorted({left for kind in kinds for left, unused in kind})
    rights = sorted({right for kind in kinds for unused, right in kind})
    count = len(lefts) + len(rights)
    inputs = refs[:count]
    left_refs = {name: inputs[i] for i, name in enumerate(lefts)}
    right_refs = {name: inputs[len(lefts) + i] for i, name in enumerate(rights)}
    ids_ref, rows_ref, head_ref, small_ref = refs[count : count + 4]
    attn_in_out, attn_out_out, ff_in_out, ff_out_out = refs[count + 4 : count + 8]
    table_out, small_out, square_out, c_in, y_in = refs[count + 8 : count + 13]
    (
        left_vm, right_a, right_b, right_c, right_d, left_t, send_c, stage, held, x_in, z1_in, z2_in,
        gathered, table_vm, table_c, table_y, small_all, small_next, square_all, square_next,
        load_sem, stage_sem, w_send, w_recv, l_send, l_recv, t_send, t_recv, s_send, s_recv, own_sem,
    ) = refs[count + 13 :]
    wide, narrow = lax.axis_index("wide"), lax.axis_index("narrow")
    z2, z1, x = wide // 4, wide // 2 % 2, wide % 2
    y, core = narrow // 2, narrow % 2

    def flipped(index, bits, r):
        for bit in bits:
            if r & bit:
                index = index + bit - 2 * bit * (index // bit % 2)
        return index

    wide_peer = lambda r: (flipped(wide, (1, 2, 4), r), narrow)
    narrow_peer = lambda g: (wide, flipped(narrow, (1, 2), g))
    greet([wide_peer(r) for r in range(1, 8)] + [narrow_peer(g) for g in range(1, 4)])

    slim, columns = ff_in_out.shape[1:]
    width = 8 * slim

    def small_copy(base, src, dst, index, peer):
        return remote(src, dst, s_send.at[base + index], s_recv.at[base + index], peer)

    def spread(base, value_ref, all_ref):
        all_ref[0] = value_ref[...]
        for r in range(1, 8):
            small_copy(base, all_ref.at[0], all_ref.at[r], r, wide_peer(r)).start()

    def spread_next(base, all_ref, next_ref):
        for r in range(1, 8):
            small_copy(base, all_ref.at[0], all_ref.at[r], r, wide_peer(r)).wait()
        next_ref[0] = jnp.sum(all_ref[...], axis=0)
        for g in range(1, 4):
            small_copy(base + 7, next_ref.at[0], next_ref.at[g], g, narrow_peer(g)).start()

    def collect(base, next_ref, result_ref):
        for g in range(1, 4):
            small_copy(base + 7, next_ref.at[0], next_ref.at[g], g, narrow_peer(g)).wait()
        result_ref[...] = jnp.sum(next_ref[...], axis=0)

    def row_copy(r):
        bit = 1 if r % 2 else (2 if r % 4 else 4)
        return remote(gathered.at[r - bit], gathered.at[r], l_send.at[r], l_recv.at[r], wide_peer(bit))

    right_space = {}

    def loads(j):
        copies = []
        for at, (left, right) in enumerate(kinds[j]):
            src = left_refs[left]
            copies.append((src, left_vm.at[at, : src.shape[0]]))
            src = right_refs[right]
            cols = src.shape[2]
            if cols == columns:
                space = right_d
            else:
                space = (right_a, right_b, right_c)[at]
            copies.append((src, space.at[:, : src.shape[1]]))
        return [
            pltpu.make_async_copy(src, dst, load_sem.at[i]) for i, (src, dst) in enumerate(copies)
        ]

    def product(j, group):
        parts = []
        for at, (left, right) in enumerate(kinds[j]):
            rows = left_refs[left].shape[0]
            cols = right_refs[right].shape[2]
            space = right_d if cols == columns else (right_a, right_b, right_c)[at]
            parts.append(dot(left_t[at, :, :rows], space[group, :rows, :], 1, 0).astype(bf16))
        whole = parts[0] if len(parts) == 1 else jnp.concatenate(parts, axis=1)
        return whole

    def w_copy(j, hop_at):
        slot = j % HELD
        if hop_at == 0:
            src, dst, peer = send_c, c_in.at[j], narrow_peer(1)
        elif hop_at == 1 and j in X_FIRST:
            src, dst, peer = held.at[slot, :, :, :, 1 - x], y_in.at[j], wide_peer(1)
        elif hop_at == 1:
            src, dst, peer = held.at[slot, 1], y_in.at[j], narrow_peer(2)
        elif hop_at == 2 and j in X_FIRST:
            src, dst, peer = held.at[slot, 1, :, :, x], x_in.at[j], narrow_peer(2)
        elif hop_at == 2:
            src, dst, peer = held.at[slot, 0, :, :, 1 - x], x_in.at[j], wide_peer(1)
        elif hop_at == 3:
            src, dst, peer = x_in.at[j, :, 1 - z1], z1_in.at[j], wide_peer(2)
        else:
            src, dst, peer = z1_in.at[j, 1 - z2], z2_in.at[j], wide_peer(4)
        return remote(src, dst, w_send.at[j, hop_at], w_recv.at[j, hop_at], peer)

    def multiply(j):
        for copy in loads(j):
            copy.wait()
        for at, (left, unused) in enumerate(kinds[j]):
            rows = left_refs[left].shape[0]
            left_t[at, :, :rows] = left_vm[at, :rows, :].T
        if j > 0:
            w_copy(j - 1, 0).wait_send()
        for side in range(2):
            send_c[side] = product(j, 2 * side + 1).reshape(send_c.shape[1:])
        w_copy(j, 0).start()
        for side in range(2):
            held[j % HELD, side] = product(j, 2 * side).reshape(held.shape[2:])
        if j + 1 < units:
            for copy in loads(j + 1):
                copy.start()

    def added(a, b):
        return (a.astype(f32) + b.astype(f32)).astype(bf16)

    def staged(src, dst):
        copy = pltpu.make_async_copy(src, dst, stage_sem.at[0])
        copy.start()
        copy.wait()

    def after_core(j):
        w_copy(j, 0).wait_recv()
        staged(c_in.at[j], stage)
        for side in (1, 0):
            held[j % HELD, side] = added(held[j % HELD, side], stage[side])
            if side == 1 and j not in X_FIRST:
                w_copy(j, 1).start()
        if j in X_FIRST:
            w_copy(j, 1).start()

    def after_first(j):
        w_copy(j, 1).wait()
        staged(y_in.at[j], stage.at[0])
        if j in X_FIRST:
            for side in (1, 0):
                held[j % HELD, side, :, :, x] = added(held[j % HELD, side, :, :, x], stage[0, side])
                if side == 1:
                    w_copy(j, 2).start()
        else:
            held[j % HELD, 0] = added(held[j % HELD, 0], stage[0])
            w_copy(j, 2).start()

    def after_second(j):
        w_copy(j, 2).wait()
        x_in[j] = added(x_in[j], held[j % HELD, 0, :, :, x])
        w_copy(j, 3).start()

    def after_z1(j):
        w_copy(j, 3).wait()
        z1_in[j] = added(z1_in[j], x_in[j, :, z1])
        w_copy(j, 4).start()

    def after_z2(j):
        w_copy(j, 4).wait()
        total = z2_in[j].astype(f32) + z1_in[j, z2].astype(f32)
        note(total)
        what, layer = places[j]
        if what == 0:
            lanes = attn_out_out.shape[1]
            parts = []
            for head in range(lanes // DH):
                for which in range(3):
                    at = which * lanes + head * DH
                    parts.append(total[:, at : at + DH])
            attn_in_out[layer] = jnp.concatenate(parts, axis=1)
            attn_out_out[layer] = total[:, 3 * lanes :].T
        elif what == 1:
            ff_in_out[layer] = total
        else:
            ff_out_out[layer] = total.T

    def note(values):
        rows = values.shape[0]
        squares = jnp.sum((values * values).reshape(rows // 8, 8, values.shape[1]), axis=0)
        for at in range(0, values.shape[1], 128):
            square_all[0] += squares[:, at : at + 128]

    quarter = table_vm.shape[1]
    tokens = gathered.shape[1]
    step = 256

    def scatter_rows(part):
        def chunk(k, unused):
            per = quarter // step
            at = pl.ds(pl.multiple_of(k % per * step, step), step)
            slot = lax.broadcasted_iota(jnp.int32, (step, 1), 0) + k * step
            hot = jnp.concatenate(
                [(slot == ids_ref[r]).astype(f32).astype(bf16) for r in range(8)], axis=1
            )
            total = table_vm[k // per, at, :].astype(f32)
            total = total + dot(hot, gathered[...].reshape(8 * tokens, width), 1, 0)
            table_vm[k // per, at, :] = total.astype(bf16)
            return unused

        count = quarter // step
        lax.fori_loop(part * count, (part + 1) * count, chunk, 0)

    def t_copy(at):
        if at == 0:
            src, dst, peer = table_vm.at[1 - core], table_c.at[0], narrow_peer(1)
        elif at == 1:
            src, dst, peer = table_vm.at[3 - core], table_c.at[1], narrow_peer(1)
        elif at == 2:
            src, dst, peer = table_vm.at[2 * (1 - y) + core], table_y, narrow_peer(2)
        elif at == 3:
            src, dst, peer = table_vm.at[narrow], table_out.at[narrow], narrow_peer(2)
        elif at == 4:
            src, dst, peer = table_vm.at[narrow], table_out.at[narrow], narrow_peer(1)
        else:
            there = 2 * (1 - y) + core
            src, dst, peer = table_out.at[there], table_out.at[there], narrow_peer(1)
        return remote(src, dst, t_send.at[at], t_recv.at[at], peer)

    def own_quarter():
        return pltpu.make_async_copy(table_vm.at[narrow], table_out.at[narrow], own_sem.at[0])

    def head_load():
        return pltpu.make_async_copy(head_ref, table_vm, own_sem.at[1])

    def rows_load():
        return pltpu.make_async_copy(rows_ref, gathered.at[0], own_sem.at[2])

    rows_load().start()
    head_load().start()
    for copy in loads(0):
        copy.start()
    square_all[0] = jnp.zeros_like(square_all[0])
    spread(0, small_ref, small_all)
    rows_load().wait()
    for r in (1, 4, 2):
        row_copy(r).start()

    def table_step(at):
        there = 2 * (1 - y) + core
        if at == 0:
            t_copy(0).start()
            t_copy(1).start()
        elif at == 1:
            for side in range(2):
                t_copy(side).wait_recv()
            table_vm[there] = added(table_vm[there], table_c[1 - y])
            t_copy(2).start()
            table_vm[narrow] = added(table_vm[narrow], table_c[y])
        elif at == 2:
            t_copy(2).wait()
            part = added(table_vm[narrow], table_y[...])
            table_vm[narrow] = part
            t_copy(3).start()
            t_copy(4).start()
            own_quarter().start()
            note(part.astype(f32))
        else:
            t_copy(3).wait_recv()
            t_copy(5).start()

    arrived = []

    def rows_step(r):
        needed = {3: 2, 5: 4, 6: 4, 7: 6}[r]
        if needed not in arrived:
            arrived.append(needed)
            row_copy(needed).wait_recv()
        row_copy(r).start()

    def scatter_step(part):
        if part == 0:
            head_load().wait()
            for r in (1, 3, 5, 7):
                row_copy(r).wait_recv()
        scatter_rows(part)

    def small_step(at):
        if at == 0:
            spread_next(0, small_all, small_next)
        else:
            collect(0, small_next, small_out)

    acts = (
        multiply, after_core, after_first, after_second, after_z1, after_z2,
        rows_step, scatter_step, table_step, small_step,
    )
    for what, index in END_ORDER:
        acts[what](index)
    for r in range(1, 8):
        small_copy(16, square_all.at[0], square_all.at[r], r, wide_peer(r)).start()
    spread_next(16, square_all, square_next)
    collect(16, square_next, square_out)
    t_copy(4).wait_recv()
    t_copy(5).wait_recv()
    for at in (0, 1, 3, 4, 5):
        t_copy(at).wait_send()
    own_quarter().wait()
    w_copy(units - 1, 0).wait_send()
    for r in range(1, 8):
        row_copy(r).wait_send()


def end_phase(kinds, places, lefts, rights, ids, rows, head, small):
    units = len(kinds)
    names = sorted({left for kind in kinds for left, unused in kind})
    right_names = sorted({right for kind in kinds for unused, right in kind})
    tokens, width = rows.shape
    slim = width // 8
    quarter = head.shape[1]
    most = max(value.shape[0] for value in lefts.values())
    any_space = pl.BlockSpec(memory_space=pl.ANY)
    vmem = pl.BlockSpec(memory_space=pltpu.VMEM)
    dma = pltpu.SemaphoreType.DMA
    narrow_cols = [rights[right].shape[2] for unused, right in max(kinds, key=len)]
    args = [lefts[name] for name in names] + [rights[name] for name in right_names]
    outs = pl.pallas_call(
        functools.partial(end_kernel, kinds, places),
        in_specs=[any_space] * len(args) + [vmem, any_space, any_space, vmem],
        out_specs=[vmem] * 4 + [any_space, vmem, vmem, any_space, any_space],
        out_shape=[
            jax.ShapeDtypeStruct((3, slim, 3 * (width // 4)), f32),
            jax.ShapeDtypeStruct((3, width // 4, slim), f32),
            jax.ShapeDtypeStruct((2, slim, width), f32),
            jax.ShapeDtypeStruct((2, width, slim), f32),
            jax.ShapeDtypeStruct((4, quarter, width), bf16),
            jax.ShapeDtypeStruct(small.shape, f32),
            jax.ShapeDtypeStruct((8, 128), f32),
            jax.ShapeDtypeStruct((units, 2, 2, 2, 2, slim, width), bf16),
            jax.ShapeDtypeStruct((units, 2, 2, 2, slim, width), bf16),
        ],
        scratch_shapes=[
            pltpu.VMEM((3, most, width), bf16),
            pltpu.VMEM((4, most, narrow_cols[0]), bf16),
            pltpu.VMEM((4, most, narrow_cols[1]), bf16),
            pltpu.VMEM((4, most, narrow_cols[2]), bf16),
            pltpu.VMEM((4, most, width), bf16),
            pltpu.VMEM((3, width, most), bf16),
            pltpu.VMEM((2, 2, 2, 2, slim, width), bf16),
            pltpu.VMEM((2, 2, 2, 2, slim, width), bf16),
            pltpu.VMEM((HELD, 2, 2, 2, 2, slim, width), bf16),
            pltpu.VMEM((units, 2, 2, slim, width), bf16),
            pltpu.VMEM((units, 2, slim, width), bf16),
            pltpu.VMEM((units, slim, width), bf16),
            pltpu.VMEM((8, tokens, width), bf16),
            pltpu.VMEM((4, quarter, width), bf16),
            pltpu.VMEM((2, quarter, width), bf16),
            pltpu.VMEM((quarter, width), bf16),
            pltpu.VMEM((8, *small.shape), f32),
            pltpu.VMEM((4, *small.shape), f32),
            pltpu.VMEM((8, 8, 128), f32),
            pltpu.VMEM((4, 8, 128), f32),
            dma((6,)),
            dma((1,)),
            dma((units, 5)),
            dma((units, 5)),
            dma((8,)),
            dma((8,)),
            dma((6,)),
            dma((6,)),
            dma((32,)),
            dma((32,)),
            dma((3,)),
        ],
        compiler_params=pltpu.CompilerParams(
            collective_id=1, has_side_effects=True, vmem_limit_bytes=62 * 2**20
        ),
        cost_estimate=pl.CostEstimate(
            flops=2 * 8 * tokens * 4 * quarter * width, bytes_accessed=100 * 2**20, transcendentals=0
        ),
    )(*args, ids, rows, head, small)
    return outs[:4], *outs[4:7]


def body(
    enc_ids, enc_len, tgt_ids, tgt_len, span_mask, buckets,
    attn_in, attn_out, ff_in, ff_out, table, gains, rel,
    mom_attn_in, mom_attn_out, mom_ff_in, mom_ff_out, mom_table, mom_gains, mom_rel,
    avg_attn_in, avg_attn_out, avg_ff_in, avg_ff_out, avg_table, avg_gains, avg_rel,
):
    wide_size = lax.axis_size("wide")
    narrow_size = lax.axis_size("narrow")
    wide_index = lax.axis_index("wide")
    narrow_index = lax.axis_index("narrow")
    micro = narrow_index // 2
    core = narrow_index % 2
    width = table.shape[1]
    vocab = table.shape[0]
    enc_rows = enc_ids.shape[2] // 2
    dec_rows = tgt_ids.shape[2] // 2
    centre = (buckets.shape[0] + 1) // 2 - 1
    lanes = attn_out.shape[1]
    heads_here = lanes // DH
    slim = attn_in.shape[1]

    shards = []
    for layer in range(3):
        packed = attn_in[layer].reshape(slim, heads_here, 3, DH).transpose(0, 2, 1, 3)
        shards.append(jnp.concatenate([packed.reshape(slim, -1), attn_out[layer].T], axis=1))
    for layer in range(2):
        shards.append(ff_in[layer])
        shards.append(ff_out[layer].T)
    shards = jnp.stack(shards).astype(bf16)
    groups = narrow_index ^ jnp.arange(narrow_size)
    small = jnp.concatenate([gains.reshape(-1), rel.reshape(-1)])
    cut = gains.size
    onehot_rev = (buckets[::-1][:, None] == jnp.arange(rel.shape[1])[None, :]).astype(f32)
    onehot_rev = jnp.pad(onehot_rev, ((0, 1), (0, 0)))
    my_enc = lax.dynamic_slice(enc_ids, (micro, 0, core * enc_rows), (1, 1, enc_rows))
    others = wide_index ^ jnp.arange(wide_size)
    targets_micro = lax.dynamic_index_in_dim(tgt_ids, micro, 0, keepdims=False)[others]
    shifted = jnp.concatenate(
        [jnp.zeros((wide_size, 1), jnp.int32), targets_micro[:, :-1]], axis=1
    )
    dec_all = lax.dynamic_slice_in_dim(shifted, core * dec_rows, dec_rows, 1)
    if wide_size == 8 and narrow_size == 4:
        my_ids = jnp.concatenate([my_enc.reshape(enc_rows), dec_all[0]])[None]
        gathered, mine, table_pad, tokens, small, small_sorted = start_phase(
            my_ids, small.reshape(-1, 128), table, shards
        )
        small = small.reshape(narrow_size, -1)
        small_sorted = small_sorted.reshape(narrow_size, -1)
        local = tokens - wide_index * vocab
        held = (local >= 0) & (local < vocab)
    else:
        small_sorted = lax.all_gather(small, "narrow", axis=0, tiled=False)
        small = small_sorted[groups]
        enc_all = gather_direct(my_enc.reshape(enc_rows), "wide")
        tokens = jnp.concatenate([enc_all, dec_all], axis=1)
        local = tokens - wide_index * vocab
        held = (local >= 0) & (local < vocab)
        gathered = []
        for shard in shards:
            column = gather_sorted(shard, "wide").reshape(width, -1)
            pair = jnp.stack([column, hop(column, "narrow", 2)])
            pair = jnp.stack([pair, swap(pair)], axis=1)
            gathered.append(pair.reshape(narrow_size, width, -1))
        table_low = table.astype(bf16)
        rows = table_low[jnp.where(held, local, 0).reshape(-1)]
        rows = jnp.where(held.reshape(-1)[:, None], rows, 0).astype(bf16)
        mine = scatter_relative(rows.reshape(*local.shape, width), "wide", bf16)
    gains_full = small_sorted[:, :cut].reshape(narrow_size, *gains.shape).transpose(1, 0, 2)
    gains_full = gains_full.reshape(gains.shape[0], -1)
    rel_full = small[:, cut:].reshape(narrow_size, *rel.shape).transpose(1, 2, 0, 3)
    rel_full = rel_full.reshape(rel.shape[0], rel.shape[1], -1)
    rel_rows = [
        jnp.dot(onehot_rev, rel_full[i], precision=highest).T[:, None, :] for i in range(2)
    ]
    low_in = [gathered[i][:, :, : 3 * lanes] for i in range(3)]
    low_out = [gathered[i][:, :, 3 * lanes :] for i in range(3)]
    low_up = [gathered[3], gathered[5]]
    low_down = [gathered[4], gathered[6]]

    enc0 = mine[:enc_rows].astype(f32)
    dec0 = mine[enc_rows:].astype(f32)

    key_len = lax.dynamic_slice(enc_len, (micro, 0), (1, 1)).reshape(())
    scal = jnp.stack([core, key_len]).astype(jnp.int32)

    def attn_forward(state, gain_row, layer, source, rel_row, causal):
        normed, inverse = rms_forward(state, gain_row)
        kv = project(normed if source is None else source, low_in[layer][:, :, lanes:]).astype(bf16)
        kv_other = swap(kv)
        q = project(normed, low_in[layer][:, :, :lanes]).astype(bf16)
        mixed, lse = attend(scal, q, kv, kv_other, rel_row, centre, causal)
        update = project_back(mixed, low_out[layer])
        return (state + update, (state, inverse, normed, q, kv, kv_other, mixed, lse))

    def attn_backward(saved, upstream, gain_row, layer, source, rel_row, causal):
        state, inverse, normed, q, kv, kv_other, mixed, lse = saved
        up = upstream.astype(bf16)
        mixed_grad = project(up, low_out[layer]).astype(bf16)
        outs = attend_back(scal, q, kv, kv_other, mixed_grad, lse, rel_row, centre, causal)
        dq, dkv_own, dkv_other = outs[:3]
        dkv = (dkv_own + swap(dkv_other).astype(f32)).astype(bf16)
        normed_grad = project_back(dq, low_in[layer][:, :, :lanes])
        kv_back = project_back(dkv, low_in[layer][:, :, lanes:])
        if source is None:
            normed_grad = normed_grad + kv_back
        state_grad, gain_grad = rms_backward(state, gain_row, inverse, normed_grad)
        pieces = ((normed, dq), (normed if source is None else source, dkv), (up, mixed))
        return (upstream + state_grad, gain_grad, pieces, kv_back, outs[3] if rel_row is not None else None)

    def ff_forward(state, gain_row, layer):
        normed, inverse = rms_forward(state, gain_row)
        pre = project(normed, low_up[layer])
        hidden = jax.nn.gelu(pre).astype(bf16)
        return (state + project_back(hidden, low_down[layer]), (state, inverse, normed, pre, hidden))

    def ff_backward(saved, upstream, gain_row, layer):
        state, inverse, normed, pre, hidden = saved
        up = upstream.astype(bf16)
        hidden_grad = project(up, low_down[layer]).astype(bf16).astype(f32)
        unused, gelu_back = jax.vjp(jax.nn.gelu, pre)
        pre_grad = gelu_back(hidden_grad)[0].astype(bf16)
        normed_grad = project_back(pre_grad, low_up[layer])
        state_grad, gain_grad = rms_backward(state, gain_row, inverse, normed_grad)
        return (upstream + state_grad, gain_grad, ((normed, pre_grad),), ((up, hidden),))

    def scatter(pieces):
        grad = jnp.concatenate([outer(*piece) for piece in pieces], axis=2).astype(bf16)
        return spread(grad)

    def spread(grad):
        pairs = grad.reshape(2, 2, width, -1)
        across = pairs[:, 0].astype(f32) + swap(pairs[:, 1]).astype(f32)
        column = across[0] + hop(across[1].astype(bf16), "narrow", 2).astype(f32)
        return scatter_sorted(column.astype(bf16).reshape(wide_size, slim, -1), "wide")

    enc1, saved_a = attn_forward(enc0, gains_full[0], 0, None, rel_rows[0], 0)
    enc2, saved_b = ff_forward(enc1, gains_full[1], 0)
    encoded, enc_inverse = rms_forward(enc2, gains_full[2])
    dec1, saved_c = attn_forward(dec0, gains_full[3], 1, None, rel_rows[1], dec_rows)
    dec2, saved_d = attn_forward(dec1, gains_full[4], 2, encoded, None, 0)
    dec3, saved_e = ff_forward(dec2, gains_full[5], 1)
    final_gain = gains_full[6] * width ** (-0.5)
    final, final_inverse = rms_forward(dec3, final_gain)

    row_weight = (jnp.arange(2 * dec_rows)[None, None, :] < tgt_len[:, :, None]).astype(
        f32
    ) * span_mask.astype(f32)
    count = jnp.sum(row_weight)
    weights_micro = lax.dynamic_index_in_dim(row_weight, micro, 0, keepdims=False)[others]
    weights = lax.dynamic_slice_in_dim(weights_micro, core * dec_rows, dec_rows, 1).reshape(-1)
    targets = lax.dynamic_slice_in_dim(targets_micro, core * dec_rows, dec_rows, 1).reshape(-1)
    targets = targets - wide_index * vocab
    if wide_size == 8 and narrow_size == 4:
        own_weights = weights[None, :dec_rows]
        shape = (wide_size, dec_rows)
        final_grad, head_part, loss_row = head_phase(
            vocab, final, table_pad,
            jnp.where(targets < vocab, targets, -1).reshape(shape), own_weights,
            (weights / count).reshape(shape),
        )
        loss_part = jnp.sum(loss_row)
    else:
        final_all = gather_relative(final, "wide").reshape(-1, width)
        logits = dot(final_all, table_low, 1, 1)
        target_hot = jnp.arange(vocab)[None, :] == targets[:, None]
        top = jnp.max(logits, axis=-1)
        total = jnp.sum(jnp.exp(logits - top[:, None]), axis=-1)
        hits = jnp.sum(jnp.where(target_hot, logits, 0.0), axis=-1)
        stats = jnp.stack([top, total, hits]).reshape(3, wide_size, dec_rows)
        if wide_size > 8:
            stats = lax.all_gather(stats[:, others], "wide", axis=0, tiled=False)[:, :, others]
        else:
            stats = jnp.stack(
                [stats]
                + [
                    hop(stats, "wide", r)[:, [q ^ r for q in range(wide_size)]]
                    for r in range(1, wide_size)
                ]
            )
        stats = stats.reshape(wide_size, 3, -1)
        best = jnp.max(stats[:, 0], axis=0)
        log_total = best + jnp.log(jnp.sum(stats[:, 1] * jnp.exp(stats[:, 0] - best[None]), axis=0))
        loss_rows = weights * (log_total - jnp.sum(stats[:, 2], axis=0))
        loss_part = jnp.sum(loss_rows[:dec_rows])
        logit_grad = (
            (weights / count)[:, None]
            * (jnp.exp(logits - log_total[:, None]) - target_hot.astype(f32))
        ).astype(bf16)
        final_grad = scatter_relative(
            dot(logit_grad, table_low, 1, 0).reshape(wide_size, dec_rows, width), "wide", f32
        )

    gain_grads = [None] * 7
    dec_grad, gain_raw = rms_backward(dec3, final_gain, final_inverse, final_grad)
    gain_grads[6] = gain_raw * width ** (-0.5)
    dec_grad, gain_grads[5], up1, down1 = ff_backward(saved_e, dec_grad, gains_full[5], 1)
    dec_grad, gain_grads[4], attn2, source_grad, unused = attn_backward(
        saved_d, dec_grad, gains_full[4], 2, encoded, None, 0
    )
    dec_grad, gain_grads[3], attn1, unused, drel_dec = attn_backward(
        saved_c, dec_grad, gains_full[3], 1, None, rel_rows[1], dec_rows
    )
    enc_grad, gain_grads[2] = rms_backward(enc2, gains_full[2], enc_inverse, source_grad)
    enc_grad, gain_grads[1], up0, down0 = ff_backward(saved_b, enc_grad, gains_full[1], 0)
    enc_grad, gain_grads[0], attn0, unused, drel_enc = attn_backward(
        saved_a, enc_grad, gains_full[0], 0, None, rel_rows[0], 0
    )
    length = onehot_rev.shape[0]
    rel_grad = jnp.stack(
        [
            jnp.dot(rel_grad_rows(drel_enc, core, enc_rows, centre, length), onehot_rev, precision=highest),
            jnp.dot(rel_grad_rows(drel_dec, core, dec_rows, centre, length), onehot_rev, precision=highest),
        ]
    )
    rel_grad = rel_grad.reshape(2, narrow_size, heads_here, -1)[:, groups]
    rel_grad = rel_grad.reshape(2, narrow_size * heads_here, -1)
    row_grads = jnp.concatenate([enc_grad, dec_grad], axis=0).astype(bf16)
    local = jnp.where(held, local, -1)
    if wide_size == 8 and narrow_size == 4:
        order = (up1, down1, attn2, attn1, up0, down0, attn0)
        kinds, lefts, rights = [], {}, {}
        names = {}
        for unit in order:
            kind = []
            for left, right in unit:
                name = names.setdefault(id(left), "l%02d" % len(names))
                lefts[name] = left
                rights["r%02d" % len(rights)] = right
                kind.append((name, "r%02d" % (len(rights) - 1)))
            kinds.append(tuple(kind))
        quarter = head_part.shape[0] // 4
        flat = jnp.concatenate(
            [jnp.stack(gain_grads).reshape(-1), rel_grad.reshape(-1), loss_part[None]]
        )
        small_rows = -(-flat.size // 1024) * 8
        small_in = jnp.pad(flat, (0, small_rows * 128 - flat.size)).reshape(small_rows, 128)
        matrix_grads, table_grad, small_sum, square_rows = end_phase(
            tuple(kinds), ((1, 1), (2, 1), (0, 2), (0, 1), (1, 0), (2, 0), (0, 0)), lefts, rights, local[:, None, :], row_grads,
            head_part.reshape(4, quarter, width), small_in,
        )
        table_grad = table_grad.reshape(4 * quarter, width)[:vocab].astype(f32)
        small_sum = small_sum.reshape(-1)
        cut = 7 * width
        gain_total = small_sum[:cut].reshape(7, width)
        rel_total = small_sum[cut : cut + rel_grad.size].reshape(rel_grad.shape)
        loss_sum = small_sum[cut + rel_grad.size]
        square_sum = jnp.sum(square_rows)
    else:
        reduced = [scatter(grad) for grad in (attn0, attn1, attn2, up0, down0, up1, down1)]

        padded = -(-vocab // 64) * 64
        slots = jnp.arange(padded)
        local = local.reshape(-1, 2, local.shape[1])
        halves, part_grads = [], []
        half = width // 2
        for start in (0, half):
            rows = row_grads[None, :, start : start + half]
            for bit in list(bits_down("wide"))[:-1]:
                rows = jnp.stack([rows, hop(rows, "wide", bit)], axis=1)
                rows = rows.reshape(-1, *rows.shape[2:])
            far = hop(rows, "wide", 1)
            partial = dot(logit_grad, final_all[:, start : start + half], 0, 0)
            partial = jnp.pad(partial, ((0, padded - vocab), (0, 0)))
            for at, values in ((local[:, 0], rows), (local[:, 1], far)):
                token_hot = (slots[:, None] == at.reshape(-1)[None, :]).astype(bf16)
                partial = partial + dot(token_hot, values.reshape(-1, half), 1, 0)
            quarters = partial.astype(bf16).reshape(narrow_size, padded // narrow_size, half)
            part = scatter_sorted(quarters, "narrow").astype(bf16)
            part_grads.append(part.astype(f32))
            halves.append(gather_sorted(part, "narrow").reshape(padded, half)[:vocab])
        table_grad = jnp.concatenate(halves, axis=1).astype(f32)

        gain_total, rel_total, loss_sum = lax.psum(
            (jnp.stack(gain_grads), rel_grad, loss_part), ("wide", "narrow")
        )
        unpack = lambda grad: (
            grad[:, : 3 * lanes].reshape(slim, 3, heads_here, DH).transpose(0, 2, 1, 3)
        ).reshape(slim, -1)
        matrix_grads = (
            jnp.stack([unpack(reduced[i]) for i in range(3)]),
            jnp.stack([reduced[i][:, 3 * lanes :].T for i in range(3)]),
            jnp.stack([reduced[3], reduced[5]]),
            jnp.stack([reduced[4].T, reduced[6].T]),
        )
        squares = sum(jnp.sum(grad * grad) for grad in reduced + part_grads)
        square_sum = lax.psum(squares, ("wide", "narrow"))
    square_sum = square_sum + jnp.sum(gain_total * gain_total) + jnp.sum(rel_total * rel_total)
    gain_mine = lax.dynamic_slice_in_dim(gain_total, narrow_index * lanes, lanes, 1)
    rel_mine = lax.dynamic_slice_in_dim(
        rel_total, narrow_index * heads_here, heads_here, 1
    ).transpose(0, 2, 1)

    grads = (*matrix_grads, table_grad, gain_mine, rel_mine)
    norm = jnp.sqrt(square_sum)
    scale = jnp.minimum(1.0, clip_norm / norm)
    base_rate = math.sqrt(PARAMS) / (3.0 * clip_norm)
    matrix_rate = base_rate / math.sqrt(width)
    rates = (
        matrix_rate, 16.0 * matrix_rate, matrix_rate, matrix_rate,
        base_rate, 0.3 * base_rate, 0.3 * base_rate,
    )
    params = (attn_in, attn_out, ff_in, ff_out, table, gains, rel)
    moms = (mom_attn_in, mom_attn_out, mom_ff_in, mom_ff_out, mom_table, mom_gains, mom_rel)
    avgs = (avg_attn_in, avg_attn_out, avg_ff_in, avg_ff_out, avg_table, avg_gains, avg_rel)
    fresh, scaled_grads, averages = ([], [], [])
    for index in range(7):
        clipped = grads[index] * scale
        moment = momentum_decay * moms[index] + clipped
        weight = params[index] - rates[index] * (clipped + momentum_decay * moment)
        fresh.append(weight)
        scaled_grads.append(clipped)
        averages.append(average_decay * avgs[index] + (1.0 - average_decay) * weight)
    return (loss_sum, count, norm, *fresh, *scaled_grads, *averages)


def solution(mesh):
    weights = (
        P(None, "wide", "narrow"),
        P(None, "narrow", "wide"),
        P(None, "wide", "narrow"),
        P(None, "narrow", "wide"),
        P("wide", None),
        P(None, "narrow"),
        P(None, None, "narrow"),
    )
    in_specs = (P(None, "wide", None), P(None, "wide"), P(), P(), P(), P()) + weights * 3
    out_specs = (P(), P(), P()) + weights * 3
    return jax.shard_map(body, mesh=mesh, in_specs=in_specs, out_specs=out_specs, check_vma=False)
```

```python
import functools
import math

import jax
import jax.numpy as jnp
from jax import lax
from jax.experimental import pallas as pl
from jax.experimental.pallas import tpu as pltpu
from jax.sharding import PartitionSpec as P

DH = 64
PARAMS = 41195520

epsilon = 1e-06
masked_score = -1000000000.0
momentum_decay = 0.9
average_decay = 0.9
clip_norm = 0.02
highest = lax.Precision.HIGHEST
bf16 = jnp.bfloat16
f32 = jnp.float32
CHUNK = 256


def dot(left, right, left_dim, right_dim):
    return lax.dot_general(
        left, right, (((left_dim,), (right_dim,)), ((), ())), preferred_element_type=f32
    )


def hop(values, axis, bit):
    size = lax.axis_size(axis)
    return lax.ppermute(values, axis, [(i, i ^ bit) for i in range(size)])


def swap(values):
    return hop(values, "narrow", 1)


def bits_down(axis):
    bit = lax.axis_size(axis) // 2
    while bit:
        yield bit
        bit //= 2


def bits_up(axis):
    return reversed(list(bits_down(axis)))


def gather_sorted(values, axis):
    index = lax.axis_index(axis)
    values = values[None]
    for bit in bits_down(axis):
        other = hop(values, axis, bit)
        upper = (index & bit) != 0
        values = jnp.stack(
            [jnp.where(upper, other, values), jnp.where(upper, values, other)], axis=1
        ).reshape(-1, *values.shape[1:])
    return values


def scatter_sorted(values, axis):
    index = lax.axis_index(axis)
    for bit in bits_up(axis):
        pairs = values.reshape(-1, 2, *values.shape[1:])
        mine = jnp.where((index & bit) != 0, 1, 0)
        kept = lax.dynamic_index_in_dim(pairs, mine, 1, keepdims=False)
        sent = lax.dynamic_index_in_dim(pairs, 1 - mine, 1, keepdims=False)
        other = hop(sent.astype(bf16), axis, bit)
        values = kept.astype(f32) + other.astype(f32)
        if values.shape[0] > 1:
            values = values.astype(bf16)
    return values[0]


def scatter_relative(values, axis, dtype):
    for bit in bits_up(axis):
        pairs = values.reshape(-1, 2, *values.shape[1:])
        other = hop(pairs[:, 1].astype(bf16), axis, bit)
        values = pairs[:, 0].astype(dtype) + other.astype(dtype)
    return values[0]


def gather_relative(values, axis):
    values = values[None]
    for bit in bits_down(axis):
        values = jnp.stack([values, hop(values, axis, bit)], axis=1)
        values = values.reshape(-1, *values.shape[2:])
    return values


def gather_direct(values, axis):
    size = lax.axis_size(axis)
    if size > 8:
        return gather_relative(values, axis)
    return jnp.stack([values] + [hop(values, axis, r) for r in range(1, size)])


def bias_strip(rel_row, base, width):
    length = rel_row.shape[1]
    row = pltpu.roll(jnp.broadcast_to(rel_row, (8, length)), length + 128 - base, 1)
    rows = jnp.broadcast_to(row[:1, : width + 128], (128, width + 128))
    return pltpu.roll(rows, 0, 1, stride=1, stride_axis=0)[:, 128:]


def part_scores(keys, queries_h, strip, col, part, core, key_len, causal):
    scores = dot(keys, queries_h, 1, 1)
    rows, cols = scores.shape
    blocks = rows // 128
    if strip is not None:
        shifts = [(blocks - 1 - j) * 128 + col for j in range(blocks)]
        bias = jnp.concatenate([strip[:, s : s + cols] for s in shifts], axis=0)
        scores = scores + bias
    where_core = core if part == 0 else 1 - core
    key_at = where_core * rows + lax.broadcasted_iota(jnp.int32, (rows, 1), 0)
    if causal:
        query_at = lax.broadcasted_iota(jnp.int32, (1, cols), 1) + col + causal * core
        return jnp.where(key_at <= query_at, scores, masked_score)
    return jnp.where(key_at < key_len, scores, masked_score)


def bases_of(size, rows, core, centre):
    own = centre - (rows // 128 - 1) * 128
    other = own - rows + core * (2 * rows)
    return own, other


def head_mask(lanes, head):
    return lax.broadcasted_iota(jnp.int32, (1, lanes), 1) // DH == head


def forward_kernel(has_bias, causal, centre, scal, q_ref, kvo_ref, kvt_ref, *rest):
    if has_bias:
        rel_ref, mixed_ref, lse_ref, so_ref, st_ref = rest
    else:
        mixed_ref, lse_ref = rest
    core, key_len = scal[0], scal[1]
    q_rows, k_rows = q_ref.shape[1], kvo_ref.shape[1]
    lanes = q_ref.shape[2]
    heads = lanes // DH
    if has_bias:
        own, other = bases_of(lanes, k_rows, core, centre)
        for head in range(heads):
            so_ref[head] = bias_strip(rel_ref[head], own, so_ref.shape[2])
            st_ref[head] = bias_strip(rel_ref[head], other, st_ref.shape[2])
    own_values, oth_values = kvo_ref[0, :, lanes:].T, kvt_ref[0, :, lanes:].T
    step = min(CHUNK, q_rows)
    for col in range(0, q_rows, step):
        mixed = []
        for head in range(heads):
            mask = head_mask(lanes, head)
            queries = jnp.where(mask, q_ref[0, col : col + step, :], 0.0).astype(bf16)
            own_s = part_scores(
                kvo_ref[0, :, :lanes], queries, so_ref.at[head] if has_bias else None,
                col, 0, core, key_len, causal,
            )
            oth_s = part_scores(
                kvt_ref[0, :, :lanes], queries, st_ref.at[head] if has_bias else None,
                col, 1, core, key_len, causal,
            )
            top = jnp.maximum(
                jnp.max(own_s, axis=0, keepdims=True), jnp.max(oth_s, axis=0, keepdims=True)
            )
            own_e, oth_e = jnp.exp(own_s - top), jnp.exp(oth_s - top)
            total = jnp.sum(own_e, axis=0, keepdims=True) + jnp.sum(oth_e, axis=0, keepdims=True)
            inverse = 1.0 / total
            rows = slice(head * DH, (head + 1) * DH)
            mixed.append(
                dot(own_values[rows], (own_e * inverse).astype(bf16), 1, 0)
                + dot(oth_values[rows], (oth_e * inverse).astype(bf16), 1, 0)
            )
            lse_ref[0, head, :, col : col + step] = top + jnp.log(total)
        mixed_ref[0, col : col + step, :] = jnp.concatenate(mixed, axis=0).T.astype(bf16)


def turned(i):
    return (i + 1 - 2 * (i % 2), 0, 0)


def attend(scal, q, kvo, kvt, rel_rows, centre, causal):
    groups, q_rows, lanes = q.shape
    k_rows = kvo.shape[1]
    heads = lanes // DH
    has_bias = rel_rows is not None
    width = q_rows + (k_rows // 128 - 1) * 128
    in_specs = [
        pl.BlockSpec(memory_space=pltpu.SMEM),
        pl.BlockSpec((1, q_rows, lanes), lambda i: (i, 0, 0)),
        pl.BlockSpec((1, k_rows, 2 * lanes), lambda i: (i, 0, 0)),
        pl.BlockSpec((1, k_rows, 2 * lanes), turned),
    ]
    args = [scal, q, kvo, kvt]
    scratch = []
    if has_bias:
        in_specs.append(pl.BlockSpec((heads, 1, rel_rows.shape[2]), lambda i: (i, 0, 0)))
        args.append(rel_rows)
        scratch = [pltpu.VMEM((heads, 128, width), f32)] * 2
    return pl.pallas_call(
        functools.partial(forward_kernel, has_bias, causal, centre),
        grid=(groups,),
        in_specs=in_specs,
        out_specs=[
            pl.BlockSpec((1, q_rows, lanes), lambda i: (i, 0, 0)),
            pl.BlockSpec((1, heads, 1, q_rows), lambda i: (i, 0, 0, 0)),
        ],
        out_shape=[
            jax.ShapeDtypeStruct((groups, q_rows, lanes), bf16),
            jax.ShapeDtypeStruct((groups, heads, 1, q_rows), f32),
        ],
        scratch_shapes=scratch,
        compiler_params=pltpu.CompilerParams(vmem_limit_bytes=40 * 2**20),
    )(*args)


def fold(strip):
    rows, width = strip.shape
    while rows > 8:
        rows //= 2
        strip = strip[:rows] + pltpu.roll(strip[rows:], width - rows, 1)
    return strip


def backward_kernel(has_bias, causal, centre, scal, q_ref, kvo_ref, kvt_ref, up_ref, lse_ref, *rest):
    if has_bias:
        rel_ref, dq_ref, dkvo_ref, dkvt_ref, drel_ref, so_ref, st_ref, go_ref, gt_ref = rest[:9]
        ko_acc, vo_acc, kt_acc, vt_acc = rest[9:]
    else:
        dq_ref, dkvo_ref, dkvt_ref, ko_acc, vo_acc, kt_acc, vt_acc = rest
    core, key_len = scal[0], scal[1]
    q_rows, k_rows = q_ref.shape[1], kvo_ref.shape[1]
    lanes = q_ref.shape[2]
    heads = lanes // DH
    if has_bias:
        own, other = bases_of(lanes, k_rows, core, centre)
        for head in range(heads):
            so_ref[head] = bias_strip(rel_ref[head], own, so_ref.shape[2])
            st_ref[head] = bias_strip(rel_ref[head], other, st_ref.shape[2])
        go_ref[...] = jnp.zeros_like(go_ref)
        gt_ref[...] = jnp.zeros_like(gt_ref)
    for acc in (ko_acc, vo_acc, kt_acc, vt_acc):
        acc[...] = jnp.zeros_like(acc)
    own_keys, oth_keys = kvo_ref[0, :, :lanes].T, kvt_ref[0, :, :lanes].T
    step = min(CHUNK, q_rows)
    for col in range(0, q_rows, step):
        all_dq = []
        for head in range(heads):
            mask = head_mask(lanes, head)
            queries = jnp.where(mask, q_ref[0, col : col + step, :], 0.0).astype(bf16)
            ups = jnp.where(mask, up_ref[0, col : col + step, :], 0.0).astype(bf16)
            lse = lse_ref[0, head, :, col : col + step]
            sides = []
            delta = jnp.zeros((1, step), f32)
            for part, kv_ref, s_ref, v_acc in (
                (0, kvo_ref, so_ref.at[head] if has_bias else None, vo_acc),
                (1, kvt_ref, st_ref.at[head] if has_bias else None, vt_acc),
            ):
                scores = part_scores(
                    kv_ref[0, :, :lanes], queries, s_ref, col, part, core, key_len, causal
                )
                probs = jnp.exp(scores - lse)
                v_acc[...] += dot(probs.astype(bf16), ups, 1, 0)
                dprobs = dot(kv_ref[0, :, lanes:], ups, 1, 1).astype(bf16).astype(f32)
                delta = delta + jnp.sum(probs * dprobs, axis=0, keepdims=True)
                sides.append((probs, dprobs))
            dq = jnp.zeros((DH, step), f32)
            for (probs, dprobs), keys, g_ref, k_acc in (
                (sides[0], own_keys, go_ref if has_bias else None, ko_acc),
                (sides[1], oth_keys, gt_ref if has_bias else None, kt_acc),
            ):
                ds = (probs * (dprobs - delta)).astype(bf16)
                k_acc[...] += dot(ds, queries, 1, 0)
                dq = dq + dot(keys[head * DH : (head + 1) * DH], ds, 1, 0)
                if has_bias:
                    wide_ds = ds.astype(f32)
                    blocks = k_rows // 128
                    for j in range(blocks):
                        at = (blocks - 1 - j) * 128 + col
                        g_ref[head, :, at : at + step] += wide_ds[j * 128 : (j + 1) * 128]
            all_dq.append(dq)
        dq_ref[0, col : col + step, :] = jnp.concatenate(all_dq, axis=0).T.astype(bf16)
    if has_bias:
        for head in range(heads):
            drel_ref[0, head, 0] = fold(go_ref[head])
            drel_ref[0, head, 1] = fold(gt_ref[head])
    dkvo_ref[0] = jnp.concatenate([ko_acc[...], vo_acc[...]], axis=1)
    dkvt_ref[0] = jnp.concatenate([kt_acc[...], vt_acc[...]], axis=1).astype(bf16)


def attend_back(scal, q, kvo, kvt, up, lse, rel_rows, centre, causal):
    groups, q_rows, lanes = q.shape
    k_rows = kvo.shape[1]
    heads = lanes // DH
    has_bias = rel_rows is not None
    width = q_rows + (k_rows // 128 - 1) * 128
    gwidth = width + 128
    per_group = lambda i: (i, 0, 0)
    in_specs = [
        pl.BlockSpec(memory_space=pltpu.SMEM),
        pl.BlockSpec((1, q_rows, lanes), per_group),
        pl.BlockSpec((1, k_rows, 2 * lanes), per_group),
        pl.BlockSpec((1, k_rows, 2 * lanes), turned),
        pl.BlockSpec((1, q_rows, lanes), per_group),
        pl.BlockSpec((1, heads, 1, q_rows), lambda i: (i, 0, 0, 0)),
    ]
    args = [scal, q, kvo, kvt, up, lse]
    out_specs = [
        pl.BlockSpec((1, q_rows, lanes), per_group),
        pl.BlockSpec((1, k_rows, 2 * lanes), per_group),
        pl.BlockSpec((1, k_rows, 2 * lanes), turned),
    ]
    out_shape = [
        jax.ShapeDtypeStruct((groups, q_rows, lanes), bf16),
        jax.ShapeDtypeStruct((groups, k_rows, 2 * lanes), f32),
        jax.ShapeDtypeStruct((groups, k_rows, 2 * lanes), bf16),
    ]
    scratch = []
    if has_bias:
        in_specs.append(pl.BlockSpec((heads, 1, rel_rows.shape[2]), lambda i: (i, 0, 0)))
        args.append(rel_rows)
        out_specs.append(pl.BlockSpec((1, heads, 2, 8, gwidth), lambda i: (i, 0, 0, 0, 0)))
        out_shape.append(jax.ShapeDtypeStruct((groups, heads, 2, 8, gwidth), f32))
        scratch = [pltpu.VMEM((heads, 128, width), f32)] * 2
        scratch = scratch + [pltpu.VMEM((heads, 128, gwidth), f32)] * 2
    scratch = scratch + [pltpu.VMEM((k_rows, lanes), f32)] * 4
    return pl.pallas_call(
        functools.partial(backward_kernel, has_bias, causal, centre),
        grid=(groups,),
        in_specs=in_specs,
        out_specs=out_specs,
        out_shape=out_shape,
        scratch_shapes=scratch,
        compiler_params=pltpu.CompilerParams(vmem_limit_bytes=40 * 2**20),
    )(*args)


def rel_grad_rows(drel, core, k_rows, centre, length):
    groups, heads, parts, eight, gwidth = drel.shape
    drel = drel.reshape(groups * heads, parts, eight, gwidth)
    line = sum(jnp.roll(drel[:, :, r, :], -r, axis=-1) for r in range(eight))
    line = jnp.roll(line, 127, axis=-1)
    own, other = bases_of(0, k_rows, core, centre)
    total = jnp.zeros((line.shape[0], length + gwidth + 128), f32)
    for part, base in ((0, own), (1, other)):
        old = lax.dynamic_slice_in_dim(total, base + 1, gwidth, 1)
        total = lax.dynamic_update_slice_in_dim(total, old + line[:, part], base + 1, 1)
    return total[:, 128 : 128 + length]


def rms_forward(inputs, gain_row):
    inverse = lax.rsqrt(jnp.mean(inputs * inputs, axis=-1, keepdims=True) + epsilon)
    return ((inputs * inverse * gain_row).astype(bf16), inverse)


def rms_backward(inputs, gain_row, inverse, upstream):
    upstream = upstream.astype(bf16).astype(f32)
    gain_grad = jnp.sum(upstream * inputs * inverse, axis=0)
    inner = jnp.sum(upstream * gain_row * inputs, axis=-1, keepdims=True)
    result = inverse * gain_row * upstream - inputs * (inverse**3 * inner / inputs.shape[-1])
    return (result, gain_grad)


def project(rows, weights):
    return jnp.einsum("rk,nkc->nrc", rows, weights, preferred_element_type=f32)


def project_back(grads, weights):
    return jnp.einsum("nrc,nkc->rk", grads, weights, preferred_element_type=f32)


def outer(rows, grads):
    return jnp.einsum("rk,nrc->nkc", rows, grads, preferred_element_type=f32)


MESH = pl.DeviceIdType.MESH


def greet(peers):
    barrier = pltpu.get_barrier_semaphore()
    for peer in peers:
        pl.semaphore_signal(barrier, inc=1, device_id=peer, device_id_type=MESH)
    pl.semaphore_wait(barrier, len(peers))


def remote(src, dst, send_sem, recv_sem, peer):
    return pltpu.make_async_remote_copy(
        src_ref=src, dst_ref=dst, send_sem=send_sem, recv_sem=recv_sem,
        device_id=peer, device_id_type=MESH,
    )


START_ORDER = (
    (9, 7), (0, 1), (1, 0), (0, 2), (9, 3), (2, 0), (1, 1), (6, 1),
    (1, 2), (0, 3), (4, 0), (2, 1), (3, 0), (2, 2), (1, 3), (3, 1),
    (6, 2), (5, 0), (8, 3), (3, 2), (0, 5), (9, 5), (4, 1), (9, 1),
    (2, 3), (9, 6), (8, 1), (9, 2), (4, 2), (8, 2), (9, 4), (3, 3),
    (6, 3), (1, 5), (5, 1), (7, 3), (4, 3), (9, 0), (7, 1), (5, 2),
    (7, 2), (5, 3), (2, 5), (3, 5), (4, 5), (8, 0), (6, 5), (5, 5),
    (7, 0),
)
OTHER_WAY = 6


def start_kernel(
    units, ids_ref, small_ref, table_in, shard_ref, *refs
):
    full_refs, refs = refs[:units], refs[units:]
    (
        mine_ref, table_ref, ids_out, small_out, small_sorted,
        ids_all, small_all, chunks, chunk_sem, small_send, small_recv, ids_col, looked,
        from_x, from_z1, from_z2,
        own_sem, w_send, w_recv, id_send, id_recv, e_send, e_recv,
    ) = refs
    wide, narrow = lax.axis_index("wide"), lax.axis_index("narrow")
    flip = lambda bit: wide + bit - 2 * bit * (wide // bit % 2)
    z2, z1, x = wide // 4, wide // 2 % 2, wide % 2
    at_x, at_z1, at_z2 = (flip(1), narrow), (flip(2), narrow), (flip(4), narrow)
    at_core = (wide, narrow + 1 - 2 * (narrow % 2))
    at_y = (wide, narrow + 2 - 4 * (narrow // 2))
    others = []
    for r in range(1, 8):
        there = wide
        for bit in (1, 2, 4):
            if r & bit:
                there = there + bit - 2 * bit * (wide // bit % 2)
        others.append((there, narrow))
    at_both = (wide, 3 - narrow)
    greet(others + [at_core, at_y, at_both])
    vocab = table_in.shape[0]

    def own(j):
        return pltpu.make_async_copy(
            shard_ref.at[j], full_refs[j].at[0, 0, z2, z1, x], own_sem.at[j]
        )

    def copy(j, stage):
        full, shard = full_refs[j], shard_ref.at[j]
        mine = full.at[0, 0, z2, z1, x]
        if j == OTHER_WAY:
            src, dst, peer = (
                (shard, mine, at_x),
                (full.at[0, 0, z2, z1], full.at[1, 0, z2, z1], at_y),
                (full.at[:, 0, z2, z1], full.at[:, 0, z2, z1], at_z1),
                (full.at[:, 0, z2], full.at[:, 0, z2], at_z2),
                None,
                (full.at[:, 0], full.at[:, 1], at_core),
            )[stage]
        else:
            src, dst, peer = (
                (shard, mine, at_z2),
                (full.at[0, 0, :, z1, x], full.at[0, 0, :, z1, x], at_z1),
                (full.at[0, 0, :, :, x], full.at[0, 0, :, :, x], at_x),
                (full.at[0, 0], full.at[1, 0], at_y),
                (full.at[0, 0], full.at[0, 1], at_core),
                (full.at[1, 0], full.at[1, 1], at_core),
            )[stage]
        return remote(src, dst, w_send.at[j, stage], w_recv.at[j, stage], peer)

    def advance(j, stage):
        if stage == 1:
            own(j).wait()
        if stage > 0:
            copy(j, {5: 3}.get(stage, stage - 1)).wait_recv()
        copy(j, stage).start()
        if stage == 3 and j != OTHER_WAY:
            copy(j, 4).start()

    def ids_copy(r):
        return remote(
            ids_all.at[0], ids_all.at[r], id_send.at[r], id_recv.at[r], others[r - 1]
        )

    def small_copy(g):
        peer = (None, at_core, at_y, at_both)[g]
        return remote(small_all.at[0], small_all.at[g], small_send.at[g], small_recv.at[g], peer)

    size = chunks.shape[1]
    spans = [(at, min(size, vocab - at)) for at in range(0, vocab, size)]

    def chunk_copy(k):
        at, count = spans[k]
        return pltpu.make_async_copy(
            table_in.at[at : at + count], chunks.at[k % 2, :count], chunk_sem.at[k % 2]
        )

    chunk_copy(0).start()
    ids_all[0] = ids_ref[...]
    small_all[0] = small_ref[...]
    for j in range(units):
        own(j).start()
    advance(0, 0)
    advance(6, 0)
    for r in range(1, 8):
        ids_copy(r).start()
    for g in range(1, 4):
        small_copy(g).start()
    for k, (at, count) in enumerate(spans):
        if k + 1 < len(spans):
            chunk_copy(k + 1).start()
        chunk_copy(k).wait()
        table_ref[at : at + count, :] = chunks[k % 2, :count, :].astype(bf16)
    table_ref[vocab:, :] = jnp.zeros((table_ref.shape[0] - vocab, table_ref.shape[1]), bf16)

    rows = ids_ref.shape[1]

    def look_up(r):
        if r > 0:
            ids_copy(r).wait_recv()
        ids = ids_all[r] - wide * vocab
        for t in range(rows // 128):
            ids_col[t * 128 : (t + 1) * 128] = jnp.broadcast_to(
                ids[:, t * 128 : (t + 1) * 128], (128, 128)
            ).T
        col = ids_col[...]
        lane = lax.broadcasted_iota(jnp.int32, (rows, 128), 1)
        hot = jnp.concatenate(
            [
                (col == lane + at).astype(f32).astype(bf16)
                for at in range(0, table_ref.shape[0], 128)
            ],
            axis=1,
        )
        looked[r] = dot(hot, table_ref[...], 1, 0).astype(bf16)

    def e_copy(hop_at, index):
        if hop_at == 0:
            src, dst, peer = looked.at[2 * index + 1], from_x.at[index], at_x
        elif hop_at == 1:
            src, dst, peer = looked.at[4 * index + 2], from_z1.at[index], at_z1
        else:
            src, dst, peer = looked.at[4], from_z2.at[0], at_z2
        slot = (0, 4, 6)[hop_at] + index
        return remote(src, dst, e_send.at[slot], e_recv.at[slot], peer)

    for what, index in START_ORDER:
        if what < 7:
            advance(what, index)
        elif what == 9:
            look_up(index)
        elif what == 8:
            e_copy(0, index).start()
        else:
            e_copy(0, index).wait_recv()
            looked[2 * index] = looked[2 * index] + from_x[index]
            if index % 2 == 1:
                e_copy(1, index // 2).start()
            else:
                e_copy(1, index // 2).wait_recv()
                looked[2 * index] = looked[2 * index] + from_z1[index // 2]
                if index == 2:
                    e_copy(2, 0).start()
    e_copy(2, 0).wait_recv()
    mine_ref[...] = looked[0] + from_z2[0]
    for g in range(1, 4):
        small_copy(g).wait()
    ids_out[...] = ids_all[...]
    small_out[...] = small_all[...]
    for g, index in enumerate((narrow, at_core[1], at_y[1], at_both[1])):
        small_sorted[index] = small_all[g]
    for j in range(units):
        core_stages = (5,) if j == OTHER_WAY else (4, 5)
        for stage in (0, 1, 2, 3, *core_stages):
            copy(j, stage).wait_send()
        for stage in core_stages:
            copy(j, stage).wait_recv()
    for r in range(1, 8):
        ids_copy(r).wait_send()
    for hop_at, count in ((0, 4), (1, 2), (2, 1)):
        for index in range(count):
            e_copy(hop_at, index).wait_send()


def start_phase(ids, small, table, shards):
    units, slim, columns = shards.shape
    rows, (vocab, width) = ids.shape[1], table.shape
    padded = -(-vocab // 2048) * 2048
    any_space = pl.BlockSpec(memory_space=pl.ANY)
    vmem = pl.BlockSpec(memory_space=pltpu.VMEM)
    dma = pltpu.SemaphoreType.DMA
    *full, mine, table_pad, ids_all, small_all, small_sorted = pl.pallas_call(
        functools.partial(start_kernel, units),
        in_specs=[vmem, vmem, any_space, any_space],
        out_specs=[any_space] * units + [vmem] * 5,
        out_shape=[jax.ShapeDtypeStruct((2, 2, 2, 2, 2, slim, columns), bf16)] * units
        + [
            jax.ShapeDtypeStruct((rows, width), bf16),
            jax.ShapeDtypeStruct((padded, width), bf16),
            jax.ShapeDtypeStruct((8, 1, rows), jnp.int32),
            jax.ShapeDtypeStruct((4, *small.shape), f32),
            jax.ShapeDtypeStruct((4, *small.shape), f32),
        ],
        scratch_shapes=[
            pltpu.VMEM((8, 1, rows), jnp.int32),
            pltpu.VMEM((4, *small.shape), f32),
            pltpu.VMEM((2, 512, width), f32),
            dma((2,)),
            dma((4,)),
            dma((4,)),
            pltpu.VMEM((rows, 128), jnp.int32),
            pltpu.VMEM((8, rows, width), bf16),
            pltpu.VMEM((4, rows, width), bf16),
            pltpu.VMEM((2, rows, width), bf16),
            pltpu.VMEM((1, rows, width), bf16),
            dma((units,)),
            dma((units, 6)),
            dma((units, 6)),
            dma((8,)),
            dma((8,)),
            dma((7,)),
            dma((7,)),
        ],
        compiler_params=pltpu.CompilerParams(
            collective_id=0, has_side_effects=True, vmem_limit_bytes=52 * 2**20
        ),
        cost_estimate=pl.CostEstimate(
            flops=2 * 8 * rows * padded * width, bytes_accessed=2 * 4 * 8 * units * slim * columns,
            transcendentals=0,
        ),
    )(ids, small, table, shards)
    full = [one.reshape(4, 8 * slim, columns) for one in full]
    return full, mine, table_pad, ids_all[:, 0], small_all, small_sorted


def head_kernel(
    vocab, final_ref, table_ref, target_ref, weight_ref, scaled_ref,
    grad_ref, part_ref, loss_ref,
    finals, table_t, logits, slopes, stats, log_total, partial, from_x, from_z1, from_z2,
    f_send, f_recv, s_send, s_recv, g_send, g_recv,
):
    wide, narrow = lax.axis_index("wide"), lax.axis_index("narrow")

    def peer(r):
        index = wide
        for bit in (1, 2, 4):
            if r & bit:
                index = index + bit - 2 * bit * (wide // bit % 2)
        return (index, narrow)

    greet([peer(r) for r in range(1, 8)])
    rows, width = final_ref.shape
    padded = table_ref.shape[0]
    step = 512
    steps = padded // step

    def f_copy(r):
        bit = 1 if r % 2 else (2 if r % 4 else 4)
        return remote(finals.at[r - bit], finals.at[r], f_send.at[r], f_recv.at[r], peer(bit))

    finals[0] = final_ref[...]
    for r in (4, 2, 1):
        f_copy(r).start()

    def chunk_at(k):
        return pl.ds(pl.multiple_of(k * step, step), step)

    def slots(k):
        return lax.broadcasted_iota(jnp.int32, (step, 1), 0) + k * step

    def pair_of(ref, p):
        return jnp.concatenate([ref[2 * p : 2 * p + 1, :], ref[2 * p + 1 : 2 * p + 2, :]], axis=1)

    def forward(p):
        both = jnp.concatenate([finals[2 * p], finals[2 * p + 1]], axis=0)
        target = pair_of(target_ref, p)

        def first(k, top):
            scores = dot(table_ref[chunk_at(k), :], both, 1, 1)
            scores = jnp.where(slots(k) < vocab, scores, -1e30)
            logits[p, chunk_at(k), :] = scores
            return jnp.maximum(top, jnp.max(scores, axis=0, keepdims=True))

        top = lax.fori_loop(0, steps, first, jnp.full((1, 2 * rows), -1e30, f32))

        def second(k, carry):
            total, hits = carry
            scores = logits[p, chunk_at(k), :]
            total = total + jnp.sum(jnp.exp(scores - top), axis=0, keepdims=True)
            hot = jnp.where(slots(k) == target, scores, 0.0)
            return total, hits + jnp.sum(hot, axis=0, keepdims=True)

        zero = jnp.zeros((1, 2 * rows), f32)
        total, hits = lax.fori_loop(0, steps, second, (zero, zero))
        for side in range(2):
            for at, value in enumerate((top, total, hits)):
                stats[0, 2 * p + side, at : at + 1, :] = value[:, side * rows : (side + 1) * rows]

    def turn(k, unused):
        at = pl.ds(pl.multiple_of(k * step, step), step)
        table_t[:, at] = table_ref[at, :].T
        return unused

    lax.fori_loop(0, steps, turn, 0)
    f_copy(2).wait_recv()
    f_copy(3).start()
    f_copy(1).wait_recv()
    forward(0)
    f_copy(4).wait_recv()
    f_copy(6).start()
    f_copy(5).start()
    f_copy(3).wait_recv()
    forward(1)
    f_copy(6).wait_recv()
    f_copy(7).start()
    f_copy(5).wait_recv()
    forward(2)
    f_copy(7).wait_recv()
    forward(3)

    def s_copy(r):
        return remote(stats.at[0], stats.at[r], s_send.at[r], s_recv.at[r], peer(r))

    for r in range(1, 8):
        s_copy(r).start()
    for r in range(1, 8):
        s_copy(r).wait()
    for q in range(8):
        tops = [stats[r, q ^ r, 0:1, :] for r in range(8)]
        best = functools.reduce(jnp.maximum, tops)
        total = sum(stats[r, q ^ r, 1:2, :] * jnp.exp(tops[r] - best) for r in range(8))
        log_total[q : q + 1, :] = best + jnp.log(total)
    hits = sum(stats[r, r, 2:3, :] for r in range(8))
    loss_ref[...] = weight_ref[...] * (log_total[0:1, :] - hits)

    def backward(p):
        target, scaled, minus = pair_of(target_ref, p), pair_of(scaled_ref, p), pair_of(log_total, p)

        def one(k, unused):
            probs = jnp.exp(logits[p, chunk_at(k), :] - minus)
            slope = scaled * (probs - (slots(k) == target).astype(f32))
            slopes[p, chunk_at(k), :] = slope.astype(bf16)
            return unused

        lax.fori_loop(0, steps, one, 0)
        down = dot(table_t[...], slopes[p], 1, 0).T.astype(bf16)
        partial[2 * p] = down[:rows]
        partial[2 * p + 1] = down[rows:]

    def g_copy(hop_at, index):
        if hop_at == 0:
            src, dst, bit = partial.at[2 * index + 1], from_x.at[index], 1
        elif hop_at == 1:
            src, dst, bit = partial.at[4 * index + 2], from_z1.at[index], 2
        else:
            src, dst, bit = partial.at[4], from_z2.at[0], 4
        slot = (0, 4, 6)[hop_at] + index
        return remote(src, dst, g_send.at[slot], g_recv.at[slot], peer(bit))

    def added(a, b):
        return (a.astype(f32) + b.astype(f32)).astype(bf16)

    def parts(start, stop):
        def one(k, unused):
            total = jnp.zeros((step, width), f32)
            for p in range(4):
                both = jnp.concatenate([finals[2 * p], finals[2 * p + 1]], axis=0)
                total = total + dot(slopes[p, chunk_at(k), :], both, 1, 0)
            part_ref[chunk_at(k), :] = total.astype(bf16)
            return unused

        lax.fori_loop(start, stop, one, 0)

    def merge(s):
        g_copy(0, s).wait_recv()
        partial[2 * s] = added(partial[2 * s], from_x[s])

    for p in (3, 1, 2, 0):
        backward(p)
        g_copy(0, p).start()
    for s in (3, 1):
        merge(s)
        g_copy(1, s // 2).start()
    parts(0, steps // 2)
    merge(2)
    g_copy(1, 1).wait_recv()
    partial[4] = added(partial[4], from_z1[1])
    g_copy(2, 0).start()
    parts(steps // 2, steps)
    merge(0)
    g_copy(1, 0).wait_recv()
    partial[0] = added(partial[0], from_z1[0])
    g_copy(2, 0).wait_recv()
    grad_ref[...] = partial[0].astype(f32) + from_z2[0].astype(f32)
    for r in range(1, 8):
        f_copy(r).wait_send()
    for hop_at, count in ((0, 4), (1, 2), (2, 1)):
        for index in range(count):
            g_copy(hop_at, index).wait_send()


def head_phase(vocab, final, table_pad, targets, weights, scaled):
    rows, width = final.shape
    padded = table_pad.shape[0]
    vmem = pl.BlockSpec(memory_space=pltpu.VMEM)
    dma = pltpu.SemaphoreType.DMA
    return pl.pallas_call(
        functools.partial(head_kernel, vocab),
        in_specs=[vmem] * 5,
        out_specs=[vmem] * 3,
        out_shape=[
            jax.ShapeDtypeStruct((rows, width), f32),
            jax.ShapeDtypeStruct((padded, width), bf16),
            jax.ShapeDtypeStruct((1, rows), f32),
        ],
        scratch_shapes=[
            pltpu.VMEM((8, rows, width), bf16),
            pltpu.VMEM((width, padded), bf16),
            pltpu.VMEM((4, padded, 2 * rows), f32),
            pltpu.VMEM((4, padded, 2 * rows), bf16),
            pltpu.VMEM((8, 8, 8, rows), f32),
            pltpu.VMEM((8, rows), f32),
            pltpu.VMEM((8, rows, width), bf16),
            pltpu.VMEM((4, rows, width), bf16),
            pltpu.VMEM((2, rows, width), bf16),
            pltpu.VMEM((1, rows, width), bf16),
            dma((8,)),
            dma((8,)),
            dma((8,)),
            dma((8,)),
            dma((7,)),
            dma((7,)),
        ],
        compiler_params=pltpu.CompilerParams(
            collective_id=2, has_side_effects=True, vmem_limit_bytes=60 * 2**20
        ),
        cost_estimate=pl.CostEstimate(
            flops=6 * 8 * rows * padded * width, bytes_accessed=20 * 2**20,
            transcendentals=2 * 8 * rows * padded,
        ),
    )(final, table_pad, targets, weights, scaled)


HELD = 4
X_FIRST = (6, )
Z_FIRST = (5, )
END_ORDER = (
    (0, 0), (1, 0), (6, 3), (0, 1), (1, 1), (6, 5), (6, 6), (2, 0),
    (9, 0), (0, 2), (1, 2), (0, 3), (1, 3), (2, 1), (3, 0), (9, 1),
    (0, 4), (1, 4), (6, 7), (3, 1), (0, 5), (1, 5), (2, 2), (7, 0),
    (7, 1), (8, 0), (3, 2), (0, 6), (8, 1), (2, 3), (7, 2), (1, 6),
    (4, 2), (8, 2), (7, 3), (8, 4), (2, 5), (2, 4), (8, 5), (2, 6),
    (3, 3), (4, 1), (8, 3), (3, 5), (3, 4), (5, 1), (4, 0), (4, 4),
    (8, 6), (4, 3), (3, 6), (4, 6), (5, 0), (5, 3), (5, 2), (5, 4),
    (4, 5), (8, 7), (5, 6), (5, 5),
)


def end_kernel(kinds, places, *refs):
    units = len(kinds)
    lefts = sorted({left for kind in kinds for left, unused in kind})
    rights = sorted({right for kind in kinds for unused, right in kind})
    count = len(lefts) + len(rights)
    inputs = refs[:count]
    left_refs = {name: inputs[i] for i, name in enumerate(lefts)}
    right_refs = {name: inputs[len(lefts) + i] for i, name in enumerate(rights)}
    ids_ref, rows_ref, head_ref, small_ref = refs[count : count + 4]
    attn_in_out, attn_out_out, ff_in_out, ff_out_out = refs[count + 4 : count + 8]
    table_out, small_out, square_out, c_in, y_in = refs[count + 8 : count + 13]
    (
        left_vm, right_a, right_b, right_c, right_d, left_t, send_c, stage, held, x_in, z1_in, z2_in,
        gathered, table_vm, table_c, table_y, small_all, small_next, square_all, square_next,
        load_sem, stage_sem, w_send, w_recv, l_send, l_recv, t_send, t_recv, s_send, s_recv, own_sem,
    ) = refs[count + 13 :]
    wide, narrow = lax.axis_index("wide"), lax.axis_index("narrow")
    z2, z1, x = wide // 4, wide // 2 % 2, wide % 2
    y, core = narrow // 2, narrow % 2

    def flipped(index, bits, r):
        for bit in bits:
            if r & bit:
                index = index + bit - 2 * bit * (index // bit % 2)
        return index

    wide_peer = lambda r: (flipped(wide, (1, 2, 4), r), narrow)
    narrow_peer = lambda g: (wide, flipped(narrow, (1, 2), g))
    greet([wide_peer(r) for r in range(1, 8)] + [narrow_peer(g) for g in range(1, 4)])

    slim, columns = ff_in_out.shape[1:]
    width = 8 * slim

    def small_copy(base, src, dst, index, peer):
        return remote(src, dst, s_send.at[base + index], s_recv.at[base + index], peer)

    def spread(base, value_ref, all_ref):
        all_ref[0] = value_ref[...]
        for r in range(1, 8):
            small_copy(base, all_ref.at[0], all_ref.at[r], r, wide_peer(r)).start()

    def spread_next(base, all_ref, next_ref):
        for r in range(1, 8):
            small_copy(base, all_ref.at[0], all_ref.at[r], r, wide_peer(r)).wait()
        next_ref[0] = jnp.sum(all_ref[...], axis=0)
        for g in range(1, 4):
            small_copy(base + 7, next_ref.at[0], next_ref.at[g], g, narrow_peer(g)).start()

    def collect(base, next_ref, result_ref):
        for g in range(1, 4):
            small_copy(base + 7, next_ref.at[0], next_ref.at[g], g, narrow_peer(g)).wait()
        result_ref[...] = jnp.sum(next_ref[...], axis=0)

    def row_copy(r):
        bit = 1 if r % 2 else (2 if r % 4 else 4)
        return remote(gathered.at[r - bit], gathered.at[r], l_send.at[r], l_recv.at[r], wide_peer(bit))

    right_space = {}

    def loads(j):
        copies = []
        for at, (left, right) in enumerate(kinds[j]):
            src = left_refs[left]
            copies.append((src, left_vm.at[at, : src.shape[0]]))
            src = right_refs[right]
            cols = src.shape[2]
            if cols == columns:
                space = right_d
            else:
                space = (right_a, right_b, right_c)[at]
            copies.append((src, space.at[:, : src.shape[1]]))
        return [
            pltpu.make_async_copy(src, dst, load_sem.at[i]) for i, (src, dst) in enumerate(copies)
        ]

    def product(j, group):
        parts = []
        for at, (left, right) in enumerate(kinds[j]):
            rows = left_refs[left].shape[0]
            cols = right_refs[right].shape[2]
            space = right_d if cols == columns else (right_a, right_b, right_c)[at]
            parts.append(dot(left_t[at, :, :rows], space[group, :rows, :], 1, 0).astype(bf16))
        whole = parts[0] if len(parts) == 1 else jnp.concatenate(parts, axis=1)
        return whole

    def w_copy(j, hop_at):
        slot = j % HELD
        if hop_at == 0:
            src, dst, peer = send_c, c_in.at[j], narrow_peer(1)
        elif j in Z_FIRST:
            src, dst, peer = (
                (held.at[slot, :, 1 - z2], y_in.at[j], wide_peer(4)),
                (held.at[slot, :, z2, 1 - z1], x_in.at[j], wide_peer(2)),
                (x_in.at[j, :, 1 - x], z1_in.at[j], wide_peer(1)),
                (z1_in.at[j, 1], z2_in.at[j], narrow_peer(2)),
            )[hop_at - 1]
        elif hop_at == 1 and j in X_FIRST:
            src, dst, peer = held.at[slot, :, :, :, 1 - x], y_in.at[j], wide_peer(1)
        elif hop_at == 1:
            src, dst, peer = held.at[slot, 1], y_in.at[j], narrow_peer(2)
        elif hop_at == 2 and j in X_FIRST:
            src, dst, peer = held.at[slot, 1, :, :, x], x_in.at[j], narrow_peer(2)
        elif hop_at == 2:
            src, dst, peer = held.at[slot, 0, :, :, 1 - x], x_in.at[j], wide_peer(1)
        elif hop_at == 3:
            src, dst, peer = x_in.at[j, :, 1 - z1], z1_in.at[j], wide_peer(2)
        else:
            src, dst, peer = z1_in.at[j, 1 - z2], z2_in.at[j], wide_peer(4)
        return remote(src, dst, w_send.at[j, hop_at], w_recv.at[j, hop_at], peer)

    def multiply(j):
        for copy in loads(j):
            copy.wait()
        for at, (left, unused) in enumerate(kinds[j]):
            rows = left_refs[left].shape[0]
            left_t[at, :, :rows] = left_vm[at, :rows, :].T
        if j > 0:
            w_copy(j - 1, 0).wait_send()
        for side in range(2):
            send_c[side] = product(j, 2 * side + 1).reshape(send_c.shape[1:])
        w_copy(j, 0).start()
        for side in range(2):
            held[j % HELD, side] = product(j, 2 * side).reshape(held.shape[2:])
        if j + 1 < units:
            for copy in loads(j + 1):
                copy.start()

    def added(a, b):
        return (a.astype(f32) + b.astype(f32)).astype(bf16)

    def staged(src, dst):
        copy = pltpu.make_async_copy(src, dst, stage_sem.at[0])
        copy.start()
        copy.wait()

    def after_core(j):
        w_copy(j, 0).wait_recv()
        staged(c_in.at[j], stage)
        for side in (1, 0):
            held[j % HELD, side] = added(held[j % HELD, side], stage[side])
            if side == 1 and j not in X_FIRST + Z_FIRST:
                w_copy(j, 1).start()
        if j in X_FIRST + Z_FIRST:
            w_copy(j, 1).start()

    def after_first(j):
        w_copy(j, 1).wait()
        staged(y_in.at[j], stage.at[0])
        if j in X_FIRST:
            for side in (1, 0):
                held[j % HELD, side, :, :, x] = added(held[j % HELD, side, :, :, x], stage[0, side])
                if side == 1:
                    w_copy(j, 2).start()
        elif j in Z_FIRST:
            held[j % HELD, :, z2] = added(held[j % HELD, :, z2], stage[0])
            w_copy(j, 2).start()
        else:
            held[j % HELD, 0] = added(held[j % HELD, 0], stage[0])
            w_copy(j, 2).start()

    def after_second(j):
        w_copy(j, 2).wait()
        if j in Z_FIRST:
            x_in[j] = added(x_in[j], held[j % HELD, :, z2, z1])
        else:
            x_in[j] = added(x_in[j], held[j % HELD, 0, :, :, x])
        w_copy(j, 3).start()

    def after_z1(j):
        w_copy(j, 3).wait()
        z1_in[j] = added(z1_in[j], x_in[j, :, x if j in Z_FIRST else z1])
        w_copy(j, 4).start()

    def after_z2(j):
        w_copy(j, 4).wait()
        total = z2_in[j].astype(f32) + z1_in[j, 0 if j in Z_FIRST else z2].astype(f32)
        note(total)
        what, layer = places[j]
        if what == 0:
            lanes = attn_out_out.shape[1]
            parts = []
            for head in range(lanes // DH):
                for which in range(3):
                    at = which * lanes + head * DH
                    parts.append(total[:, at : at + DH])
            attn_in_out[layer] = jnp.concatenate(parts, axis=1)
            attn_out_out[layer] = total[:, 3 * lanes :].T
        elif what == 1:
            ff_in_out[layer] = total
        else:
            ff_out_out[layer] = total.T

    def note(values):
        rows = values.shape[0]
        squares = jnp.sum((values * values).reshape(rows // 8, 8, values.shape[1]), axis=0)
        for at in range(0, values.shape[1], 128):
            square_all[0] += squares[:, at : at + 128]

    quarter = table_vm.shape[1]
    tokens = gathered.shape[1]
    step = 256

    half = quarter // 2
    per = half // step

    def scatter_rows(part):
        def chunk(k, unused):
            which = 2 * (part % 2) + k // per
            first = part // 2 * half + k % per * step
            at = pl.ds(pl.multiple_of(first, step), step)
            slot = lax.broadcasted_iota(jnp.int32, (step, 1), 0) + which * quarter + first
            hot = jnp.concatenate(
                [(slot == ids_ref[r]).astype(f32).astype(bf16) for r in range(8)], axis=1
            )
            total = table_vm[which, at, :].astype(f32)
            total = total + dot(hot, gathered[...].reshape(8 * tokens, width), 1, 0)
            table_vm[which, at, :] = total.astype(bf16)
            return unused

        lax.fori_loop(0, 2 * per, chunk, 0)

    def t_copy(number):
        at, part = number % 6, pl.ds(number // 6 * half, half)
        there = 2 * (1 - y) + core
        src, dst, peer = (
            (table_vm.at[1 - core, part], table_c.at[0, part], narrow_peer(1)),
            (table_vm.at[3 - core, part], table_c.at[1, part], narrow_peer(1)),
            (table_vm.at[there, part], table_y.at[part], narrow_peer(2)),
            (table_vm.at[narrow, part], table_out.at[narrow, part], narrow_peer(2)),
            (table_vm.at[narrow, part], table_out.at[narrow, part], narrow_peer(1)),
            (table_out.at[there, part], table_out.at[there, part], narrow_peer(1)),
        )[at]
        return remote(src, dst, t_send.at[number], t_recv.at[number], peer)

    def own_half(side):
        part = pl.ds(side * half, half)
        return pltpu.make_async_copy(
            table_vm.at[narrow, part], table_out.at[narrow, part], own_sem.at[3 + side]
        )

    def head_load():
        return pltpu.make_async_copy(head_ref, table_vm, own_sem.at[1])

    def rows_load():
        return pltpu.make_async_copy(rows_ref, gathered.at[0], own_sem.at[2])

    rows_load().start()
    head_load().start()
    for copy in loads(0):
        copy.start()
    square_all[0] = jnp.zeros_like(square_all[0])
    spread(0, small_ref, small_all)
    rows_load().wait()
    for r in (1, 4, 2):
        row_copy(r).start()

    def table_step(index):
        there = 2 * (1 - y) + core
        at, side = index % 4, index // 4
        part, base = slice(side * half, (side + 1) * half), 6 * side
        if at == 0:
            t_copy(base).start()
            t_copy(base + 1).start()
        elif at == 1:
            t_copy(base).wait_recv()
            t_copy(base + 1).wait_recv()
            table_vm[there, part] = added(table_vm[there, part], table_c[1 - y, part])
            t_copy(base + 2).start()
            table_vm[narrow, part] = added(table_vm[narrow, part], table_c[y, part])
        elif at == 2:
            t_copy(base + 2).wait()
            total = added(table_vm[narrow, part], table_y[part])
            table_vm[narrow, part] = total
            t_copy(base + 3).start()
            t_copy(base + 4).start()
            own_half(side).start()
            note(total.astype(f32))
        else:
            t_copy(base + 3).wait_recv()
            t_copy(base + 5).start()

    arrived = []

    def rows_step(r):
        needed = {3: 2, 5: 4, 6: 4, 7: 6}[r]
        if needed not in arrived:
            arrived.append(needed)
            row_copy(needed).wait_recv()
        row_copy(r).start()

    def scatter_step(part):
        if part == 0:
            head_load().wait()
            for r in (1, 3, 5, 7):
                row_copy(r).wait_recv()
        scatter_rows(part)

    def small_step(at):
        if at == 0:
            spread_next(0, small_all, small_next)
        else:
            collect(0, small_next, small_out)

    acts = (
        multiply, after_core, after_first, after_second, after_z1, after_z2,
        rows_step, scatter_step, table_step, small_step,
    )
    for what, index in END_ORDER:
        acts[what](index)
    for r in range(1, 8):
        small_copy(16, square_all.at[0], square_all.at[r], r, wide_peer(r)).start()
    spread_next(16, square_all, square_next)
    collect(16, square_next, square_out)
    for side in range(2):
        for at in (4, 5):
            t_copy(6 * side + at).wait_recv()
        for at in (0, 1, 3, 4, 5):
            t_copy(6 * side + at).wait_send()
        own_half(side).wait()
    w_copy(units - 1, 0).wait_send()
    for r in range(1, 8):
        row_copy(r).wait_send()


def end_phase(kinds, places, lefts, rights, ids, rows, head, small):
    units = len(kinds)
    names = sorted({left for kind in kinds for left, unused in kind})
    right_names = sorted({right for kind in kinds for unused, right in kind})
    tokens, width = rows.shape
    slim = width // 8
    quarter = head.shape[1]
    most = max(value.shape[0] for value in lefts.values())
    any_space = pl.BlockSpec(memory_space=pl.ANY)
    vmem = pl.BlockSpec(memory_space=pltpu.VMEM)
    dma = pltpu.SemaphoreType.DMA
    narrow_cols = [rights[right].shape[2] for unused, right in max(kinds, key=len)]
    args = [lefts[name] for name in names] + [rights[name] for name in right_names]
    outs = pl.pallas_call(
        functools.partial(end_kernel, kinds, places),
        in_specs=[any_space] * len(args) + [vmem, any_space, any_space, vmem],
        out_specs=[vmem] * 4 + [any_space, vmem, vmem, any_space, any_space],
        out_shape=[
            jax.ShapeDtypeStruct((3, slim, 3 * (width // 4)), f32),
            jax.ShapeDtypeStruct((3, width // 4, slim), f32),
            jax.ShapeDtypeStruct((2, slim, width), f32),
            jax.ShapeDtypeStruct((2, width, slim), f32),
            jax.ShapeDtypeStruct((4, quarter, width), bf16),
            jax.ShapeDtypeStruct(small.shape, f32),
            jax.ShapeDtypeStruct((8, 128), f32),
            jax.ShapeDtypeStruct((units, 2, 2, 2, 2, slim, width), bf16),
            jax.ShapeDtypeStruct((units, 2, 2, 2, slim, width), bf16),
        ],
        scratch_shapes=[
            pltpu.VMEM((3, most, width), bf16),
            pltpu.VMEM((4, most, narrow_cols[0]), bf16),
            pltpu.VMEM((4, most, narrow_cols[1]), bf16),
            pltpu.VMEM((4, most, narrow_cols[2]), bf16),
            pltpu.VMEM((4, most, width), bf16),
            pltpu.VMEM((3, width, most), bf16),
            pltpu.VMEM((2, 2, 2, 2, slim, width), bf16),
            pltpu.VMEM((2, 2, 2, 2, slim, width), bf16),
            pltpu.VMEM((HELD, 2, 2, 2, 2, slim, width), bf16),
            pltpu.VMEM((units, 2, 2, slim, width), bf16),
            pltpu.VMEM((units, 2, slim, width), bf16),
            pltpu.VMEM((units, slim, width), bf16),
            pltpu.VMEM((8, tokens, width), bf16),
            pltpu.VMEM((4, quarter, width), bf16),
            pltpu.VMEM((2, quarter, width), bf16),
            pltpu.VMEM((quarter, width), bf16),
            pltpu.VMEM((8, *small.shape), f32),
            pltpu.VMEM((4, *small.shape), f32),
            pltpu.VMEM((8, 8, 128), f32),
            pltpu.VMEM((4, 8, 128), f32),
            dma((6,)),
            dma((1,)),
            dma((units, 5)),
            dma((units, 5)),
            dma((8,)),
            dma((8,)),
            dma((12,)),
            dma((12,)),
            dma((32,)),
            dma((32,)),
            dma((5,)),
        ],
        compiler_params=pltpu.CompilerParams(
            collective_id=1, has_side_effects=True, vmem_limit_bytes=62 * 2**20
        ),
        cost_estimate=pl.CostEstimate(
            flops=2 * 8 * tokens * 4 * quarter * width, bytes_accessed=100 * 2**20, transcendentals=0
        ),
    )(*args, ids, rows, head, small)
    return outs[:4], *outs[4:7]


def body(
    enc_ids, enc_len, tgt_ids, tgt_len, span_mask, buckets,
    attn_in, attn_out, ff_in, ff_out, table, gains, rel,
    mom_attn_in, mom_attn_out, mom_ff_in, mom_ff_out, mom_table, mom_gains, mom_rel,
    avg_attn_in, avg_attn_out, avg_ff_in, avg_ff_out, avg_table, avg_gains, avg_rel,
):
    wide_size = lax.axis_size("wide")
    narrow_size = lax.axis_size("narrow")
    wide_index = lax.axis_index("wide")
    narrow_index = lax.axis_index("narrow")
    micro = narrow_index // 2
    core = narrow_index % 2
    width = table.shape[1]
    vocab = table.shape[0]
    enc_rows = enc_ids.shape[2] // 2
    dec_rows = tgt_ids.shape[2] // 2
    centre = (buckets.shape[0] + 1) // 2 - 1
    lanes = attn_out.shape[1]
    heads_here = lanes // DH
    slim = attn_in.shape[1]

    shards = []
    for layer in range(3):
        packed = attn_in[layer].reshape(slim, heads_here, 3, DH).transpose(0, 2, 1, 3)
        shards.append(jnp.concatenate([packed.reshape(slim, -1), attn_out[layer].T], axis=1))
    for layer in range(2):
        shards.append(ff_in[layer])
        shards.append(ff_out[layer].T)
    shards = jnp.stack(shards).astype(bf16)
    groups = narrow_index ^ jnp.arange(narrow_size)
    small = jnp.concatenate([gains.reshape(-1), rel.reshape(-1)])
    cut = gains.size
    onehot_rev = (buckets[::-1][:, None] == jnp.arange(rel.shape[1])[None, :]).astype(f32)
    onehot_rev = jnp.pad(onehot_rev, ((0, 1), (0, 0)))
    my_enc = lax.dynamic_slice(enc_ids, (micro, 0, core * enc_rows), (1, 1, enc_rows))
    others = wide_index ^ jnp.arange(wide_size)
    targets_micro = lax.dynamic_index_in_dim(tgt_ids, micro, 0, keepdims=False)[others]
    shifted = jnp.concatenate(
        [jnp.zeros((wide_size, 1), jnp.int32), targets_micro[:, :-1]], axis=1
    )
    dec_all = lax.dynamic_slice_in_dim(shifted, core * dec_rows, dec_rows, 1)
    if wide_size == 8 and narrow_size == 4:
        my_ids = jnp.concatenate([my_enc.reshape(enc_rows), dec_all[0]])[None]
        gathered, mine, table_pad, tokens, small, small_sorted = start_phase(
            my_ids, small.reshape(-1, 128), table, shards
        )
        small = small.reshape(narrow_size, -1)
        small_sorted = small_sorted.reshape(narrow_size, -1)
        local = tokens - wide_index * vocab
        held = (local >= 0) & (local < vocab)
    else:
        small_sorted = lax.all_gather(small, "narrow", axis=0, tiled=False)
        small = small_sorted[groups]
        enc_all = gather_direct(my_enc.reshape(enc_rows), "wide")
        tokens = jnp.concatenate([enc_all, dec_all], axis=1)
        local = tokens - wide_index * vocab
        held = (local >= 0) & (local < vocab)
        gathered = []
        for shard in shards:
            column = gather_sorted(shard, "wide").reshape(width, -1)
            pair = jnp.stack([column, hop(column, "narrow", 2)])
            pair = jnp.stack([pair, swap(pair)], axis=1)
            gathered.append(pair.reshape(narrow_size, width, -1))
        table_low = table.astype(bf16)
        rows = table_low[jnp.where(held, local, 0).reshape(-1)]
        rows = jnp.where(held.reshape(-1)[:, None], rows, 0).astype(bf16)
        mine = scatter_relative(rows.reshape(*local.shape, width), "wide", bf16)
    gains_full = small_sorted[:, :cut].reshape(narrow_size, *gains.shape).transpose(1, 0, 2)
    gains_full = gains_full.reshape(gains.shape[0], -1)
    rel_full = small[:, cut:].reshape(narrow_size, *rel.shape).transpose(1, 2, 0, 3)
    rel_full = rel_full.reshape(rel.shape[0], rel.shape[1], -1)
    rel_rows = [
        jnp.dot(onehot_rev, rel_full[i], precision=highest).T[:, None, :] for i in range(2)
    ]
    low_in = [gathered[i][:, :, : 3 * lanes] for i in range(3)]
    low_out = [gathered[i][:, :, 3 * lanes :] for i in range(3)]
    low_up = [gathered[3], gathered[5]]
    low_down = [gathered[4], gathered[6]]

    enc0 = mine[:enc_rows].astype(f32)
    dec0 = mine[enc_rows:].astype(f32)

    key_len = lax.dynamic_slice(enc_len, (micro, 0), (1, 1)).reshape(())
    scal = jnp.stack([core, key_len]).astype(jnp.int32)

    def attn_forward(state, gain_row, layer, source, rel_row, causal):
        normed, inverse = rms_forward(state, gain_row)
        kv = project(normed if source is None else source, low_in[layer][:, :, lanes:]).astype(bf16)
        kv_other = swap(kv)
        q = project(normed, low_in[layer][:, :, :lanes]).astype(bf16)
        mixed, lse = attend(scal, q, kv, kv_other, rel_row, centre, causal)
        update = project_back(mixed, low_out[layer])
        return (state + update, (state, inverse, normed, q, kv, kv_other, mixed, lse))

    def attn_backward(saved, upstream, gain_row, layer, source, rel_row, causal):
        state, inverse, normed, q, kv, kv_other, mixed, lse = saved
        up = upstream.astype(bf16)
        mixed_grad = project(up, low_out[layer]).astype(bf16)
        outs = attend_back(scal, q, kv, kv_other, mixed_grad, lse, rel_row, centre, causal)
        dq, dkv_own, dkv_other = outs[:3]
        dkv = (dkv_own + swap(dkv_other).astype(f32)).astype(bf16)
        normed_grad = project_back(dq, low_in[layer][:, :, :lanes])
        kv_back = project_back(dkv, low_in[layer][:, :, lanes:])
        if source is None:
            normed_grad = normed_grad + kv_back
        state_grad, gain_grad = rms_backward(state, gain_row, inverse, normed_grad)
        pieces = ((normed, dq), (normed if source is None else source, dkv), (up, mixed))
        return (upstream + state_grad, gain_grad, pieces, kv_back, outs[3] if rel_row is not None else None)

    def ff_forward(state, gain_row, layer):
        normed, inverse = rms_forward(state, gain_row)
        pre = project(normed, low_up[layer])
        hidden = jax.nn.gelu(pre).astype(bf16)
        return (state + project_back(hidden, low_down[layer]), (state, inverse, normed, pre, hidden))

    def ff_backward(saved, upstream, gain_row, layer):
        state, inverse, normed, pre, hidden = saved
        up = upstream.astype(bf16)
        hidden_grad = project(up, low_down[layer]).astype(bf16).astype(f32)
        unused, gelu_back = jax.vjp(jax.nn.gelu, pre)
        pre_grad = gelu_back(hidden_grad)[0].astype(bf16)
        normed_grad = project_back(pre_grad, low_up[layer])
        state_grad, gain_grad = rms_backward(state, gain_row, inverse, normed_grad)
        return (upstream + state_grad, gain_grad, ((normed, pre_grad),), ((up, hidden),))

    def scatter(pieces):
        grad = jnp.concatenate([outer(*piece) for piece in pieces], axis=2).astype(bf16)
        return spread(grad)

    def spread(grad):
        pairs = grad.reshape(2, 2, width, -1)
        across = pairs[:, 0].astype(f32) + swap(pairs[:, 1]).astype(f32)
        column = across[0] + hop(across[1].astype(bf16), "narrow", 2).astype(f32)
        return scatter_sorted(column.astype(bf16).reshape(wide_size, slim, -1), "wide")

    enc1, saved_a = attn_forward(enc0, gains_full[0], 0, None, rel_rows[0], 0)
    enc2, saved_b = ff_forward(enc1, gains_full[1], 0)
    encoded, enc_inverse = rms_forward(enc2, gains_full[2])
    dec1, saved_c = attn_forward(dec0, gains_full[3], 1, None, rel_rows[1], dec_rows)
    dec2, saved_d = attn_forward(dec1, gains_full[4], 2, encoded, None, 0)
    dec3, saved_e = ff_forward(dec2, gains_full[5], 1)
    final_gain = gains_full[6] * width ** (-0.5)
    final, final_inverse = rms_forward(dec3, final_gain)

    row_weight = (jnp.arange(2 * dec_rows)[None, None, :] < tgt_len[:, :, None]).astype(
        f32
    ) * span_mask.astype(f32)
    count = jnp.sum(row_weight)
    weights_micro = lax.dynamic_index_in_dim(row_weight, micro, 0, keepdims=False)[others]
    weights = lax.dynamic_slice_in_dim(weights_micro, core * dec_rows, dec_rows, 1).reshape(-1)
    targets = lax.dynamic_slice_in_dim(targets_micro, core * dec_rows, dec_rows, 1).reshape(-1)
    targets = targets - wide_index * vocab
    if wide_size == 8 and narrow_size == 4:
        own_weights = weights[None, :dec_rows]
        shape = (wide_size, dec_rows)
        final_grad, head_part, loss_row = head_phase(
            vocab, final, table_pad,
            jnp.where(targets < vocab, targets, -1).reshape(shape), own_weights,
            (weights / count).reshape(shape),
        )
        loss_part = jnp.sum(loss_row)
    else:
        final_all = gather_relative(final, "wide").reshape(-1, width)
        logits = dot(final_all, table_low, 1, 1)
        target_hot = jnp.arange(vocab)[None, :] == targets[:, None]
        top = jnp.max(logits, axis=-1)
        total = jnp.sum(jnp.exp(logits - top[:, None]), axis=-1)
        hits = jnp.sum(jnp.where(target_hot, logits, 0.0), axis=-1)
        stats = jnp.stack([top, total, hits]).reshape(3, wide_size, dec_rows)
        if wide_size > 8:
            stats = lax.all_gather(stats[:, others], "wide", axis=0, tiled=False)[:, :, others]
        else:
            stats = jnp.stack(
                [stats]
                + [
                    hop(stats, "wide", r)[:, [q ^ r for q in range(wide_size)]]
                    for r in range(1, wide_size)
                ]
            )
        stats = stats.reshape(wide_size, 3, -1)
        best = jnp.max(stats[:, 0], axis=0)
        log_total = best + jnp.log(jnp.sum(stats[:, 1] * jnp.exp(stats[:, 0] - best[None]), axis=0))
        loss_rows = weights * (log_total - jnp.sum(stats[:, 2], axis=0))
        loss_part = jnp.sum(loss_rows[:dec_rows])
        logit_grad = (
            (weights / count)[:, None]
            * (jnp.exp(logits - log_total[:, None]) - target_hot.astype(f32))
        ).astype(bf16)
        final_grad = scatter_relative(
            dot(logit_grad, table_low, 1, 0).reshape(wide_size, dec_rows, width), "wide", f32
        )

    gain_grads = [None] * 7
    dec_grad, gain_raw = rms_backward(dec3, final_gain, final_inverse, final_grad)
    gain_grads[6] = gain_raw * width ** (-0.5)
    dec_grad, gain_grads[5], up1, down1 = ff_backward(saved_e, dec_grad, gains_full[5], 1)
    dec_grad, gain_grads[4], attn2, source_grad, unused = attn_backward(
        saved_d, dec_grad, gains_full[4], 2, encoded, None, 0
    )
    dec_grad, gain_grads[3], attn1, unused, drel_dec = attn_backward(
        saved_c, dec_grad, gains_full[3], 1, None, rel_rows[1], dec_rows
    )
    enc_grad, gain_grads[2] = rms_backward(enc2, gains_full[2], enc_inverse, source_grad)
    enc_grad, gain_grads[1], up0, down0 = ff_backward(saved_b, enc_grad, gains_full[1], 0)
    enc_grad, gain_grads[0], attn0, unused, drel_enc = attn_backward(
        saved_a, enc_grad, gains_full[0], 0, None, rel_rows[0], 0
    )
    length = onehot_rev.shape[0]
    rel_grad = jnp.stack(
        [
            jnp.dot(rel_grad_rows(drel_enc, core, enc_rows, centre, length), onehot_rev, precision=highest),
            jnp.dot(rel_grad_rows(drel_dec, core, dec_rows, centre, length), onehot_rev, precision=highest),
        ]
    )
    rel_grad = rel_grad.reshape(2, narrow_size, heads_here, -1)[:, groups]
    rel_grad = rel_grad.reshape(2, narrow_size * heads_here, -1)
    row_grads = jnp.concatenate([enc_grad, dec_grad], axis=0).astype(bf16)
    local = jnp.where(held, local, -1)
    if wide_size == 8 and narrow_size == 4:
        order = (up1, down1, attn2, attn1, up0, down0, attn0)
        kinds, lefts, rights = [], {}, {}
        names = {}
        for unit in order:
            kind = []
            for left, right in unit:
                name = names.setdefault(id(left), "l%02d" % len(names))
                lefts[name] = left
                rights["r%02d" % len(rights)] = right
                kind.append((name, "r%02d" % (len(rights) - 1)))
            kinds.append(tuple(kind))
        quarter = head_part.shape[0] // 4
        flat = jnp.concatenate(
            [jnp.stack(gain_grads).reshape(-1), rel_grad.reshape(-1), loss_part[None]]
        )
        small_rows = -(-flat.size // 1024) * 8
        small_in = jnp.pad(flat, (0, small_rows * 128 - flat.size)).reshape(small_rows, 128)
        matrix_grads, table_grad, small_sum, square_rows = end_phase(
            tuple(kinds), ((1, 1), (2, 1), (0, 2), (0, 1), (1, 0), (2, 0), (0, 0)), lefts, rights, local[:, None, :], row_grads,
            head_part.reshape(4, quarter, width), small_in,
        )
        table_grad = table_grad.reshape(4 * quarter, width)[:vocab].astype(f32)
        small_sum = small_sum.reshape(-1)
        cut = 7 * width
        gain_total = small_sum[:cut].reshape(7, width)
        rel_total = small_sum[cut : cut + rel_grad.size].reshape(rel_grad.shape)
        loss_sum = small_sum[cut + rel_grad.size]
        square_sum = jnp.sum(square_rows)
    else:
        reduced = [scatter(grad) for grad in (attn0, attn1, attn2, up0, down0, up1, down1)]

        padded = -(-vocab // 64) * 64
        slots = jnp.arange(padded)
        local = local.reshape(-1, 2, local.shape[1])
        halves, part_grads = [], []
        half = width // 2
        for start in (0, half):
            rows = row_grads[None, :, start : start + half]
            for bit in list(bits_down("wide"))[:-1]:
                rows = jnp.stack([rows, hop(rows, "wide", bit)], axis=1)
                rows = rows.reshape(-1, *rows.shape[2:])
            far = hop(rows, "wide", 1)
            partial = dot(logit_grad, final_all[:, start : start + half], 0, 0)
            partial = jnp.pad(partial, ((0, padded - vocab), (0, 0)))
            for at, values in ((local[:, 0], rows), (local[:, 1], far)):
                token_hot = (slots[:, None] == at.reshape(-1)[None, :]).astype(bf16)
                partial = partial + dot(token_hot, values.reshape(-1, half), 1, 0)
            quarters = partial.astype(bf16).reshape(narrow_size, padded // narrow_size, half)
            part = scatter_sorted(quarters, "narrow").astype(bf16)
            part_grads.append(part.astype(f32))
            halves.append(gather_sorted(part, "narrow").reshape(padded, half)[:vocab])
        table_grad = jnp.concatenate(halves, axis=1).astype(f32)

        gain_total, rel_total, loss_sum = lax.psum(
            (jnp.stack(gain_grads), rel_grad, loss_part), ("wide", "narrow")
        )
        unpack = lambda grad: (
            grad[:, : 3 * lanes].reshape(slim, 3, heads_here, DH).transpose(0, 2, 1, 3)
        ).reshape(slim, -1)
        matrix_grads = (
            jnp.stack([unpack(reduced[i]) for i in range(3)]),
            jnp.stack([reduced[i][:, 3 * lanes :].T for i in range(3)]),
            jnp.stack([reduced[3], reduced[5]]),
            jnp.stack([reduced[4].T, reduced[6].T]),
        )
        squares = sum(jnp.sum(grad * grad) for grad in reduced + part_grads)
        square_sum = lax.psum(squares, ("wide", "narrow"))
    square_sum = square_sum + jnp.sum(gain_total * gain_total) + jnp.sum(rel_total * rel_total)
    gain_mine = lax.dynamic_slice_in_dim(gain_total, narrow_index * lanes, lanes, 1)
    rel_mine = lax.dynamic_slice_in_dim(
        rel_total, narrow_index * heads_here, heads_here, 1
    ).transpose(0, 2, 1)

    grads = (*matrix_grads, table_grad, gain_mine, rel_mine)
    norm = jnp.sqrt(square_sum)
    scale = jnp.minimum(1.0, clip_norm / norm)
    base_rate = math.sqrt(PARAMS) / (3.0 * clip_norm)
    matrix_rate = base_rate / math.sqrt(width)
    rates = (
        matrix_rate, 16.0 * matrix_rate, matrix_rate, matrix_rate,
        base_rate, 0.3 * base_rate, 0.3 * base_rate,
    )
    params = (attn_in, attn_out, ff_in, ff_out, table, gains, rel)
    moms = (mom_attn_in, mom_attn_out, mom_ff_in, mom_ff_out, mom_table, mom_gains, mom_rel)
    avgs = (avg_attn_in, avg_attn_out, avg_ff_in, avg_ff_out, avg_table, avg_gains, avg_rel)
    fresh, scaled_grads, averages = ([], [], [])
    for index in range(7):
        clipped = grads[index] * scale
        moment = momentum_decay * moms[index] + clipped
        weight = params[index] - rates[index] * (clipped + momentum_decay * moment)
        fresh.append(weight)
        scaled_grads.append(clipped)
        averages.append(average_decay * avgs[index] + (1.0 - average_decay) * weight)
    return (loss_sum, count, norm, *fresh, *scaled_grads, *averages)


def solution(mesh):
    weights = (
        P(None, "wide", "narrow"),
        P(None, "narrow", "wide"),
        P(None, "wide", "narrow"),
        P(None, "narrow", "wide"),
        P("wide", None),
        P(None, "narrow"),
        P(None, None, "narrow"),
    )
    in_specs = (P(None, "wide", None), P(None, "wide"), P(), P(), P(), P()) + weights * 3
    out_specs = (P(), P(), P()) + weights * 3
    return jax.shard_map(body, mesh=mesh, in_specs=in_specs, out_specs=out_specs, check_vma=False)
```
